32 devices in a mesh: dp: 16 (over z, y, core), branch: 2 (over x).
Axes of the slice: x: 2, y: 2, z: 4, core: 2. Of those that a mesh axis runs over, the one named last changes fastest.
Arguments:
- stream: bfloat16 [16384, 1024], P(('dp', 'branch')), may hold values from -6 to 6
- cotangent: bfloat16 [16384, 1024], P(('dp', 'branch')), may hold values from -6 to 6
- lengths: int32 [16], P('dp'), may hold values from 128 to 1024, as said below
- steps_taken: int32 [1], replicated, may hold values from 2 to 20
- learning_rates: float32 [6], replicated
- mixing: float32 [1024, 3072], P(('dp', 'branch')), may hold values from -0.1875 to 0.1875
- merging: float32 [1024, 1024], P(('dp', 'branch')), may hold values from -3 to 3
- expand: float32 [1024, 4096], P(('dp', 'branch')), may hold values from -0.1875 to 0.1875
- shrink: float32 [4096, 1024], P(('dp', 'branch')), may hold values from -0.09375 to 0.09375
- vectors: float32 [2, 1024], P(None, ('dp', 'branch')), may hold values from -1 to 2
- offsets: float32 [5120], P(('dp', 'branch')), may hold values from -1.75 to 1.75
- mixing_momentum: float32 [1024, 3072], P(('dp', 'branch'))
- merging_momentum: float32 [1024, 1024], P(('dp', 'branch'))
- expand_momentum: float32 [1024, 4096], P(('dp', 'branch'))
- shrink_momentum: float32 [4096, 1024], P(('dp', 'branch'))
- vectors_momentum: float32 [2, 1024], P(None, ('dp', 'branch'))
- offsets_momentum: float32 [5120], P(('dp', 'branch'))
- mixing_variance: float32 [1024, 3072], P(('dp', 'branch'))
- merging_variance: float32 [1024, 1024], P(('dp', 'branch'))
- expand_variance: float32 [1024, 4096], P(('dp', 'branch'))
- shrink_variance: float32 [4096, 1024], P(('dp', 'branch'))
- vectors_variance: float32 [2, 1024], P(None, ('dp', 'branch'))
- offsets_variance: float32 [5120], P(('dp', 'branch'))
Outputs:
- residual: bfloat16 [16384, 1024], P(('dp', 'branch'))
- stream_grad: float32 [16384, 1024], P(('dp', 'branch'))
- mixing_next: float32 [1024, 3072], P(('dp', 'branch'))
- mixing_half: bfloat16 [1024, 3072], P(('dp', 'branch'))
- mixing_drift: float32 [1024, 3072], P(('dp', 'branch'))
- mixing_power: float32 [1024, 3072], P(('dp', 'branch'))
- merging_next: float32 [1024, 1024], P(('dp', 'branch'))
- merging_half: bfloat16 [1024, 1024], P(('dp', 'branch'))
- merging_drift: float32 [1024, 1024], P(('dp', 'branch'))
- merging_power: float32 [1024, 1024], P(('dp', 'branch'))
- expand_next: float32 [1024, 4096], P(('dp', 'branch'))
- expand_half: bfloat16 [1024, 4096], P(('dp', 'branch'))
- expand_drift: float32 [1024, 4096], P(('dp', 'branch'))
- expand_power: float32 [1024, 4096], P(('dp', 'branch'))
- shrink_next: float32 [4096, 1024], P(('dp', 'branch'))
- shrink_half: bfloat16 [4096, 1024], P(('dp', 'branch'))
- shrink_drift: float32 [4096, 1024], P(('dp', 'branch'))
- shrink_power: float32 [4096, 1024], P(('dp', 'branch'))
- vectors_next: float32 [2, 1024], P(None, ('dp', 'branch'))
- vectors_half: bfloat16 [2, 1024], P(None, ('dp', 'branch'))
- vectors_drift: float32 [2, 1024], P(None, ('dp', 'branch'))
- vectors_power: float32 [2, 1024], P(None, ('dp', 'branch'))
- offsets_next: float32 [5120], P(('dp', 'branch'))
- offsets_half: bfloat16 [5120], P(('dp', 'branch'))
- offsets_drift: float32 [5120], P(('dp', 'branch'))
- offsets_power: float32 [5120], P(('dp', 'branch'))
The draws below stay inside these ranges and needn't reach their ends.
Inputs may be any that keep to these rules, and one draw needn't show every extreme that they name: `lengths`: at least one protein of all has exactly 1024 residues.
All inputs are finite; a program needn't handle non-finite values.
Results may differ from the reference program's by a relative error of at most 0.01.
The reference program's roundings to bfloat16 on the way count: a program that leaves them out, or rounds other values in their place, can miss the bound.
Values may be sent and summed in bfloat16 or wider, within the bound.
A program may use at most 256 MiB of HBM per device.

```python
import math
import jax
import jax.numpy as jnp
from jax import lax

D = 1024
HEADS = 16
HEAD = 64
ROT = 32
FF = 4096
LEN = 1024
SEQUENCES = 16
TOKENS = 16384


def grad_size(factor):
    return factor * math.sqrt(0.56 * TOKENS)


def first_moment(key, shape, factor):
    return 0.111 * grad_size(factor) * jax.random.truncated_normal(key, -4.0, 4.0, shape, jnp.float32)


def second_moment(key, shape, factor):
    spread = jnp.exp(jax.random.uniform(key, shape, jnp.float32, math.log(0.5), math.log(2.0)))
    return 0.105 * grad_size(factor) ** 2 * spread


def bias_factors():
    return jnp.concatenate([jnp.full((FF,), 0.3, jnp.float32), jnp.full((D,), 1.0, jnp.float32)])


def draw_lengths(key, part):
    first, second = jax.random.split(key)
    drawn = jax.random.randint(first, (SEQUENCES,), LEN // 8, LEN + 1)
    picked = jax.random.randint(second, (), 0, SEQUENCES)
    return jnp.where(jnp.arange(SEQUENCES) == picked, LEN, drawn).astype(jnp.int32)


def draw_learning_rates(key, part):
    base = jnp.array([2.0 / math.sqrt(D), 2.0 / math.sqrt(max(D // 256, 1)), 2.0 / math.sqrt(D), 2.0 / math.sqrt(FF), 0.5, 0.6], jnp.float32)
    return base * jax.random.uniform(key, (6,), jnp.float32, 0.8, 1.25)


def draw_vectors(key, part):
    first, second = jax.random.split(key)
    gains = jax.random.uniform(first, (1, D), jnp.float32, 0.7, 1.3)
    biases = 0.3 * jax.random.truncated_normal(second, -3.0, 3.0, (1, D), jnp.float32)
    return jnp.concatenate([gains, biases], axis=0)


def draw_mixing_momentum(key, part):
    return first_moment(key, (D, 3 * D), 1.0)


def draw_merging_momentum(key, part):
    return first_moment(key, (D, D), 0.15)


def draw_expand_momentum(key, part):
    return first_moment(key, (D, FF), 0.3)


def draw_shrink_momentum(key, part):
    return first_moment(key, (FF, D), 0.6)


def draw_vectors_momentum(key, part):
    return first_moment(key, (2, D), 1.5)


def draw_offsets_momentum(key, part):
    return first_moment(key, (FF + D,), 1.0) * bias_factors()


def draw_mixing_variance(key, part):
    return second_moment(key, (D, 3 * D), 1.0)


def draw_merging_variance(key, part):
    return second_moment(key, (D, D), 0.15)


def draw_expand_variance(key, part):
    return second_moment(key, (D, FF), 0.3)


def draw_shrink_variance(key, part):
    return second_moment(key, (FF, D), 0.6)


def draw_vectors_variance(key, part):
    return second_moment(key, (2, D), 1.5)


def draw_offsets_variance(key, part):
    factors = bias_factors()
    return second_moment(key, (FF + D,), 1.0) * (factors * factors)


def levels(rng, extent, shards, least, largest):
    factor_of, own = 1.0, jax.random.fold_in(rng, 6)
    for position, parts in shards:
        draws = jnp.exp(jax.random.uniform(jax.random.fold_in(own, position), (parts,), jnp.float32, least / len(shards), largest / len(shards)))
        factor_of = factor_of * jnp.repeat(draws, extent[position] // parts).reshape([-1 if axis == position else 1 for axis in range(len(extent))])
    return factor_of


def bell_draw(key, shape, width, bound, cuts=(), dtype=jnp.bfloat16):
    values = jax.random.normal(key, shape, jnp.float32) * width
    if len(cuts) > 0:
        values = levels(key, shape, cuts, -0.22, 0.18) * values
    return jnp.clip(values, min=-bound, max=bound).astype(dtype)


def setup_inputs(seed: int = 0) -> dict:
    seeds = jax.random.split(jax.random.key(seed), 24)
    return {
        "stream": bell_draw(seeds[0], (TOKENS, D), 1.0, 6.0, ((0, 32),)),
        "cotangent": bell_draw(seeds[1], (TOKENS, D), 1.0, 6.0, ((0, 32),)),
        "lengths": draw_lengths(jax.random.fold_in(seeds[23], 71), 0),
        "steps_taken": jax.random.randint(seeds[3], (1,), 2, 21).astype(jnp.int32),
        "learning_rates": draw_learning_rates(jax.random.fold_in(seeds[23], 71), 0),
        "mixing": bell_draw(seeds[5], (D, 3 * D), D ** -0.5, 0.1875, ((0, 32),), jnp.float32),
        "merging": bell_draw(seeds[6], (D, D), (max(D // 256, 1)) ** -0.5, 3.0, ((0, 32),), jnp.float32),
        "expand": bell_draw(seeds[7], (D, FF), D ** -0.5, 0.1875, ((0, 32),), jnp.float32),
        "shrink": bell_draw(seeds[8], (FF, D), FF ** -0.5, 0.09375, ((0, 32),), jnp.float32),
        "vectors": draw_vectors(jax.random.fold_in(seeds[23], 71), 0),
        "offsets": bell_draw(seeds[10], (FF + D,), 0.3, 1.75, ((0, 32),), jnp.float32),
        "mixing_momentum": draw_mixing_momentum(jax.random.fold_in(seeds[23], 71), 0),
        "merging_momentum": draw_merging_momentum(jax.random.fold_in(seeds[23], 71), 0),
        "expand_momentum": draw_expand_momentum(jax.random.fold_in(seeds[23], 71), 0),
        "shrink_momentum": draw_shrink_momentum(jax.random.fold_in(seeds[23], 71), 0),
        "vectors_momentum": draw_vectors_momentum(jax.random.fold_in(seeds[23], 71), 0),
        "offsets_momentum": draw_offsets_momentum(jax.random.fold_in(seeds[23], 71), 0),
        "mixing_variance": draw_mixing_variance(jax.random.fold_in(seeds[23], 71), 0),
        "merging_variance": draw_merging_variance(jax.random.fold_in(seeds[23], 71), 0),
        "expand_variance": draw_expand_variance(jax.random.fold_in(seeds[23], 71), 0),
        "shrink_variance": draw_shrink_variance(jax.random.fold_in(seeds[23], 71), 0),
        "vectors_variance": draw_vectors_variance(jax.random.fold_in(seeds[23], 71), 0),
        "offsets_variance": draw_offsets_variance(jax.random.fold_in(seeds[23], 71), 0),
    }


beta_one = 0.9
beta_two = 0.95
adam_eps = 1e-08
decay_rate = 0.1
norm_eps = 1e-05
rope_base = 10000.0
masked_score = -1e+30
highest = lax.Precision.HIGHEST

@jax.custom_vjp
def low(v):
    return lax.optimization_barrier(v.astype(jnp.bfloat16)).astype(jnp.float32)

@jax.custom_vjp
def low_back(v):
    return v

def low_keep(v):
    return (low(v), None)

def low_pass(kept, grad):
    return (grad,)

def back_keep(v):
    return (v, None)

def back_low(kept, grad):
    return (low(grad),)
low.defvjp(low_keep, low_pass)
low_back.defvjp(back_keep, back_low)

def rope_tables(length, head_dim, rot_dim):
    places = jnp.arange(length).astype(jnp.float32)[:, None]
    column = jnp.arange(head_dim)
    paired = (column // 2).astype(jnp.float32)
    frequency = jnp.exp(paired * (-2.0 / rot_dim) * jnp.log(rope_base))
    angles = places * frequency[None, :]
    inside = (column < rot_dim)[None, :]
    cosine = jnp.where(inside, jnp.cos(angles), 1.0)
    signed = jnp.where(column % 2 == 0, -1.0, 1.0)[None, :]
    sine = jnp.where(inside, jnp.sin(angles) * signed, 0.0)
    return (cosine[:, None, :], sine[:, None, :])

def swap_pairs(tensor):
    shaped = tensor.reshape(tensor.shape[:-1] + (tensor.shape[-1] // 2, 2))
    return jnp.flip(shaped, axis=-1).reshape(tensor.shape)

def rotate(tensor, cosine, sine):
    return tensor * cosine + swap_pairs(tensor) * sine

def exact_dot(left, right):
    return jnp.dot(left, right, precision=highest, preferred_element_type=jnp.float32)

def gelu_tanh(tensor):
    return jax.nn.gelu(tensor, approximate=True)

def layer_sequence(sequence, length, mixing, merging, expand, shrink, tail_bias, hidden_bias):
    positions = jnp.arange(LEN)
    cosine, sine = rope_tables(LEN, HEAD, ROT)
    projected = low_back(exact_dot(sequence, mixing))
    query_rows = low(rotate(projected[:, :D].reshape(LEN, HEADS, HEAD), cosine, sine))
    key_rows = low(rotate(projected[:, D:2 * D].reshape(LEN, HEADS, HEAD), cosine, sine))
    value_rows = low(projected[:, 2 * D:].reshape(LEN, HEADS, HEAD))
    scores = low_back(jnp.einsum('qhd,khd->hqk', query_rows, key_rows, precision=highest) * HEAD ** (-0.5))
    causal = positions[:, None] >= positions[None, :]
    scores = jnp.where(causal[None], scores, masked_score)
    row_max = lax.optimization_barrier(jnp.max(scores, axis=2, keepdims=True))
    log_total = row_max + jnp.log(lax.optimization_barrier(jnp.sum(jnp.exp(scores - row_max), axis=2, keepdims=True)))
    weights = jnp.exp(scores - log_total)
    mixed = jnp.einsum('hqk,khd->qhd', low(weights), value_rows, precision=highest)
    mixed = jnp.where((positions < length)[:, None, None], mixed, 0.0)
    attention = low(low_back(mixed)).reshape(LEN, D)
    attn_branch = low(exact_dot(attention, merging))
    before_gelu = low_back(exact_dot(sequence, expand) + hidden_bias)
    hidden = low(gelu_tanh(before_gelu))
    feed_branch = low(exact_dot(hidden, shrink) + tail_bias)
    return attn_branch + feed_branch

def forward(stream_f, mixing, merging, expand, shrink, vectors, offsets, lengths):
    centred = stream_f - lax.optimization_barrier(jnp.mean(stream_f, axis=1, keepdims=True))
    inverse = lax.rsqrt(lax.optimization_barrier(jnp.mean(centred * centred, axis=1, keepdims=True)) + norm_eps)
    normed = low(centred * inverse * vectors[0] + vectors[1])
    sequences = normed.reshape(SEQUENCES, LEN, D)
    hidden_bias = offsets[:FF]
    tail_bias = offsets[FF:]

    def per_sequence(carried, sequence_in):
        outcome = jax.checkpoint(layer_sequence)(sequence_in[0], sequence_in[1], mixing, merging, expand, shrink, tail_bias, hidden_bias)
        return (carried, outcome)
    unused, branches = lax.scan(per_sequence, jnp.zeros((), jnp.float32), (sequences, lengths))
    return stream_f + branches.reshape(TOKENS, D)

def adam_update(master, gradient, momentum, variance, rate, count, decay):
    drift = beta_one * momentum + (1.0 - beta_one) * gradient
    power = beta_two * variance + (1.0 - beta_two) * gradient * gradient
    first_fix = 1.0 - jnp.power(beta_one, count)
    second_fix = 1.0 - jnp.power(beta_two, count)
    moved = drift / first_fix / (jnp.sqrt(power / second_fix) + adam_eps)
    updated = master - rate * (moved + decay * master)
    return (updated, updated.astype(jnp.bfloat16), drift, power)

def reference(stream, cotangent, lengths, steps_taken, learning_rates, mixing, merging, expand, shrink, vectors, offsets, mixing_momentum, merging_momentum, expand_momentum, shrink_momentum, vectors_momentum, offsets_momentum, mixing_variance, merging_variance, expand_variance, shrink_variance, vectors_variance, offsets_variance):
    masters = (mixing, merging, expand, shrink, vectors, offsets)
    floats = [master.astype(jnp.bfloat16).astype(jnp.float32) for master in masters]
    positions = jnp.arange(LEN)
    live_rows = (positions[None, :] < lengths[:, None]).reshape(TOKENS)
    grads_masked = jnp.where(live_rows[:, None], cotangent.astype(jnp.float32), 0.0)
    outputs, pullback = jax.vjp(lambda *tensors: forward(*tensors, lengths), stream.astype(jnp.float32), floats[0], floats[1], floats[2], floats[3], floats[4], floats[5])
    gradients = pullback(grads_masked)
    count = steps_taken[0].astype(jnp.float32)
    mixing_next, mixing_half, mixing_drift, mixing_power = adam_update(mixing, gradients[1], mixing_momentum, mixing_variance, learning_rates[0], count, decay_rate)
    merging_next, merging_half, merging_drift, merging_power = adam_update(merging, gradients[2], merging_momentum, merging_variance, learning_rates[1], count, decay_rate)
    expand_next, expand_half, expand_drift, expand_power = adam_update(expand, gradients[3], expand_momentum, expand_variance, learning_rates[2], count, decay_rate)
    shrink_next, shrink_half, shrink_drift, shrink_power = adam_update(shrink, gradients[4], shrink_momentum, shrink_variance, learning_rates[3], count, decay_rate)
    vectors_next, vectors_half, vectors_drift, vectors_power = adam_update(vectors, gradients[5], vectors_momentum, vectors_variance, learning_rates[4], count, 0.0)
    offsets_next, offsets_half, offsets_drift, offsets_power = adam_update(offsets, gradients[6], offsets_momentum, offsets_variance, learning_rates[5], count, 0.0)
    return (outputs.astype(jnp.bfloat16), gradients[0], mixing_next, mixing_half, mixing_drift, mixing_power, merging_next, merging_half, merging_drift, merging_power, expand_next, expand_half, expand_drift, expand_power, shrink_next, shrink_half, shrink_drift, shrink_power, vectors_next, vectors_half, vectors_drift, vectors_power, offsets_next, offsets_half, offsets_drift, offsets_power)
```

```python
import functools

import jax
import jax.numpy as jnp
from jax import lax
from jax.sharding import PartitionSpec as P

HEAD = 64
ROT = 32
beta_one = 0.9
beta_two = 0.95
adam_eps = 1e-08
decay_rate = 0.1
norm_eps = 1e-05
rope_base = 10000.0
masked_score = -1e30
BF = jnp.bfloat16
F32 = jnp.float32


def dot(left, right):
    return jnp.dot(left, right, preferred_element_type=F32)


def dot_left(left, right):
    return lax.dot_general(left, right, (((0,), (0,)), ((), ())), preferred_element_type=F32)


def dot_right(left, right):
    return lax.dot_general(left, right, (((1,), (1,)), ((), ())), preferred_element_type=F32)


def rope_tables(length):
    places = jnp.arange(length).astype(F32)[:, None]
    column = jnp.arange(2 * HEAD) % HEAD
    paired = (column // 2).astype(F32)
    frequency = jnp.exp(paired * (-2.0 / ROT) * jnp.log(rope_base))
    angles = places * frequency[None, :]
    inside = (column < ROT)[None, :]
    cosine = jnp.where(inside, jnp.cos(angles), 1.0)
    signed = jnp.where(column % 2 == 0, -1.0, 1.0)[None, :]
    sine = jnp.where(inside, jnp.sin(angles) * signed, 0.0)
    return cosine, sine


def adam_update(master, gradient, momentum, variance, rate, count, decay):
    drift = beta_one * momentum + (1.0 - beta_one) * gradient
    power = beta_two * variance + (1.0 - beta_two) * gradient * gradient
    first_fix = 1.0 - jnp.power(beta_one, count)
    second_fix = 1.0 - jnp.power(beta_two, count)
    moved = drift / first_fix / (jnp.sqrt(power / second_fix) + adam_eps)
    updated = master - rate * (moved + decay * master)
    return (updated, updated.astype(BF), drift, power)


class Plan:
    def __init__(self, n, stream, mixing, merging, expand, shrink, vectors, offsets):
        self.n = n
        self.own_rows, self.D = stream.shape
        self.rows = 2 * self.own_rows
        self.W = self.D // 2
        self.FF = expand.shape[1]
        self.rq = mixing.shape[0]
        self.rr = merging.shape[0]
        self.mr = max(16, self.rr)
        self.hb = shrink.shape[0]
        self.C = 4 if self.hb >= 64 else 2
        self.q = self.hb // self.C
        self.CW = self.FF // 2 // self.C
        self.wb = self.D // self.CW
        self.vc = vectors.shape[1]
        self.ow = offsets.shape[0]
        self.o_merge = 6 * self.rq
        self.o_small = self.o_merge + 2 * self.mr
        self.g_rows = self.o_small + 16
        self.c_rows = 2 * self.rq + self.wb * self.q


def pick(array, index, axis):
    return lax.dynamic_index_in_dim(array, index, axis, keepdims=False)


def small_pack(p, gain_bias, offs, plane):
    hid = pick(offs[: p.FF].reshape(p.n, 2, p.C, p.q), plane, 1)
    hid = hid.transpose(1, 0, 2).reshape(-1)
    flat = jnp.concatenate([gain_bias.reshape(-1), hid, offs[p.FF :]])
    flat = jnp.pad(flat, (0, 16 * p.W - flat.shape[0]))
    return flat.reshape(16, p.W)


def pack_for(p, plane, mixing, expand, vectors, offsets, linear):
    mix = pick(mixing.reshape(p.rq, 3, 2, p.W), plane, 2).transpose(1, 0, 2)
    exp = pick(expand.reshape(p.rq, p.n, 2, p.C, p.q), plane, 2)
    exp = exp.transpose(2, 0, 1, 3).reshape(p.C, p.rq, p.CW)
    gain_bias = lax.dynamic_update_slice(jnp.zeros((2, p.D), BF), vectors, (0, linear * p.vc))
    offs = lax.dynamic_update_slice(jnp.zeros((p.FF + p.D,), BF), offsets, (linear * p.ow,))
    return mix, exp, small_pack(p, gain_bias, offs, plane)


def swap_branch(tree):
    return jax.tree.map(lambda a: lax.ppermute(a, "branch", [(0, 1), (1, 0)]), tree)


def both(b, mine, theirs, axis):
    first = jnp.where(b == 0, mine, theirs)
    second = jnp.where(b == 0, theirs, mine)
    return jnp.concatenate([first, second], axis=axis)


def merge_perm(n):
    return [(linear, (linear % n) * 2 + linear // n) for linear in range(2 * n)]


def prepare(p, b, linear, mixing, merging, expand, shrink, vectors, offsets):
    mixing, merging, expand, shrink, vectors, offsets = (
        a.astype(BF) for a in (mixing, merging, expand, shrink, vectors, offsets)
    )
    keep = pack_for(p, b, mixing, expand, vectors, offsets, linear)
    give = pack_for(p, 1 - b, mixing, expand, vectors, offsets, linear)
    got = swap_branch(give)
    mix = both(b, keep[0], got[0], 1).reshape(6 * p.rq, p.W)
    small = keep[2] + got[2]
    mer = lax.ppermute(merging, ("dp", "branch"), merge_perm(p.n))
    mer = mer.reshape(p.rr, 2, p.W).transpose(1, 0, 2)
    mer = jnp.pad(mer, ((0, 0), (0, p.mr - p.rr), (0, 0))).reshape(2 * p.mr, p.W)
    group = jnp.concatenate([mix, mer, small], axis=0)
    exp = both(b, keep[1], got[1], 1)
    shr = shrink.reshape(p.C, p.q, p.wb, p.CW).transpose(0, 2, 1, 3).reshape(p.C, -1, p.CW)
    chunks = jnp.concatenate([exp, shr], axis=1)
    return group, chunks


def swap_pairs(tensor):
    shaped = tensor.reshape(tensor.shape[:-1] + (tensor.shape[-1] // 2, 2))
    return jnp.flip(shaped, axis=-1).reshape(tensor.shape)


def core(p, b, group, chunks, stream, cotangent, lengths):
    heads = p.W // HEAD
    full = lax.all_gather(group, "dp", axis=0)
    parts = lax.all_gather(chunks, "dp", axis=0)
    both_rows = lax.all_gather(stream, "branch", axis=0, tiled=True).astype(F32)
    grads = lax.all_gather(cotangent, "branch", axis=0, tiled=True)
    positions = jnp.arange(p.rows)
    live = positions < lengths[0]
    g = jnp.where(live[:, None], grads, jnp.zeros_like(grads))
    small = jnp.sum(full[:, p.o_small :].astype(F32), axis=0)
    flat = small.reshape(-1)
    gain, bias = flat[: p.D], flat[p.D : 2 * p.D]
    hidden_bias = flat[2 * p.D : 2 * p.D + p.FF // 2]
    tail = flat[2 * p.D + p.FF // 2 : 3 * p.D + p.FF // 2]
    wq, wk, wv = (
        full[:, t * 2 * p.rq : (t + 1) * 2 * p.rq].reshape(p.D, p.W) for t in range(3)
    )
    wo = jnp.concatenate(
        [
            full[:, p.o_merge + t * p.mr : p.o_merge + t * p.mr + p.rr].reshape(p.W, p.W)
            for t in range(2)
        ],
        axis=1,
    )
    mean = jnp.mean(both_rows, axis=1, keepdims=True)
    centred = both_rows - mean
    inverse = lax.rsqrt(jnp.mean(centred * centred, axis=1, keepdims=True) + norm_eps)
    z = centred * inverse
    normed = (z * gain + bias).astype(BF)
    cosine, sine = rope_tables(p.rows)
    cosine = jnp.tile(cosine, (1, heads // 2))
    sine = jnp.tile(sine, (1, heads // 2))

    def turn(a):
        return (a * cosine + swap_pairs(a) * sine).astype(BF)

    def turn_back(a):
        return (a * cosine + swap_pairs(a * sine)).astype(BF)

    def split(a):
        return a.reshape(p.rows, heads, HEAD)

    query = split(turn(dot(normed, wq)))
    key = split(turn(dot(normed, wk)))
    value = split(dot(normed, wv).astype(BF))
    scores = jnp.einsum("qhd,khd->hqk", query, key, preferred_element_type=F32) * HEAD**-0.5
    scores = jnp.where((positions[:, None] >= positions[None, :])[None], scores, masked_score)
    weights = jax.nn.softmax(scores, axis=2)
    rounded = weights.astype(BF)
    mixed = jnp.einsum("hqk,khd->qhd", rounded, value, preferred_element_type=F32)
    att = jnp.where(live[:, None], mixed.reshape(p.rows, p.W), 0.0).astype(BF)
    d_att = split(dot_right(g, wo).astype(BF))
    d_weights = jnp.einsum("qhd,khd->hqk", d_att, value, preferred_element_type=F32)
    delta = jnp.sum(weights * d_weights, axis=2, keepdims=True)
    d_scores = (weights * (d_weights - delta)).astype(BF)
    d_value = jnp.einsum("hqk,qhd->khd", rounded, d_att, preferred_element_type=F32)
    d_query = jnp.einsum("hqk,khd->qhd", d_scores, key, preferred_element_type=F32) * HEAD**-0.5
    d_key = jnp.einsum("hqk,qhd->khd", d_scores, query, preferred_element_type=F32) * HEAD**-0.5
    dq = turn_back(d_query.reshape(p.rows, p.W))
    dk = turn_back(d_key.reshape(p.rows, p.W))
    dv = d_value.reshape(p.rows, p.W).astype(BF)
    out = dot(att, wo)
    d_norm = dot_right(dq, wq) + dot_right(dk, wk) + dot_right(dv, wv)
    grad_mix = jnp.stack([dot_left(normed, t).reshape(p.n, 2 * p.rq, p.W) for t in (dq, dk, dv)], 1)
    grad_mer = dot_left(att, g).reshape(p.n, p.rr, 2, p.W).transpose(0, 2, 1, 3)
    grad_mer = jnp.pad(grad_mer, ((0, 0), (0, 0), (0, p.mr - p.rr), (0, 0)))
    grad_group = jnp.concatenate(
        [grad_mix.reshape(p.n, -1, p.W), grad_mer.reshape(p.n, -1, p.W)], axis=1
    )
    grad_chunks = []
    bias_grads = []
    for j in range(p.C):
        we = parts[:, j, : 2 * p.rq].reshape(p.D, p.CW)
        ws = parts[:, j, 2 * p.rq :].reshape(p.n, p.wb, p.q, p.CW).transpose(0, 2, 1, 3)
        ws = ws.reshape(p.CW, p.D)
        pre = dot(normed, we) + hidden_bias[j * p.CW : (j + 1) * p.CW]
        activated, gelu_back = jax.vjp(lambda t: jax.nn.gelu(t, approximate=True), pre)
        hidden = activated.astype(BF)
        out = out + dot(hidden, ws)
        d_pre = gelu_back(dot_right(g, ws))[0].astype(BF)
        d_norm = d_norm + dot_right(d_pre, we)
        grad_we = dot_left(normed, d_pre).reshape(p.n, 2 * p.rq, p.CW)
        grad_ws = dot_left(hidden, g).reshape(p.n, p.q, p.wb, p.CW).transpose(0, 2, 1, 3)
        grad_chunks.append(
            jnp.concatenate([grad_we, grad_ws.reshape(p.n, -1, p.CW)], axis=1)
        )
        bias_grads.append(jnp.sum(d_pre.astype(F32), axis=0))
    tail_grad = jnp.sum(g.astype(F32), axis=0)
    small_grad = jnp.concatenate(
        [jnp.sum(d_norm * z, axis=0), jnp.sum(d_norm, axis=0), *bias_grads, tail_grad]
    )
    small_grad = jnp.pad(small_grad, (0, 16 * p.W - small_grad.shape[0])).reshape(16, p.W)
    out = out + jnp.where(b == 0, tail, 0.0)
    own = lax.psum_scatter(out.astype(BF), "branch", scatter_dimension=0, tiled=True).astype(F32)
    residual = (stream.astype(F32) + own).astype(BF)
    d_own = lax.psum_scatter(d_norm.astype(BF), "branch", scatter_dimension=0, tiled=True)
    d_own = d_own.astype(F32)

    def mine(a):
        return lax.dynamic_slice_in_dim(a, b * p.own_rows, p.own_rows, 0)

    du = d_own * gain
    z_own = mine(z)
    stream_grad = mine(g).astype(F32) + mine(inverse) * (
        du
        - jnp.mean(du, axis=1, keepdims=True)
        - z_own * jnp.mean(du * z_own, axis=1, keepdims=True)
    )

    def scatter(a):
        return lax.psum_scatter(a.astype(BF), "dp", scatter_dimension=0, tiled=False).astype(F32)

    return (
        residual,
        stream_grad,
        scatter(grad_group),
        scatter(jnp.stack(grad_chunks, 1)),
        lax.psum(small_grad, "dp"),
    )


def finish(p, b, linear, group, chunks, small):
    mix = group[: 6 * p.rq].reshape(3, 2, p.rq, p.W)
    exp = chunks[:, : 2 * p.rq].reshape(p.C, 2, p.rq, p.CW)
    keep = (pick(mix, b, 1), pick(exp, b, 1), small)
    give = (pick(mix, 1 - b, 1), pick(exp, 1 - b, 1), small)
    got = swap_branch(jax.tree.map(lambda a: a.astype(BF), give[:2]) + (give[2],))

    def weave(axis, mine, theirs):
        theirs = theirs.astype(F32)
        return jnp.stack([jnp.where(b == 0, mine, theirs), jnp.where(b == 0, theirs, mine)], axis)

    grad_mixing = weave(2, keep[0].transpose(1, 0, 2), got[0].transpose(1, 0, 2))
    grad_mixing = grad_mixing.reshape(p.rq, -1)

    def columns(a):
        return a.reshape(p.C, p.rq, p.n, p.q).transpose(1, 2, 0, 3)

    grad_expand = weave(2, columns(keep[1]), columns(got[1])).reshape(p.rq, p.FF)
    mer = group[p.o_merge : p.o_merge + 2 * p.mr].reshape(2, p.mr, p.W)[:, : p.rr]
    mer = mer.transpose(1, 0, 2).reshape(p.rr, p.D)
    grad_merging = lax.ppermute(
        mer.astype(BF), ("dp", "branch"), [(t, s) for s, t in merge_perm(p.n)]
    ).astype(F32)
    shr = chunks[:, 2 * p.rq : 2 * p.rq + p.wb * p.q].reshape(p.C, p.wb, p.q, p.CW)
    grad_shrink = shr.transpose(0, 2, 1, 3).reshape(p.hb, p.D)
    mine, theirs = keep[2].reshape(-1), got[2].reshape(-1)
    total = mine + theirs
    grad_vectors = lax.dynamic_slice(
        total[: 2 * p.D].reshape(2, p.D), (0, linear * p.vc), (2, p.vc)
    )
    lo, hi = 2 * p.D, 2 * p.D + p.FF // 2

    def hidden(a):
        return a[lo:hi].reshape(p.C, p.n, p.q).transpose(1, 0, 2)

    hid = weave(1, hidden(mine), hidden(theirs)).reshape(p.FF)
    tail = mine[hi : hi + p.D]
    offs = jnp.concatenate([hid, tail])
    grad_offsets = lax.dynamic_slice(offs, (linear * p.ow,), (p.ow,))
    return grad_mixing, grad_merging, grad_expand, grad_shrink, grad_vectors, grad_offsets


def local(n, stream, cotangent, lengths, steps_taken, learning_rates, *params):
    masters, momenta, variances = params[:6], params[6:12], params[12:]
    p = Plan(n, stream, *masters)
    b = lax.axis_index("branch")
    linear = lax.axis_index("dp") * 2 + b
    group, chunks = prepare(p, b, linear, *masters)
    residual, stream_grad, group, chunks, small = core(
        p, b, group, chunks, stream, cotangent, lengths
    )
    grads = finish(p, b, linear, group, chunks, small)
    count = steps_taken[0].astype(F32)
    outs = [residual, stream_grad]
    for k in range(6):
        decay = decay_rate if k < 4 else 0.0
        outs.extend(
            adam_update(
                masters[k], grads[k], momenta[k], variances[k], learning_rates[k], count, decay
            )
        )
    return tuple(outs)


def solution(mesh):
    rows = P(("dp", "branch"), None)
    cols = P(None, ("dp", "branch"))
    flat = P(("dp", "branch"))
    six = (rows, rows, rows, rows, cols, flat)
    return jax.shard_map(
        functools.partial(local, mesh.shape["dp"]),
        mesh=mesh,
        in_specs=(rows, rows, P("dp"), P(), P()) + six * 3,
        out_specs=(rows, rows) + sum(((s,) * 4 for s in six), ()),
        check_vma=False,
    )
```

```python
import functools

import jax
import jax.numpy as jnp
from jax import lax
from jax.experimental import pallas as pl
from jax.experimental.pallas import tpu as pltpu
from jax.sharding import PartitionSpec as P

HEAD = 64
ROT = 32
beta_one = 0.9
beta_two = 0.95
adam_eps = 1e-08
decay_rate = 0.1
norm_eps = 1e-05
rope_base = 10000.0
masked_score = -1e30
BF = jnp.bfloat16
F32 = jnp.float32


def dot(left, right):
    return jnp.dot(left, right, preferred_element_type=F32)


def dot_left(left, right):
    return lax.dot_general(left, right, (((0,), (0,)), ((), ())), preferred_element_type=F32)


def dot_right(left, right):
    return lax.dot_general(left, right, (((1,), (1,)), ((), ())), preferred_element_type=F32)


def rope_tables(length):
    places = jnp.arange(length).astype(F32)[:, None]
    column = jnp.arange(2 * HEAD) % HEAD
    paired = (column // 2).astype(F32)
    frequency = jnp.exp(paired * (-2.0 / ROT) * jnp.log(rope_base))
    angles = places * frequency[None, :]
    inside = (column < ROT)[None, :]
    cosine = jnp.where(inside, jnp.cos(angles), 1.0)
    signed = jnp.where(column % 2 == 0, -1.0, 1.0)[None, :]
    sine = jnp.where(inside, jnp.sin(angles) * signed, 0.0)
    return cosine, sine


def adam_update(master, gradient, momentum, variance, rate, count, decay):
    drift = beta_one * momentum + (1.0 - beta_one) * gradient
    power = beta_two * variance + (1.0 - beta_two) * gradient * gradient
    first_fix = 1.0 - jnp.power(beta_one, count)
    second_fix = 1.0 - jnp.power(beta_two, count)
    moved = drift / first_fix / (jnp.sqrt(power / second_fix) + adam_eps)
    updated = master - rate * (moved + decay * master)
    return (updated, updated.astype(BF), drift, power)


class Plan:
    def __init__(self, n, stream, mixing, merging, expand, shrink, vectors, offsets):
        self.n = n
        self.own_rows, self.D = stream.shape
        self.rows = 2 * self.own_rows
        self.W = self.D // 2
        self.FF = expand.shape[1]
        self.rq = mixing.shape[0]
        self.rr = merging.shape[0]
        self.mr = max(16, self.rr)
        self.hb = shrink.shape[0]
        self.C = 4 if self.hb >= 64 else 2
        self.q = self.hb // self.C
        self.CW = self.FF // 2 // self.C
        self.wb = self.D // self.CW
        self.vc = vectors.shape[1]
        self.ow = offsets.shape[0]
        self.o_merge = 6 * self.rq
        self.o_small = self.o_merge + 2 * self.mr
        self.g_rows = self.o_small + 16
        self.c_rows = 2 * self.rq + self.wb * self.q


def pick(array, index, axis):
    return lax.dynamic_index_in_dim(array, index, axis, keepdims=False)


def small_pack(p, gain_bias, offs, plane):
    hid = pick(offs[: p.FF].reshape(p.n, 2, p.C, p.q), plane, 1)
    hid = hid.transpose(1, 0, 2).reshape(-1)
    flat = jnp.concatenate([gain_bias.reshape(-1), hid, offs[p.FF :]])
    flat = jnp.pad(flat, (0, 16 * p.W - flat.shape[0]))
    return flat.reshape(16, p.W)


def pack_for(p, plane, mixing, expand, vectors, offsets, linear):
    mix = pick(mixing.reshape(p.rq, 3, 2, p.W), plane, 2).transpose(1, 0, 2)
    exp = pick(expand.reshape(p.rq, p.n, 2, p.C, p.q), plane, 2)
    exp = exp.transpose(2, 0, 1, 3).reshape(p.C, p.rq, p.CW)
    gain_bias = lax.dynamic_update_slice(jnp.zeros((2, p.D), BF), vectors, (0, linear * p.vc))
    offs = lax.dynamic_update_slice(jnp.zeros((p.FF + p.D,), BF), offsets, (linear * p.ow,))
    return mix, exp, small_pack(p, gain_bias, offs, plane)


def swap_branch(tree):
    return jax.tree.map(lambda a: lax.ppermute(a, "branch", [(0, 1), (1, 0)]), tree)


def both(b, mine, theirs, axis):
    first = jnp.where(b == 0, mine, theirs)
    second = jnp.where(b == 0, theirs, mine)
    return jnp.concatenate([first, second], axis=axis)


def merge_perm(n):
    return [(linear, (linear % n) * 2 + linear // n) for linear in range(2 * n)]


def prepare(p, b, linear, mixing, merging, expand, shrink, vectors, offsets):
    mixing, merging, expand, shrink, vectors, offsets = (
        a.astype(BF) for a in (mixing, merging, expand, shrink, vectors, offsets)
    )
    keep = pack_for(p, b, mixing, expand, vectors, offsets, linear)
    give = pack_for(p, 1 - b, mixing, expand, vectors, offsets, linear)
    got = swap_branch(give)
    mix = both(b, keep[0], got[0], 1).reshape(6 * p.rq, p.W)
    small = keep[2] + got[2]
    mer = lax.ppermute(merging, ("dp", "branch"), merge_perm(p.n))
    mer = mer.reshape(p.rr, 2, p.W).transpose(1, 0, 2)
    mer = jnp.pad(mer, ((0, 0), (0, p.mr - p.rr), (0, 0))).reshape(2 * p.mr, p.W)
    group = jnp.concatenate([mix, mer, small], axis=0)
    exp = both(b, keep[1], got[1], 1)
    shr = shrink.reshape(p.C, p.q, p.wb, p.CW).transpose(0, 2, 1, 3).reshape(p.C, -1, p.CW)
    chunks = jnp.concatenate([exp, shr], axis=1)
    return group, chunks


MESH = pl.DeviceIdType.MESH
BLOCK = 256


def turned(a, cosine, sine, back):
    lanes = a.shape[1]
    even = lax.broadcasted_iota(jnp.int32, a.shape, 1) % 2 == 0
    t = a * sine if back else a
    swapped = jnp.where(even, pltpu.roll(t, lanes - 1, 1), pltpu.roll(t, 1, 1))
    return a * cosine + (swapped if back else swapped * sine)


def tile_lanes(a, times):
    return jnp.concatenate([a] * times, axis=1) if times > 1 else a


def flat2(a):
    return a.reshape(-1, a.shape[-1])


def gelu_parts(pre):
    root = 0.7978845608028654
    square = pre * pre
    t = jnp.tanh(root * pre * (1.0 + 0.044715 * square))
    hidden = 0.5 * pre * (1.0 + t)
    slope = 0.5 * (1.0 + t) + 0.5 * pre * (1.0 - t * t) * root * (1.0 + 0.134145 * square)
    return hidden, slope


def block_kernel(
    p,
    a_in,
    b_in,
    c_in,
    stream,
    cotangent,
    length,
    cos_ref,
    sin_ref,
    res_out,
    sg_out,
    ga_out,
    gb_out,
    gc_out,
    gs_out,
    wa,
    wb,
    wc,
    ws,
    x,
    g,
    normed,
    lanes,
    dk_acc,
    dv_acc,
    out,
    dnorm,
    small,
    trade,
    sib_a,
    sib_b,
    sib_c,
    sib_s,
    slot_a,
    slot_b,
    slot_c,
    slot_s,
    ag_send,
    ag_recv,
    as_send,
    as_recv,
    rs_send,
    rs_recv,
    ss_send,
    ss_recv,
    x_send,
    x_recv,
    own_sem,
):
    n, C, D, W, CW, rq, q = p.n, p.C, p.D, p.W, p.CW, p.rq, p.q
    m = n // 2
    half = m // 2
    blocks = p.rows // BLOCK
    pairs = W // 128
    groups = CW // 128
    at_q, at_k, at_v, at_att, at_da = (t * pairs for t in range(5))
    at_hid, at_dpre = 0, groups
    d = lax.axis_index("dp")
    b = lax.axis_index("branch")
    core = lax.rem(d, 2)
    chip = d // 2
    ring = jnp.where(lax.rem(chip, 2) == 0, chip // 2, m - 1 - chip // 2)
    step = 1 - 2 * core

    def around(k):
        pos = lax.rem(ring + step * k + m, m)
        return jnp.where(pos < half, 2 * pos, 2 * (m - 1 - pos) + 1)

    ahead = (2 * around(1) + core, b)
    behind = (2 * around(-1) + core, b)
    sibling = (d + step, b)
    partner = (d, 1 - b)
    ways = (ahead, behind)

    barrier = pltpu.get_barrier_semaphore()
    for other in (ahead, behind, sibling, partner):
        pl.semaphore_signal(barrier, inc=1, device_id=other, device_id_type=MESH)
    pl.semaphore_wait(barrier, 4)

    def remote(src, dst, send, recv, to):
        return pltpu.make_async_remote_copy(
            src_ref=src, dst_ref=dst, send_sem=send, recv_sem=recv, device_id=to, device_id_type=MESH
        )

    own_rows = pl.ds(pl.multiple_of(b * p.own_rows, p.own_rows), p.own_rows)
    their_rows = pl.ds(pl.multiple_of((1 - b) * p.own_rows, p.own_rows), p.own_rows)

    def gather_ref(k):
        return wa if k == 0 else wb if k == 1 else wc.at[k - 2]

    def last_hop(way):
        return half - way

    def gather_copy(k, way, hop):
        shard = gather_ref(k).at[around((1 - hop) * (1 - 2 * way)), core]
        return remote(shard, shard, ag_send.at[k, way, hop], ag_recv.at[k, way, hop], ways[way])

    def gather_arrival(k, way, hop):
        shard = gather_ref(k).at[around(-hop * (1 - 2 * way)), core]
        return remote(shard, shard, ag_send.at[k, way, hop], ag_recv.at[k, way, hop], ways[way])

    def gather_sibling(k, whose):
        part = gather_ref(k).at[:, whose]
        return remote(part, part, as_send.at[k], as_recv.at[k], sibling)

    def gather_start(k):
        for way in range(2):
            gather_copy(k, way, 1).start()

    def gather_event(k, hop):
        for way in range(2):
            if hop <= last_hop(way):
                gather_arrival(k, way, hop).wait_recv()
                if hop < last_hop(way):
                    gather_copy(k, way, hop + 1).start()
        if hop == half:
            gather_sibling(k, core).start()

    def gather_ready(k):
        gather_sibling(k, 1 - core).wait_recv()

    def gather_done(k):
        for way in range(2):
            for hop in range(1, last_hop(way) + 1):
                gather_copy(k, way, hop).wait_send()
        gather_sibling(k, core).wait_send()

    def scatter_refs(k):
        if k == 0:
            return wa, sib_a, slot_a, ga_out, 6 * rq
        if k == 1:
            return wb, sib_b, slot_b, gb_out, 2 * p.mr
        if k < C + 2:
            return wc.at[k - 2], sib_c.at[k - 2], slot_c.at[k - 2], gc_out.at[k - 2], p.c_rows
        return ws, sib_s, slot_s, gs_out, 16

    def scatter_sibling(k):
        whole, sib, _, _, rows = scatter_refs(k)
        src = whole.at[:, 1 - core, pl.ds(0, rows)]
        return remote(src, sib, ss_send.at[k], ss_recv.at[k], sibling)

    def slot_of(way, hop):
        return (hop - 1) if way == 0 else half + hop - 1

    def scatter_copy(k, way, hop):
        whole, _, slots, _, rows = scatter_refs(k)
        target = around((last_hop(way) + 1 - hop) * (1 - 2 * way))
        src = whole.at[target, core, pl.ds(0, rows)]
        return remote(
            src, slots.at[slot_of(way, hop)], rs_send.at[k, way, hop], rs_recv.at[k, way, hop], ways[way]
        )

    def scatter_event(k, hop):
        whole, sib, slots, result, rows = scatter_refs(k)
        if hop == 0:
            scatter_sibling(k).start()
            return
        if hop == 1:
            scatter_sibling(k).wait_recv()
        for way in range(2):
            if hop <= last_hop(way):
                target = around((last_hop(way) + 1 - hop) * (1 - 2 * way))
                here = whole.at[target, core, pl.ds(0, rows)]
                total = here[...].astype(F32) + sib[target].astype(F32)
                if hop > 1:
                    scatter_copy(k, way, hop - 1).wait_recv()
                    total = total + slots[slot_of(way, hop - 1)].astype(F32)
                here[...] = total.astype(BF)
                scatter_copy(k, way, hop).start()
        if hop == half + 1:
            total = whole[chip, core, pl.ds(0, rows)].astype(F32) + sib[chip].astype(F32)
            for way in range(2):
                scatter_copy(k, way, last_hop(way)).wait_recv()
                total = total + slots[slot_of(way, last_hop(way))].astype(F32)
            result[...] = total
            for way in range(2):
                for sent in range(1, last_hop(way) + 1):
                    scatter_copy(k, way, sent).wait_send()
            scatter_sibling(k).wait_send()

    give_x = remote(stream, x.at[own_rows], x_send.at[0], x_recv.at[0], partner)
    give_g = remote(cotangent, g.at[own_rows], x_send.at[1], x_recv.at[1], partner)
    keep_x = pltpu.make_async_copy(stream, x.at[own_rows], own_sem.at[0])
    keep_g = pltpu.make_async_copy(cotangent, g.at[own_rows], own_sem.at[1])
    wa[chip, core] = a_in[...]
    gather_start(0)
    give_x.start()
    wb[chip, core] = b_in[...]
    gather_start(1)
    give_g.start()
    keep_x.start()
    keep_g.start()
    for j in range(C):
        wc[j, chip, core] = c_in[j]
    for hop in range(1, half + 1):
        gather_event(0, hop)
        gather_event(1, hop)
        if hop == half - 1:
            gather_start(2)
    for j in range(1, C):
        gather_start(2 + j)

    def weight(t):
        return flat2(wa[:, :, t * 2 * rq : (t + 1) * 2 * rq, :])

    def merge_weight(t):
        whole = wb[:, :, t * p.mr : (t + 1) * p.mr, :]
        if p.mr == p.rr:
            return flat2(whole)
        whole = whole.astype(F32).reshape(n, p.mr, W)[:, : p.rr]
        return whole.reshape(W, W).astype(BF)

    keep_x.wait()
    keep_g.wait()
    gather_ready(0)
    small[:16] = jnp.sum(wa[:, :, 6 * rq :, :].reshape(n, 16, W).astype(F32), axis=0)
    give_x.wait_recv()
    gather_ready(1)
    give_g.wait_recv()

    def wide(row):
        return jnp.concatenate([small[row : row + 1], small[row + 1 : row + 2]], axis=1)

    def unit(rows):
        v = x[rows].astype(F32)
        centred = v - jnp.mean(v, axis=1, keepdims=True)
        inverse = lax.rsqrt(jnp.mean(centred * centred, axis=1, keepdims=True) + norm_eps)
        return centred * inverse, inverse

    def rows_of(i):
        return pl.ds(pl.multiple_of(i * BLOCK, BLOCK), BLOCK)

    def project(i, carry):
        rows = rows_of(i)
        z, _ = unit(rows)
        nb = (z * wide(0) + wide(2)).astype(BF)
        normed[rows] = nb
        cosine = tile_lanes(cos_ref[rows], pairs)
        sine = tile_lanes(sin_ref[rows], pairs)
        query = (turned(dot(nb, weight(0)), cosine, sine, False) * HEAD**-0.5).astype(BF)
        key = turned(dot(nb, weight(1)), cosine, sine, False).astype(BF)
        value = dot(nb, weight(2)).astype(BF)
        position = lax.broadcasted_iota(jnp.int32, (BLOCK, D), 0) + i * BLOCK
        gb = jnp.where(position < length[0], g[rows].astype(F32), 0.0).astype(BF)
        g[rows] = gb
        da = (dot_right(gb[:, :W], merge_weight(0)) + dot_right(gb[:, W:], merge_weight(1))).astype(BF)
        for t in range(pairs):
            cut = slice(t * 128, (t + 1) * 128)
            lanes[at_q + t, rows] = query[:, cut]
            lanes[at_k + t, rows] = key[:, cut]
            lanes[at_v + t, rows] = value[:, cut]
            lanes[at_da + t, rows] = da[:, cut]
        return carry

    lax.fori_loop(0, blocks, project, 0)

    events = []
    for first in range(0, C, 2):
        for hop in range(1, half + 1):
            events += [(2 + first, hop), (3 + first, hop)]
    slots_total = pairs * blocks
    per_slot = -(-len(events) // slots_total)

    def attend(t, carry):
        lane = lax.broadcasted_iota(jnp.int32, (BLOCK, 128), 1)
        for i in range(blocks):
            rows = slice(i * BLOCK, (i + 1) * BLOCK)
            width = (i + 1) * BLOCK
            qb, dab = lanes[at_q + t, rows], lanes[at_da + t, rows]
            keys, values = lanes[at_k + t, :width], lanes[at_v + t, :width]
            zero = jnp.zeros_like(qb)
            mixed = []
            dquery = []
            dkey = jnp.zeros((width, 128), F32)
            dvalue = jnp.zeros((width, 128), F32)
            for h in range(2):
                mine = (lane < HEAD) if h == 0 else (lane >= HEAD)
                qm = jnp.where(mine, qb, zero)
                dm = jnp.where(mine, dab, zero)
                scores = dot_right(qm, keys)
                down = lax.broadcasted_iota(jnp.int32, (BLOCK, BLOCK), 0)
                over = lax.broadcasted_iota(jnp.int32, (BLOCK, BLOCK), 1)
                edge = jnp.where(down >= over, scores[:, width - BLOCK :], masked_score)
                scores = jnp.concatenate([scores[:, : width - BLOCK], edge], axis=1) if i else edge
                weights = jnp.exp(scores - jnp.max(scores, axis=1, keepdims=True))
                weights = weights * (1.0 / jnp.sum(weights, axis=1, keepdims=True))
                rounded = weights.astype(BF)
                dweights = dot_right(dm, values)
                delta = jnp.sum(weights * dweights, axis=1, keepdims=True)
                dscores = (weights * (dweights - delta)).astype(BF)
                mixed.append(dot(rounded, values))
                dquery.append(dot(dscores, keys))
                dvalue = dvalue + dot_left(rounded, dm)
                dkey = dkey + dot_left(dscores, qm)
            first = lane < HEAD
            position = lax.broadcasted_iota(jnp.int32, (BLOCK, 128), 0) + i * BLOCK
            whole = jnp.where(first, mixed[0], mixed[1])
            lanes[at_att + t, rows] = jnp.where(position < length[0], whole, 0.0).astype(BF)
            dq = jnp.where(first, dquery[0], dquery[1]) * HEAD**-0.5
            lanes[at_q + t, rows] = turned(dq, cos_ref[rows], sin_ref[rows], True).astype(BF)
            if i:
                dk_acc[: width - BLOCK] += dkey[: width - BLOCK]
                dv_acc[: width - BLOCK] += dvalue[: width - BLOCK]
            dk_acc[rows] = dkey[width - BLOCK :]
            dv_acc[rows] = dvalue[width - BLOCK :]
            for t0 in range(pairs):
                at = (t0 * blocks + i) * per_slot
                todo = events[at : at + per_slot]
                if todo:

                    @pl.when(t == t0)
                    def _(todo=todo):
                        for k, hop in todo:
                            gather_event(k, hop)

        lanes[at_k + t] = turned(dk_acc[...], cos_ref[...], sin_ref[...], True).astype(BF)
        lanes[at_v + t] = dv_acc[...].astype(BF)
        return carry

    lax.fori_loop(0, pairs, attend, 0)

    def side(at, rows, count=pairs):
        return jnp.concatenate([lanes[at + t, rows] for t in range(count)], axis=1)

    def merge(i, carry):
        rows = rows_of(i)
        ab = side(at_att, rows)
        out[rows, :W] = dot(ab, merge_weight(0))
        out[rows, W:] = dot(ab, merge_weight(1))
        total = dot_right(side(at_q, rows), weight(0))
        total = total + dot_right(side(at_k, rows), weight(1))
        dnorm[rows] = total + dot_right(side(at_v, rows), weight(2))
        return carry

    lax.fori_loop(0, blocks, merge, 0)
    gather_done(0)
    gather_done(1)
    every = slice(0, p.rows)
    chips = BLOCK // (4 * rq)

    def mix_grads(i, carry):
        left = normed[:, rows_of(i)]
        where = pl.ds(i * chips, chips)
        for t in range(3):
            res = dot_left(left, side(t * pairs, every)).astype(BF)
            wa[where, :, t * 2 * rq : (t + 1) * 2 * rq, :] = res.reshape(chips, 2, 2 * rq, W)
        return carry

    lax.fori_loop(0, D // BLOCK, mix_grads, 0)
    scatter_event(0, 0)
    merged = BLOCK // (2 * p.rr)
    for i in range(W // BLOCK):
        left = side(at_att + 2 * i, every, 2)
        for t in range(2):
            res = dot_left(left, g[:, t * W : (t + 1) * W]).reshape(merged, 2, p.rr, W)
            if p.mr != p.rr:
                res = jnp.concatenate([res, jnp.zeros((merged, 2, p.mr - p.rr, W), F32)], axis=2)
            wb[i * merged : (i + 1) * merged, :, t * p.mr : (t + 1) * p.mr, :] = res.astype(BF)
    scatter_event(1, 0)

    pending = []
    for hop in range(1, half + 2):
        pending += [(0, hop), (1, hop)]

    def hidden_bias(j):
        at = (2 * D + j * CW) // W
        return jnp.concatenate([small[at + t : at + t + 1] for t in range(CW // W)], axis=1)

    for j in range(C):
        here = wc.at[j]
        gather_ready(2 + j)
        width = -(-len(pending) // blocks)
        queue = [pending[t * width : (t + 1) * width] for t in range(blocks)]

        def feed(i, carry, here=here, j=j, queue=queue):
            rows = rows_of(i)
            we = flat2(here[:, :, : 2 * rq, :])
            gb = g[rows]
            pre = dot(normed[rows], we) + hidden_bias(j)
            hid, slope = gelu_parts(pre)
            hid = hid.astype(BF)
            for t in range(groups):
                lanes[at_hid + t, rows] = hid[:, t * 128 : (t + 1) * 128]
            dhid = jnp.zeros((BLOCK, CW), F32)
            for t in range(p.wb):
                wst = flat2(here[:, :, 2 * rq + t * q : 2 * rq + (t + 1) * q, :])
                cols = slice(t * CW, (t + 1) * CW)
                dhid = dhid + dot_right(gb[:, cols], wst)
                out[rows, cols] += dot(hid, wst)
            dp = (dhid * slope).astype(BF)
            for t in range(groups):
                lanes[at_dpre + t, rows] = dp[:, t * 128 : (t + 1) * 128]
            dnorm[rows] += dot_right(dp, we)
            for i0 in range(blocks):
                if queue[i0]:

                    @pl.when(i == i0)
                    def _(todo=queue[i0]):
                        for k, hop in todo:
                            scatter_event(k, hop)

            return carry + jnp.sum(dp.astype(F32), axis=0, keepdims=True)

        bias_grad = lax.fori_loop(0, blocks, feed, jnp.zeros((1, CW), F32))
        at = (2 * D + j * CW) // W
        for t in range(CW // W):
            small[16 + at + t : 17 + at + t] = bias_grad[:, t * W : (t + 1) * W]
        gather_done(2 + j)

        def expand_grads(i, carry, here=here):
            res = dot_left(normed[:, rows_of(i)], side(at_dpre, every, groups)).astype(BF)
            here[pl.ds(i * chips, chips), :, : 2 * rq, :] = res.reshape(chips, 2, 2 * rq, CW)
            return carry

        lax.fori_loop(0, D // BLOCK, expand_grads, 0)
        per = BLOCK // (2 * q)

        def shrink_grads(i, carry, here=here):
            left = side(at_hid + 2 * i, every, 2)
            for t in range(p.wb):
                res = dot_left(left, g[:, t * CW : (t + 1) * CW]).astype(BF)
                cut = slice(2 * rq + t * q, 2 * rq + (t + 1) * q)
                here[pl.ds(i * per, per), :, cut, :] = res.reshape(per, 2, q, CW)
            return carry

        lax.fori_loop(0, CW // BLOCK, shrink_grads, 0)
        scatter_event(2 + j, 0)
        pending = [(2 + j, hop) for hop in range(1, half + 2)]

    trade[0] = out[their_rows].astype(BF)
    give_out = remote(trade.at[0], trade.at[1], x_send.at[2], x_recv.at[2], partner)
    give_out.start()
    trade[2] = dnorm[their_rows].astype(BF)
    give_dn = remote(trade.at[2], trade.at[3], x_send.at[3], x_recv.at[3], partner)
    give_dn.start()

    def vector_grads(i, carry):
        rows = rows_of(i)
        z, _ = unit(rows)
        dn = dnorm[rows]
        gain = carry[0] + jnp.sum(dn * z, axis=0, keepdims=True)
        shift = carry[1] + jnp.sum(dn, axis=0, keepdims=True)
        return gain, shift, carry[2] + jnp.sum(g[rows].astype(F32), axis=0, keepdims=True)

    zero_row = jnp.zeros((1, D), F32)
    sums = lax.fori_loop(0, blocks, vector_grads, (zero_row, zero_row, zero_row))
    last = (2 * D + p.FF // 2) // W
    for at, row in ((0, sums[0]), (2, sums[1]), (last, sums[2])):
        small[16 + at : 17 + at] = row[:, :W]
        small[17 + at : 18 + at] = row[:, W:]
    small[16 + last + 2 : 32] = jnp.zeros((14 - last, W), F32)
    ws[...] = jnp.broadcast_to(small[16:32].astype(BF)[None, None], (m, 2, 16, W))
    scatter_event(C + 2, 0)
    for hop in range(1, half + 2):
        scatter_event(C + 1, hop)
        scatter_event(C + 2, hop)

    small_rows = p.own_rows // blocks
    give_out.wait_recv()
    give_dn.wait_recv()

    def finish_rows(i, carry):
        local = pl.ds(pl.multiple_of(i * small_rows, small_rows), small_rows)
        rows = pl.ds(pl.multiple_of(b * p.own_rows + i * small_rows, small_rows), small_rows)
        z, inverse = unit(rows)
        tail = wide(last)
        total = out[rows] + trade[1, local].astype(F32) + tail
        res_out[local] = (x[rows].astype(F32) + total).astype(BF)
        du = (dnorm[rows] + trade[3, local].astype(F32)) * wide(0)
        back = du - jnp.mean(du, axis=1, keepdims=True) - z * jnp.mean(du * z, axis=1, keepdims=True)
        sg_out[local] = g[rows].astype(F32) + inverse * back
        return carry

    lax.fori_loop(0, blocks, finish_rows, 0)
    for copy in (give_x, give_g, give_out, give_dn):
        copy.wait_send()


def core(p, b, group, chunks, stream, cotangent, lengths):
    n, C, D, W, CW, rq = p.n, p.C, p.D, p.W, p.CW, p.rq
    m = n // 2
    half = m // 2
    hops = 2 * half - 1
    rows = p.rows
    a_rows = 6 * rq + 16
    b_rows = 2 * p.mr
    a_own = jnp.concatenate([group[: 6 * rq], group[p.o_small :]], axis=0)
    b_own = group[p.o_merge : p.o_small]
    cosine, sine = rope_tables(rows)
    vmem = pl.BlockSpec(memory_space=pltpu.VMEM)
    hbm = pl.BlockSpec(memory_space=pl.ANY)
    dma = pltpu.SemaphoreType.DMA
    V = pltpu.VMEM
    scratch = [
        V((m, 2, a_rows, W), BF),
        V((m, 2, b_rows, W), BF),
        V((C, m, 2, p.c_rows, CW), BF),
        V((m, 2, 16, W), BF),
        V((rows, D), BF),
        V((rows, D), BF),
        V((rows, D), BF),
        V((5 * W // 128, rows, 128), BF),
        V((rows, 128), F32),
        V((rows, 128), F32),
        V((rows, D), F32),
        V((rows, D), F32),
        V((32, W), F32),
        V((4, p.own_rows, D), BF),
        V((m, 6 * rq, W), BF),
        V((m, b_rows, W), BF),
        V((C, m, p.c_rows, CW), BF),
        V((m, 16, W), BF),
        V((hops, 6 * rq, W), BF),
        V((hops, b_rows, W), BF),
        V((C, hops, p.c_rows, CW), BF),
        V((hops, 16, W), BF),
        dma((C + 2, 2, half + 1)),
        dma((C + 2, 2, half + 1)),
        dma((C + 2,)),
        dma((C + 2,)),
        dma((C + 3, 2, half + 1)),
        dma((C + 3, 2, half + 1)),
        dma((C + 3,)),
        dma((C + 3,)),
        dma((4,)),
        dma((4,)),
        dma((2,)),
    ]
    shapes = (
        jax.ShapeDtypeStruct((p.own_rows, D), BF),
        jax.ShapeDtypeStruct((p.own_rows, D), F32),
        jax.ShapeDtypeStruct((6 * rq, W), F32),
        jax.ShapeDtypeStruct((b_rows, W), F32),
        jax.ShapeDtypeStruct((C, p.c_rows, CW), F32),
        jax.ShapeDtypeStruct((16, W), F32),
    )
    flops = 2 * rows * D * (6 * p.FF // 2 + 9 * W + 3 * W) + 12 * rows * rows * W
    residual, stream_grad, ga, gb, gc, gs = pl.pallas_call(
        functools.partial(block_kernel, p),
        out_shape=shapes,
        in_specs=[vmem, vmem, vmem, hbm, hbm, pl.BlockSpec(memory_space=pltpu.SMEM), vmem, vmem],
        out_specs=tuple(vmem for _ in shapes),
        scratch_shapes=scratch,
        compiler_params=pltpu.CompilerParams(
            collective_id=0, has_side_effects=True, vmem_limit_bytes=63 * 1024 * 1024
        ),
        cost_estimate=pl.CostEstimate(flops=flops, bytes_accessed=8 << 20, transcendentals=0),
    )(a_own, b_own, chunks, stream, cotangent, lengths, cosine, sine)
    grad_group = jnp.concatenate([ga, gb], axis=0)
    return residual, stream_grad, grad_group, gc, gs


def finish(p, b, linear, group, chunks, small):
    mix = group[: 6 * p.rq].reshape(3, 2, p.rq, p.W)
    exp = chunks[:, : 2 * p.rq].reshape(p.C, 2, p.rq, p.CW)
    keep = (pick(mix, b, 1), pick(exp, b, 1), small)
    give = (pick(mix, 1 - b, 1), pick(exp, 1 - b, 1), small)
    got = swap_branch(jax.tree.map(lambda a: a.astype(BF), give[:2]) + (give[2],))

    def weave(axis, mine, theirs):
        theirs = theirs.astype(F32)
        return jnp.stack([jnp.where(b == 0, mine, theirs), jnp.where(b == 0, theirs, mine)], axis)

    grad_mixing = weave(2, keep[0].transpose(1, 0, 2), got[0].transpose(1, 0, 2))
    grad_mixing = grad_mixing.reshape(p.rq, -1)

    def columns(a):
        return a.reshape(p.C, p.rq, p.n, p.q).transpose(1, 2, 0, 3)

    grad_expand = weave(2, columns(keep[1]), columns(got[1])).reshape(p.rq, p.FF)
    mer = group[p.o_merge : p.o_merge + 2 * p.mr].reshape(2, p.mr, p.W)[:, : p.rr]
    mer = mer.transpose(1, 0, 2).reshape(p.rr, p.D)
    grad_merging = lax.ppermute(
        mer.astype(BF), ("dp", "branch"), [(t, s) for s, t in merge_perm(p.n)]
    ).astype(F32)
    shr = chunks[:, 2 * p.rq : 2 * p.rq + p.wb * p.q].reshape(p.C, p.wb, p.q, p.CW)
    grad_shrink = shr.transpose(0, 2, 1, 3).reshape(p.hb, p.D)
    mine, theirs = keep[2].reshape(-1), got[2].reshape(-1)
    total = mine + theirs
    grad_vectors = lax.dynamic_slice(
        total[: 2 * p.D].reshape(2, p.D), (0, linear * p.vc), (2, p.vc)
    )
    lo, hi = 2 * p.D, 2 * p.D + p.FF // 2

    def hidden(a):
        return a[lo:hi].reshape(p.C, p.n, p.q).transpose(1, 0, 2)

    hid = weave(1, hidden(mine), hidden(theirs)).reshape(p.FF)
    tail = mine[hi : hi + p.D]
    offs = jnp.concatenate([hid, tail])
    grad_offsets = lax.dynamic_slice(offs, (linear * p.ow,), (p.ow,))
    return grad_mixing, grad_merging, grad_expand, grad_shrink, grad_vectors, grad_offsets


def local(n, stream, cotangent, lengths, steps_taken, learning_rates, *params):
    masters, momenta, variances = params[:6], params[6:12], params[12:]
    p = Plan(n, stream, *masters)
    b = lax.axis_index("branch")
    linear = lax.axis_index("dp") * 2 + b
    group, chunks = prepare(p, b, linear, *masters)
    residual, stream_grad, group, chunks, small = core(
        p, b, group, chunks, stream, cotangent, lengths
    )
    grads = finish(p, b, linear, group, chunks, small)
    count = steps_taken[0].astype(F32)
    outs = [residual, stream_grad]
    for k in range(6):
        decay = decay_rate if k < 4 else 0.0
        outs.extend(
            adam_update(
                masters[k], grads[k], momenta[k], variances[k], learning_rates[k], count, decay
            )
        )
    return tuple(outs)


def solution(mesh):
    rows = P(("dp", "branch"), None)
    cols = P(None, ("dp", "branch"))
    flat = P(("dp", "branch"))
    six = (rows, rows, rows, rows, cols, flat)
    return jax.shard_map(
        functools.partial(local, mesh.shape["dp"]),
        mesh=mesh,
        in_specs=(rows, rows, P("dp"), P(), P()) + six * 3,
        out_specs=(rows, rows) + sum(((s,) * 4 for s in six), ()),
        check_vma=False,
    )
```

```python
import functools

import jax
import jax.numpy as jnp
from jax import lax
from jax.experimental import pallas as pl
from jax.experimental.pallas import tpu as pltpu
from jax.sharding import PartitionSpec as P

HEAD = 64
ROT = 32
beta_one = 0.9
beta_two = 0.95
adam_eps = 1e-08
decay_rate = 0.1
norm_eps = 1e-05
rope_base = 10000.0
masked_score = -1e30
BF = jnp.bfloat16
F32 = jnp.float32


def dot(left, right):
    return jnp.dot(left, right, preferred_element_type=F32)


def dot_left(left, right):
    return lax.dot_general(left, right, (((0,), (0,)), ((), ())), preferred_element_type=F32)


def dot_right(left, right):
    return lax.dot_general(left, right, (((1,), (1,)), ((), ())), preferred_element_type=F32)


def rope_tables(length):
    places = jnp.arange(length).astype(F32)[:, None]
    column = jnp.arange(2 * HEAD) % HEAD
    paired = (column // 2).astype(F32)
    frequency = jnp.exp(paired * (-2.0 / ROT) * jnp.log(rope_base))
    angles = places * frequency[None, :]
    inside = (column < ROT)[None, :]
    cosine = jnp.where(inside, jnp.cos(angles), 1.0)
    signed = jnp.where(column % 2 == 0, -1.0, 1.0)[None, :]
    sine = jnp.where(inside, jnp.sin(angles) * signed, 0.0)
    return cosine, sine


def adam_update(master, gradient, momentum, variance, rate, count, decay):
    drift = beta_one * momentum + (1.0 - beta_one) * gradient
    power = beta_two * variance + (1.0 - beta_two) * gradient * gradient
    first_fix = 1.0 - jnp.power(beta_one, count)
    second_fix = 1.0 - jnp.power(beta_two, count)
    moved = drift / first_fix / (jnp.sqrt(power / second_fix) + adam_eps)
    updated = master - rate * (moved + decay * master)
    return (updated, updated.astype(BF), drift, power)


class Plan:
    def __init__(self, n, stream, mixing, merging, expand, shrink, vectors, offsets):
        self.n = n
        self.own_rows, self.D = stream.shape
        self.rows = 2 * self.own_rows
        self.W = self.D // 2
        self.FF = expand.shape[1]
        self.rq = mixing.shape[0]
        self.rr = merging.shape[0]
        self.mr = max(16, self.rr)
        self.hb = shrink.shape[0]
        self.C = 4 if self.hb >= 64 else 2
        self.q = self.hb // self.C
        self.CW = self.FF // 2 // self.C
        self.wb = self.D // self.CW
        self.vc = vectors.shape[1]
        self.ow = offsets.shape[0]
        self.o_merge = 6 * self.rq
        self.o_small = self.o_merge + 2 * self.mr
        self.g_rows = self.o_small + 16
        self.c_rows = 2 * self.rq + self.wb * self.q


def pick(array, index, axis):
    return lax.dynamic_index_in_dim(array, index, axis, keepdims=False)


def small_pack(p, gain_bias, offs, plane):
    hid = pick(offs[: p.FF].reshape(p.n, 2, p.C, p.q), plane, 1)
    hid = hid.transpose(1, 0, 2).reshape(-1)
    flat = jnp.concatenate([gain_bias.reshape(-1), hid, offs[p.FF :]])
    flat = jnp.pad(flat, (0, 16 * p.W - flat.shape[0]))
    return flat.reshape(16, p.W)


def pack_for(p, plane, mixing, expand, vectors, offsets, linear):
    mix = pick(mixing.reshape(p.rq, 3, 2, p.W), plane, 2).transpose(1, 0, 2)
    exp = pick(expand.reshape(p.rq, p.n, 2, p.C, p.q), plane, 2)
    exp = exp.transpose(2, 0, 1, 3).reshape(p.C, p.rq, p.CW)
    gain_bias = lax.dynamic_update_slice(jnp.zeros((2, p.D), BF), vectors, (0, linear * p.vc))
    offs = lax.dynamic_update_slice(jnp.zeros((p.FF + p.D,), BF), offsets, (linear * p.ow,))
    return mix, exp, small_pack(p, gain_bias, offs, plane)


def swap_branch(tree):
    return jax.tree.map(lambda a: lax.ppermute(a, "branch", [(0, 1), (1, 0)]), tree)


def both(b, mine, theirs, axis):
    first = jnp.where(b == 0, mine, theirs)
    second = jnp.where(b == 0, theirs, mine)
    return jnp.concatenate([first, second], axis=axis)


def merge_perm(n):
    return [(linear, (linear % n) * 2 + linear // n) for linear in range(2 * n)]


def prepare(p, b, linear, mixing, merging, expand, shrink, vectors, offsets):
    mixing, merging, expand, shrink, vectors, offsets = (
        a.astype(BF) for a in (mixing, merging, expand, shrink, vectors, offsets)
    )
    keep = pack_for(p, b, mixing, expand, vectors, offsets, linear)
    give = pack_for(p, 1 - b, mixing, expand, vectors, offsets, linear)
    got = swap_branch(give)
    mix = both(b, keep[0], got[0], 1).reshape(6 * p.rq, p.W)
    small = keep[2] + got[2]
    mer = lax.ppermute(merging, ("dp", "branch"), merge_perm(p.n))
    mer = mer.reshape(p.rr, 2, p.W).transpose(1, 0, 2)
    mer = jnp.pad(mer, ((0, 0), (0, p.mr - p.rr), (0, 0))).reshape(2 * p.mr, p.W)
    group = jnp.concatenate([mix, mer, small], axis=0)
    exp = both(b, keep[1], got[1], 1)
    shr = shrink.reshape(p.C, p.q, p.wb, p.CW).transpose(0, 2, 1, 3).reshape(p.C, -1, p.CW)
    chunks = jnp.concatenate([exp, shr], axis=1)
    return group, chunks


MESH = pl.DeviceIdType.MESH
BLOCK = 256
ATTEND_SHARE = 12
AB_START, AB_STEP = 1.0, 6.0
C_START, C_STEP = 0.5, 5.0


def turned(a, cosine, sine, back):
    lanes = a.shape[1]
    even = lax.broadcasted_iota(jnp.int32, a.shape, 1) % 2 == 0
    t = a * sine if back else a
    swapped = jnp.where(even, pltpu.roll(t, lanes - 1, 1), pltpu.roll(t, 1, 1))
    return a * cosine + (swapped if back else swapped * sine)


def tile_lanes(a, times):
    return jnp.concatenate([a] * times, axis=1) if times > 1 else a


def flat2(a):
    return a.reshape(-1, a.shape[-1])


def gelu_parts(pre):
    root = 0.7978845608028654
    square = pre * pre
    t = jnp.tanh(root * pre * (1.0 + 0.044715 * square))
    hidden = 0.5 * pre * (1.0 + t)
    slope = 0.5 * (1.0 + t) + 0.5 * pre * (1.0 - t * t) * root * (1.0 + 0.134145 * square)
    return hidden, slope


def block_kernel(
    p,
    a_in,
    b_in,
    c_in,
    stream,
    cotangent,
    length,
    cos_ref,
    sin_ref,
    res_out,
    sg_out,
    ga_out,
    gb_out,
    gc_out,
    gs_out,
    wa,
    wb,
    wc,
    ws,
    x,
    g,
    normed,
    lanes,
    out,
    dnorm,
    small,
    trade,
    sib_a,
    sib_b,
    sib_c,
    sib_s,
    slot_a,
    slot_b,
    slot_c,
    slot_s,
    ag_send,
    ag_recv,
    as_send,
    as_recv,
    rs_send,
    rs_recv,
    ss_send,
    ss_recv,
    x_send,
    x_recv,
    own_sem,
):
    n, C, D, W, CW, rq, q = p.n, p.C, p.D, p.W, p.CW, p.rq, p.q
    m = n // 2
    half = m // 2
    blocks = p.rows // BLOCK
    pairs = W // 128
    groups = CW // 128
    at_q, at_k, at_v, at_att, at_da = (t * pairs for t in range(5))
    at_hid, at_slope = 0, C * groups
    d = lax.axis_index("dp")
    b = lax.axis_index("branch")
    core = lax.rem(d, 2)
    chip = d // 2
    ring = jnp.where(lax.rem(chip, 2) == 0, chip // 2, m - 1 - chip // 2)
    step = 1 - 2 * core

    def around(k):
        pos = lax.rem(ring + step * k + m, m)
        return jnp.where(pos < half, 2 * pos, 2 * (m - 1 - pos) + 1)

    ahead = (2 * around(1) + core, b)
    behind = (2 * around(-1) + core, b)
    sibling = (d + step, b)
    partner = (d, 1 - b)
    ways = (ahead, behind)

    barrier = pltpu.get_barrier_semaphore()
    for other in (ahead, behind, sibling, partner):
        pl.semaphore_signal(barrier, inc=1, device_id=other, device_id_type=MESH)
    pl.semaphore_wait(barrier, 4)

    def remote(src, dst, send, recv, to):
        return pltpu.make_async_remote_copy(
            src_ref=src, dst_ref=dst, send_sem=send, recv_sem=recv, device_id=to, device_id_type=MESH
        )

    own_rows = pl.ds(pl.multiple_of(b * p.own_rows, p.own_rows), p.own_rows)
    their_rows = pl.ds(pl.multiple_of((1 - b) * p.own_rows, p.own_rows), p.own_rows)

    def gather_ref(k):
        return wa if k == 0 else wb if k == 1 else wc.at[k - 2]

    def last_hop(way):
        return half - way

    def gather_copy(k, way, hop):
        shard = gather_ref(k).at[around((1 - hop) * (1 - 2 * way)), core]
        return remote(shard, shard, ag_send.at[k, way, hop], ag_recv.at[k, way, hop], ways[way])

    def gather_arrival(k, way, hop):
        shard = gather_ref(k).at[around(-hop * (1 - 2 * way)), core]
        return remote(shard, shard, ag_send.at[k, way, hop], ag_recv.at[k, way, hop], ways[way])

    def gather_sibling(k, whose):
        part = gather_ref(k).at[:, whose]
        return remote(part, part, as_send.at[k], as_recv.at[k], sibling)

    def gather_start(k):
        for way in range(2):
            gather_copy(k, way, 1).start()

    def gather_event(k, hop):
        for way in range(2):
            if hop <= last_hop(way):
                gather_arrival(k, way, hop).wait_recv()
                if hop < last_hop(way):
                    gather_copy(k, way, hop + 1).start()
        if hop == half:
            gather_sibling(k, core).start()

    def gather_ready(k):
        gather_sibling(k, 1 - core).wait_recv()

    def gather_done(k):
        for way in range(2):
            for hop in range(1, last_hop(way) + 1):
                gather_copy(k, way, hop).wait_send()
        gather_sibling(k, core).wait_send()

    def scatter_refs(k):
        if k == 0:
            return wa, sib_a, slot_a, ga_out, 6 * rq
        if k == 1:
            return wb, sib_b, slot_b, gb_out, 2 * p.mr
        if k < C + 2:
            return wc.at[k - 2], sib_c.at[k - 2], slot_c.at[k - 2], gc_out.at[k - 2], p.c_rows
        return ws, sib_s, slot_s, gs_out, 16

    def scatter_sibling(k):
        whole, sib, _, _, rows = scatter_refs(k)
        src = whole.at[:, 1 - core, pl.ds(0, rows)]
        return remote(src, sib, ss_send.at[k], ss_recv.at[k], sibling)

    def slot_of(way, hop):
        return (hop - 1) if way == 0 else half + hop - 1

    def scatter_copy(k, way, hop):
        whole, _, slots, _, rows = scatter_refs(k)
        target = around((last_hop(way) + 1 - hop) * (1 - 2 * way))
        src = whole.at[target, core, pl.ds(0, rows)]
        return remote(
            src, slots.at[slot_of(way, hop)], rs_send.at[k, way, hop], rs_recv.at[k, way, hop], ways[way]
        )

    def scatter_event(k, hop):
        whole, sib, slots, result, rows = scatter_refs(k)
        if hop == 0:
            scatter_sibling(k).start()
            return
        if hop == 1:
            scatter_sibling(k).wait_recv()
        for way in range(2):
            if hop <= last_hop(way):
                target = around((last_hop(way) + 1 - hop) * (1 - 2 * way))
                here = whole.at[target, core, pl.ds(0, rows)]
                total = here[...].astype(F32) + sib[target].astype(F32)
                if hop > 1:
                    scatter_copy(k, way, hop - 1).wait_recv()
                    total = total + slots[slot_of(way, hop - 1)].astype(F32)
                here[...] = total.astype(BF)
                scatter_copy(k, way, hop).start()
        if hop == half + 1:
            total = whole[chip, core, pl.ds(0, rows)].astype(F32) + sib[chip].astype(F32)
            for way in range(2):
                scatter_copy(k, way, last_hop(way)).wait_recv()
                total = total + slots[slot_of(way, last_hop(way))].astype(F32)
            result[...] = total
            for way in range(2):
                for sent in range(1, last_hop(way) + 1):
                    scatter_copy(k, way, sent).wait_send()
            scatter_sibling(k).wait_send()

    piece = p.own_rows // 2

    def quarter(whose, t):
        return pl.ds(pl.multiple_of(whose * p.own_rows + t * piece, piece), piece)

    def row_copy(kind, t, receiving):
        src, dst = ((stream, x), (cotangent, g))[kind]
        sem = 2 * kind + t
        there = dst.at[quarter(1 - b if receiving else b, t)]
        return remote(src.at[pl.ds(t * piece, piece)], there, x_send.at[sem], x_recv.at[sem], partner)

    keep_x = pltpu.make_async_copy(stream, x.at[own_rows], own_sem.at[0])
    keep_g = pltpu.make_async_copy(cotangent, g.at[own_rows], own_sem.at[1])
    wa[chip, core] = a_in[...]
    gather_start(0)
    row_copy(0, 0, False).start()
    wb[chip, core] = b_in[...]
    gather_start(1)

    @pl.when(b == 0)
    def _():
        row_copy(0, 1, False).start()
        row_copy(1, 0, False).start()

    @pl.when(b == 1)
    def _():
        row_copy(1, 0, False).start()
        row_copy(0, 1, False).start()

    row_copy(1, 1, False).start()
    keep_x.start()
    keep_g.start()
    for j in range(C):
        wc[j, chip, core] = c_in[j]
    out[...] = jnp.zeros((p.rows, D), F32)
    for hop in range(1, half + 1):
        gather_event(0, hop)
        gather_event(1, hop)
        if hop == half - 1:
            gather_start(2)
    for j in range(1, C):
        gather_start(2 + j)

    def weight(t):
        return flat2(wa[:, :, t * 2 * rq : (t + 1) * 2 * rq, :])

    def merge_weight(t):
        whole = wb[:, :, t * p.mr : (t + 1) * p.mr, :]
        if p.mr == p.rr:
            return flat2(whole)
        whole = whole.astype(F32).reshape(n, p.mr, W)[:, : p.rr]
        return whole.reshape(W, W).astype(BF)

    def wide(row):
        return jnp.concatenate([small[row : row + 1], small[row + 1 : row + 2]], axis=1)

    def unit(rows):
        v = x[rows].astype(F32)
        centred = v - jnp.mean(v, axis=1, keepdims=True)
        inverse = lax.rsqrt(jnp.mean(centred * centred, axis=1, keepdims=True) + norm_eps)
        return centred * inverse, inverse

    def rows_of(i):
        return pl.ds(pl.multiple_of(i * BLOCK, BLOCK), BLOCK)

    def project(i):
        rows = rows_of(i)
        z, _ = unit(rows)
        nb = (z * wide(0) + wide(2)).astype(BF)
        normed[rows] = nb
        cosine = tile_lanes(cos_ref[rows], pairs)
        sine = tile_lanes(sin_ref[rows], pairs)
        query = (turned(dot(nb, weight(0)), cosine, sine, False) * HEAD**-0.5).astype(BF)
        key = turned(dot(nb, weight(1)), cosine, sine, False).astype(BF)
        value = dot(nb, weight(2)).astype(BF)
        for t in range(pairs):
            cut = slice(t * 128, (t + 1) * 128)
            lanes[at_q + t, rows] = query[:, cut]
            lanes[at_k + t, rows] = key[:, cut]
            lanes[at_v + t, rows] = value[:, cut]

    def gradient(i):
        rows = rows_of(i)
        position = lax.broadcasted_iota(jnp.int32, (BLOCK, D), 0) + i * BLOCK
        gb = jnp.where(position < length[0], g[rows].astype(F32), 0.0).astype(BF)
        g[rows] = gb
        da = (dot_right(gb[:, :W], merge_weight(0)) + dot_right(gb[:, W:], merge_weight(1))).astype(BF)
        for t in range(pairs):
            lanes[at_da + t, rows] = da[:, t * 128 : (t + 1) * 128]

    def each(body, start, count):
        def run(i, carry):
            body(start + i)
            return carry

        lax.fori_loop(0, count, run, 0)

    keep_x.wait()
    keep_g.wait()
    gather_ready(0)
    small[:16] = jnp.sum(wa[:, :, 6 * rq :, :].reshape(n, 16, W).astype(F32), axis=0)
    part = blocks // 2
    each(project, b * part, part)
    gather_ready(1)
    each(gradient, b * part, part)

    @pl.when(b == 1)
    def _():
        row_copy(0, 0, True).wait_recv()
        row_copy(0, 1, True).wait_recv()
        each(project, 0, part)

    def spread(items, count, first=0):
        return [items[len(items) * t // count : len(items) * (t + 1) // count] for t in range(count)]

    events = []
    for lead in range(0, C, 2):
        for hop in range(1, half + 1):
            events += [(2 + lead, hop), (3 + lead, hop)]
    attend_slots = spread(events[: len(events) * ATTEND_SHARE // 16], blocks * pairs)
    merge_events = events[len(events) * ATTEND_SHARE // 16 :]

    def attend(i, t):
        lane = lax.broadcasted_iota(jnp.int32, (BLOCK, 128), 1)
        rows = slice(i * BLOCK, (i + 1) * BLOCK)
        width = (i + 1) * BLOCK
        qb, dab = lanes[at_q + t, rows], lanes[at_da + t, rows]
        keys, values = lanes[at_k + t, :width], lanes[at_v + t, :width]
        zero = jnp.zeros_like(qb)
        mixed = []
        dquery = []
        dkey = jnp.zeros((width, 128), F32)
        dvalue = jnp.zeros((width, 128), F32)
        for h in range(2):
            mine = (lane < HEAD) if h == 0 else (lane >= HEAD)
            qm = jnp.where(mine, qb, zero)
            dm = jnp.where(mine, dab, zero)
            scores = dot_right(qm, keys)
            down = lax.broadcasted_iota(jnp.int32, (BLOCK, BLOCK), 0)
            over = lax.broadcasted_iota(jnp.int32, (BLOCK, BLOCK), 1)
            edge = jnp.where(down >= over, scores[:, width - BLOCK :], masked_score)
            scores = jnp.concatenate([scores[:, : width - BLOCK], edge], axis=1) if i else edge
            weights = jnp.exp(scores - jnp.max(scores, axis=1, keepdims=True))
            weights = weights * (1.0 / jnp.sum(weights, axis=1, keepdims=True))
            rounded = weights.astype(BF)
            dweights = dot_right(dm, values)
            delta = jnp.sum(weights * dweights, axis=1, keepdims=True)
            dscores = (weights * (dweights - delta)).astype(BF)
            mixed.append(dot(rounded, values))
            dquery.append(dot(dscores, keys))
            dvalue = dvalue + dot_left(rounded, dm)
            dkey = dkey + dot_left(dscores, qm)
        first = lane < HEAD
        position = lax.broadcasted_iota(jnp.int32, (BLOCK, 128), 0) + i * BLOCK
        whole = jnp.where(first, mixed[0], mixed[1])
        lanes[at_att + t, rows] = jnp.where(position < length[0], whole, 0.0).astype(BF)
        dq = jnp.where(first, dquery[0], dquery[1]) * HEAD**-0.5
        lanes[at_q + t, rows] = turned(dq, cos_ref[rows], sin_ref[rows], True).astype(BF)
        out[:width, head_lanes(t, 0)] += dkey
        out[:width, head_lanes(t, 1)] += dvalue

    def head_lanes(t, which):
        return pl.ds(pl.multiple_of(which * W + t * 128, 128), 128)

    def attention(it, carry):
        stage, t = it // pairs, lax.rem(it, pairs)
        now = lax.rem(stage + b * part, blocks)

        @pl.when((t == 0) & (b == 0) & (stage >= part))
        def _():
            for u in range(2):

                @pl.when(stage == part + u * (part // 2))
                def _(u=u):
                    row_copy(0, u, True).wait_recv()
                    row_copy(1, u, True).wait_recv()
                    each(project, part + u * (part // 2), part // 2)
                    each(gradient, part + u * (part // 2), part // 2)

        @pl.when((t == 0) & (b == 1) & (stage == part))
        def _():
            row_copy(1, 0, True).wait_recv()
            row_copy(1, 1, True).wait_recv()
            each(gradient, 0, part)

        for i in range(blocks):

            @pl.when(now == i)
            def _(i=i):
                attend(i, t)

        @pl.when(stage == blocks - 1)
        def _():
            dk = out[:, head_lanes(t, 0)]
            lanes[at_k + t] = turned(dk, cos_ref[...], sin_ref[...], True).astype(BF)
            lanes[at_v + t] = out[:, head_lanes(t, 1)].astype(BF)

        for slot, todo in enumerate(attend_slots):
            if todo:

                @pl.when(it == slot)
                def _(todo=todo):
                    for k, hop in todo:
                        gather_event(k, hop)

        return carry

    lax.fori_loop(0, blocks * pairs, attention, 0)

    def side(at, rows, count=pairs):
        return jnp.concatenate([lanes[at + t, rows] for t in range(count)], axis=1)

    def merge(i, carry):
        rows = rows_of(i)
        ab = side(at_att, rows)
        out[rows, :W] = dot(ab, merge_weight(0))
        out[rows, W:] = dot(ab, merge_weight(1))
        total = dot_right(side(at_q, rows), weight(0))
        total = total + dot_right(side(at_k, rows), weight(1))
        dnorm[rows] = total + dot_right(side(at_v, rows), weight(2))
        return carry

    lax.fori_loop(0, blocks, merge, 0)
    for k, hop in merge_events[: len(merge_events) // 2]:
        gather_event(k, hop)
    gather_done(0)
    gather_done(1)
    every = slice(0, p.rows)
    chips = BLOCK // (4 * rq)

    def mix_grads(i, carry):
        left = normed[:, rows_of(i)]
        where = pl.ds(i * chips, chips)
        for t in range(3):
            res = dot_left(left, side(t * pairs, every)).astype(BF)
            wa[where, :, t * 2 * rq : (t + 1) * 2 * rq, :] = res.reshape(chips, 2, 2 * rq, W)
        return carry

    lax.fori_loop(0, D // BLOCK, mix_grads, 0)
    scatter_event(0, 0)
    for k, hop in merge_events[len(merge_events) // 2 :]:
        gather_event(k, hop)
    merged = BLOCK // (2 * p.rr)
    for i in range(W // BLOCK):
        left = side(at_att + 2 * i, every, 2)
        for t in range(2):
            res = dot_left(left, g[:, t * W : (t + 1) * W]).reshape(merged, 2, p.rr, W)
            if p.mr != p.rr:
                res = jnp.concatenate([res, jnp.zeros((merged, 2, p.mr - p.rr, W), F32)], axis=2)
            wb[i * merged : (i + 1) * merged, :, t * p.mr : (t + 1) * p.mr, :] = res.astype(BF)
    scatter_event(1, 0)

    fore, aft = C * blocks, C * (blocks + 2)
    timed = []
    pace = 4.0 / half
    for hop in range(1, half + 2):
        timed += [(AB_START + (hop - 1) * AB_STEP * pace, k, hop) for k in range(2)]
        for j in range(C):
            begin = fore + (j + 1) * (blocks + 2) + C_START
            timed.append((begin + (hop - 1) * C_STEP * pace, 2 + j, hop))
    timed.sort()
    slots = [[e[1:] for e in timed if t <= e[0] < t + 1] for t in range(fore + aft)]
    leftover = [e[1:] for e in timed if e[0] >= fore + aft]

    def run_slot(slot):
        for k, hop in slots[slot]:
            scatter_event(k, hop)

    def run_when(i, start):
        for i0 in range(blocks):
            if slots[start + i0]:

                @pl.when(i == i0)
                def _(i0=i0):
                    run_slot(start + i0)

    def hidden_bias(j):
        at = (2 * D + j * CW) // W
        return jnp.concatenate([small[at + t : at + t + 1] for t in range(CW // W)], axis=1)

    def shrink_weight(j, t):
        return flat2(wc[j, :, :, 2 * rq + t * q : 2 * rq + (t + 1) * q, :])

    last = (2 * D + p.FF // 2) // W
    for j in range(C):
        gather_ready(2 + j)

        def feed(i, carry, j=j):
            rows = rows_of(i)
            pre = dot(normed[rows], flat2(wc[j, :, :, : 2 * rq, :])) + hidden_bias(j)
            hid, slope = gelu_parts(pre)
            hid, slope = hid.astype(BF), slope.astype(BF)
            for t in range(groups):
                lanes[at_hid + j * groups + t, rows] = hid[:, t * 128 : (t + 1) * 128]
                lanes[at_slope + j * groups + t, rows] = slope[:, t * 128 : (t + 1) * 128]
            for t in range(p.wb):
                out[rows, t * CW : (t + 1) * CW] += dot(hid, shrink_weight(j, t))
            run_when(i, j * blocks)
            return carry

        lax.fori_loop(0, blocks, feed, 0)
    res_out[...] = out[their_rows].astype(BF)
    give_out = remote(res_out, trade.at[0], x_send.at[4], x_recv.at[4], partner)
    give_out.start()
    for j in range(C):
        start = fore + j * (blocks + 2)

        def back(i, carry, j=j, start=start):
            rows = rows_of(i)
            gb = g[rows]
            dhid = dot_right(gb[:, :CW], shrink_weight(j, 0))
            for t in range(1, p.wb):
                dhid = dhid + dot_right(gb[:, t * CW : (t + 1) * CW], shrink_weight(j, t))
            dp = (dhid * side(at_slope + j * groups, rows, groups).astype(F32)).astype(BF)
            for t in range(groups):
                lanes[at_slope + j * groups + t, rows] = dp[:, t * 128 : (t + 1) * 128]
            dnorm[rows] += dot_right(dp, flat2(wc[j, :, :, : 2 * rq, :]))
            run_when(i, start)
            return carry + jnp.sum(dp.astype(F32), axis=0, keepdims=True)

        bias_grad = lax.fori_loop(0, blocks, back, jnp.zeros((1, CW), F32))
        at = (2 * D + j * CW) // W
        for t in range(CW // W):
            small[16 + at + t : 17 + at + t] = bias_grad[:, t * W : (t + 1) * W]
        if j == C - 1:
            give_out.wait_send()
            res_out[...] = dnorm[their_rows].astype(BF)
            give_dn = remote(res_out, trade.at[1], x_send.at[5], x_recv.at[5], partner)
            give_dn.start()
        gather_done(2 + j)

        def expand_grads(i, carry, j=j):
            res = dot_left(normed[:, rows_of(i)], side(at_slope + j * groups, every, groups)).astype(BF)
            wc[j, pl.ds(i * chips, chips), :, : 2 * rq, :] = res.reshape(chips, 2, 2 * rq, CW)
            return carry

        lax.fori_loop(0, D // BLOCK, expand_grads, 0)
        run_slot(start + blocks)
        per = BLOCK // (2 * q)

        def shrink_grads(i, carry, j=j):
            left = side(at_hid + j * groups + 2 * i, every, 2)
            for t in range(p.wb):
                res = dot_left(left, g[:, t * CW : (t + 1) * CW]).astype(BF)
                cut = slice(2 * rq + t * q, 2 * rq + (t + 1) * q)
                wc[j, pl.ds(i * per, per), :, cut, :] = res.reshape(per, 2, q, CW)
            return carry

        lax.fori_loop(0, CW // BLOCK, shrink_grads, 0)
        scatter_event(2 + j, 0)
        run_slot(start + blocks + 1)

    def vector_grads(i, carry):
        rows = rows_of(i)
        z, _ = unit(rows)
        dn = dnorm[rows]
        gain = carry[0] + jnp.sum(dn * z, axis=0, keepdims=True)
        shift = carry[1] + jnp.sum(dn, axis=0, keepdims=True)
        return gain, shift, carry[2] + jnp.sum(g[rows].astype(F32), axis=0, keepdims=True)

    zero_row = jnp.zeros((1, D), F32)
    sums = lax.fori_loop(0, blocks, vector_grads, (zero_row, zero_row, zero_row))
    for at, row in ((0, sums[0]), (2, sums[1]), (last, sums[2])):
        small[16 + at : 17 + at] = row[:, :W]
        small[17 + at : 18 + at] = row[:, W:]
    small[16 + last + 2 : 32] = jnp.zeros((14 - last, W), F32)
    ws[...] = jnp.broadcast_to(small[16:32].astype(BF)[None, None], (m, 2, 16, W))
    scatter_event(C + 2, 0)
    for k, hop in leftover:
        scatter_event(k, hop)
        if k == C + 1:
            scatter_event(C + 2, hop)

    small_rows = p.own_rows // blocks
    give_out.wait_recv()
    give_dn.wait_recv()
    give_dn.wait_send()

    def finish_rows(i, carry):
        local = pl.ds(pl.multiple_of(i * small_rows, small_rows), small_rows)
        rows = pl.ds(pl.multiple_of(b * p.own_rows + i * small_rows, small_rows), small_rows)
        z, inverse = unit(rows)
        tail = wide(last)
        total = out[rows] + trade[0, local].astype(F32) + tail
        res_out[local] = (x[rows].astype(F32) + total).astype(BF)
        du = (dnorm[rows] + trade[1, local].astype(F32)) * wide(0)
        back = du - jnp.mean(du, axis=1, keepdims=True) - z * jnp.mean(du * z, axis=1, keepdims=True)
        sg_out[local] = g[rows].astype(F32) + inverse * back
        return carry

    lax.fori_loop(0, blocks, finish_rows, 0)
    for kind in range(2):
        for t in range(2):
            row_copy(kind, t, False).wait_send()


def core(p, b, group, chunks, stream, cotangent, lengths):
    n, C, D, W, CW, rq = p.n, p.C, p.D, p.W, p.CW, p.rq
    m = n // 2
    half = m // 2
    hops = 2 * half - 1
    rows = p.rows
    a_rows = 6 * rq + 16
    b_rows = 2 * p.mr
    a_own = jnp.concatenate([group[: 6 * rq], group[p.o_small :]], axis=0)
    b_own = group[p.o_merge : p.o_small]
    cosine, sine = rope_tables(rows)
    vmem = pl.BlockSpec(memory_space=pltpu.VMEM)
    hbm = pl.BlockSpec(memory_space=pl.ANY)
    dma = pltpu.SemaphoreType.DMA
    V = pltpu.VMEM
    scratch = [
        V((m, 2, a_rows, W), BF),
        V((m, 2, b_rows, W), BF),
        V((C, m, 2, p.c_rows, CW), BF),
        V((m, 2, 16, W), BF),
        V((rows, D), BF),
        V((rows, D), BF),
        V((rows, D), BF),
        V((max(5 * W, 2 * p.C * CW) // 128, rows, 128), BF),
        V((rows, D), F32),
        V((rows, D), F32),
        V((32, W), F32),
        V((2, p.own_rows, D), BF),
        V((m, 6 * rq, W), BF),
        V((m, b_rows, W), BF),
        V((C, m, p.c_rows, CW), BF),
        V((m, 16, W), BF),
        V((hops, 6 * rq, W), BF),
        V((hops, b_rows, W), BF),
        V((C, hops, p.c_rows, CW), BF),
        V((hops, 16, W), BF),
        dma((C + 2, 2, half + 1)),
        dma((C + 2, 2, half + 1)),
        dma((C + 2,)),
        dma((C + 2,)),
        dma((C + 3, 2, half + 1)),
        dma((C + 3, 2, half + 1)),
        dma((C + 3,)),
        dma((C + 3,)),
        dma((6,)),
        dma((6,)),
        dma((2,)),
    ]
    shapes = (
        jax.ShapeDtypeStruct((p.own_rows, D), BF),
        jax.ShapeDtypeStruct((p.own_rows, D), F32),
        jax.ShapeDtypeStruct((6 * rq, W), F32),
        jax.ShapeDtypeStruct((b_rows, W), F32),
        jax.ShapeDtypeStruct((C, p.c_rows, CW), F32),
        jax.ShapeDtypeStruct((16, W), F32),
    )
    flops = 2 * rows * D * (6 * p.FF // 2 + 9 * W + 3 * W) + 12 * rows * rows * W
    residual, stream_grad, ga, gb, gc, gs = pl.pallas_call(
        functools.partial(block_kernel, p),
        out_shape=shapes,
        in_specs=[vmem, vmem, vmem, hbm, hbm, pl.BlockSpec(memory_space=pltpu.SMEM), vmem, vmem],
        out_specs=tuple(vmem for _ in shapes),
        scratch_shapes=scratch,
        compiler_params=pltpu.CompilerParams(
            collective_id=0, has_side_effects=True, vmem_limit_bytes=63 * 1024 * 1024
        ),
        cost_estimate=pl.CostEstimate(flops=flops, bytes_accessed=8 << 20, transcendentals=0),
    )(a_own, b_own, chunks, stream, cotangent, lengths, cosine, sine)
    grad_group = jnp.concatenate([ga, gb], axis=0)
    return residual, stream_grad, grad_group, gc, gs


def finish(p, b, linear, group, chunks, small):
    mix = group[: 6 * p.rq].reshape(3, 2, p.rq, p.W)
    exp = chunks[:, : 2 * p.rq].reshape(p.C, 2, p.rq, p.CW)
    keep = (pick(mix, b, 1), pick(exp, b, 1), small)
    give = (pick(mix, 1 - b, 1), pick(exp, 1 - b, 1), small)
    got = swap_branch(jax.tree.map(lambda a: a.astype(BF), give[:2]) + (give[2],))

    def weave(axis, mine, theirs):
        theirs = theirs.astype(F32)
        return jnp.stack([jnp.where(b == 0, mine, theirs), jnp.where(b == 0, theirs, mine)], axis)

    grad_mixing = weave(2, keep[0].transpose(1, 0, 2), got[0].transpose(1, 0, 2))
    grad_mixing = grad_mixing.reshape(p.rq, -1)

    def columns(a):
        return a.reshape(p.C, p.rq, p.n, p.q).transpose(1, 2, 0, 3)

    grad_expand = weave(2, columns(keep[1]), columns(got[1])).reshape(p.rq, p.FF)
    mer = group[p.o_merge : p.o_merge + 2 * p.mr].reshape(2, p.mr, p.W)[:, : p.rr]
    mer = mer.transpose(1, 0, 2).reshape(p.rr, p.D)
    grad_merging = lax.ppermute(
        mer.astype(BF), ("dp", "branch"), [(t, s) for s, t in merge_perm(p.n)]
    ).astype(F32)
    shr = chunks[:, 2 * p.rq : 2 * p.rq + p.wb * p.q].reshape(p.C, p.wb, p.q, p.CW)
    grad_shrink = shr.transpose(0, 2, 1, 3).reshape(p.hb, p.D)
    mine, theirs = keep[2].reshape(-1), got[2].reshape(-1)
    total = mine + theirs
    grad_vectors = lax.dynamic_slice(
        total[: 2 * p.D].reshape(2, p.D), (0, linear * p.vc), (2, p.vc)
    )
    lo, hi = 2 * p.D, 2 * p.D + p.FF // 2

    def hidden(a):
        return a[lo:hi].reshape(p.C, p.n, p.q).transpose(1, 0, 2)

    hid = weave(1, hidden(mine), hidden(theirs)).reshape(p.FF)
    tail = mine[hi : hi + p.D]
    offs = jnp.concatenate([hid, tail])
    grad_offsets = lax.dynamic_slice(offs, (linear * p.ow,), (p.ow,))
    return grad_mixing, grad_merging, grad_expand, grad_shrink, grad_vectors, grad_offsets


def local(n, stream, cotangent, lengths, steps_taken, learning_rates, *params):
    masters, momenta, variances = params[:6], params[6:12], params[12:]
    p = Plan(n, stream, *masters)
    b = lax.axis_index("branch")
    linear = lax.axis_index("dp") * 2 + b
    group, chunks = prepare(p, b, linear, *masters)
    residual, stream_grad, group, chunks, small = core(
        p, b, group, chunks, stream, cotangent, lengths
    )
    grads = finish(p, b, linear, group, chunks, small)
    count = steps_taken[0].astype(F32)
    outs = [residual, stream_grad]
    for k in range(6):
        decay = decay_rate if k < 4 else 0.0
        outs.extend(
            adam_update(
                masters[k], grads[k], momenta[k], variances[k], learning_rates[k], count, decay
            )
        )
    return tuple(outs)


def solution(mesh):
    rows = P(("dp", "branch"), None)
    cols = P(None, ("dp", "branch"))
    flat = P(("dp", "branch"))
    six = (rows, rows, rows, rows, cols, flat)
    return jax.shard_map(
        functools.partial(local, mesh.shape["dp"]),
        mesh=mesh,
        in_specs=(rows, rows, P("dp"), P(), P()) + six * 3,
        out_specs=(rows, rows) + sum(((s,) * 4 for s in six), ()),
        check_vma=False,
    )
```

```python
import functools

import jax
import jax.numpy as jnp
import numpy as np
from jax import lax
from jax.experimental import pallas as pl
from jax.experimental.pallas import tpu as pltpu
from jax.sharding import PartitionSpec as P

HEAD = 64
ROT = 32
beta_one = 0.9
beta_two = 0.95
adam_eps = 1e-08
decay_rate = 0.1
norm_eps = 1e-05
rope_base = 10000.0
masked_score = -1e30
BF = jnp.bfloat16
F32 = jnp.float32


def dot(left, right):
    return jnp.dot(left, right, preferred_element_type=F32)


def dot_left(left, right):
    return lax.dot_general(left, right, (((0,), (0,)), ((), ())), preferred_element_type=F32)


def dot_right(left, right):
    return lax.dot_general(left, right, (((1,), (1,)), ((), ())), preferred_element_type=F32)


def rope_tables(length):
    places = np.arange(length, dtype=np.float32)[:, None]
    column = np.arange(2 * HEAD) % HEAD
    paired = (column // 2).astype(np.float32)
    frequency = np.exp(paired * np.float32(-2.0 / ROT) * np.log(np.float32(rope_base)))
    angles = (places * frequency[None, :].astype(np.float32)).astype(np.float64)
    inside = (column < ROT)[None, :]
    signed = np.where(column % 2 == 0, -1.0, 1.0)[None, :]
    cosine = np.where(inside, np.cos(angles), 1.0).astype(np.float32)
    sine = np.where(inside, np.sin(angles) * signed, 0.0).astype(np.float32)
    return cosine, sine


def adam_update(master, gradient, momentum, variance, rate, count, decay):
    drift = beta_one * momentum + (1.0 - beta_one) * gradient
    power = beta_two * variance + (1.0 - beta_two) * gradient * gradient
    first_fix = 1.0 - jnp.power(beta_one, count)
    second_fix = 1.0 - jnp.power(beta_two, count)
    moved = drift / first_fix / (jnp.sqrt(power / second_fix) + adam_eps)
    updated = master - rate * (moved + decay * master)
    return (updated, updated.astype(BF), drift, power)


class Plan:
    def __init__(self, n, stream, mixing, merging, expand, shrink, vectors, offsets):
        self.n = n
        self.own_rows, self.D = stream.shape
        self.rows = 2 * self.own_rows
        self.W = self.D // 2
        self.FF = expand.shape[1]
        self.rq = mixing.shape[0]
        self.rr = merging.shape[0]
        self.mr = max(16, self.rr)
        self.hb = shrink.shape[0]
        self.C = 4 if self.hb >= 64 else 2
        self.q = self.hb // self.C
        self.CW = self.FF // 2 // self.C
        self.wb = self.D // self.CW
        self.vc = vectors.shape[1]
        self.ow = offsets.shape[0]
        self.o_merge = 6 * self.rq
        self.o_small = self.o_merge + 2 * self.mr
        self.g_rows = self.o_small + 16
        self.c_rows = 2 * self.rq + self.wb * self.q


MESH = pl.DeviceIdType.MESH
BLOCK = 256
ATTEND_SHARE = 14
LATE = 2
AB_START = 1.0
AB_STEP = 6.0
C_START = 0.5
C_STEP = 5.0


def turned(a, cosine, sine, back):
    lanes = a.shape[1]
    even = lax.broadcasted_iota(jnp.int32, a.shape, 1) % 2 == 0
    t = a * sine if back else a
    swapped = jnp.where(even, pltpu.roll(t, lanes - 1, 1), pltpu.roll(t, 1, 1))
    return a * cosine + (swapped if back else swapped * sine)


def tile_lanes(a, times):
    return jnp.concatenate([a] * times, axis=1) if times > 1 else a


def flat2(a):
    return a.reshape(-1, a.shape[-1])


def gelu_parts(pre):
    root = 0.7978845608028654
    square = pre * pre
    t = jnp.tanh(root * pre * (1.0 + 0.044715 * square))
    hidden = 0.5 * pre * (1.0 + t)
    slope = 0.5 * (1.0 + t) + 0.5 * pre * (1.0 - t * t) * root * (1.0 + 0.134145 * square)
    return hidden, slope


def block_kernel(
    p,
    stream,
    cotangent,
    mixing,
    merging,
    expand,
    shrink,
    small_own,
    length,
    cos_ref,
    sin_ref,
    res_out,
    sg_out,
    gmix_out,
    gmer_out,
    gexp_out,
    gshr_out,
    gsmall_out,
    wa,
    wb,
    wc,
    ws,
    x,
    g,
    normed,
    lanes,
    out,
    dnorm,
    small,
    trade,
    sib_a,
    sib_b,
    sib_c,
    sib_s,
    slot_a,
    slot_b,
    slot_c,
    slot_s,
    ag_send,
    ag_recv,
    as_send,
    as_recv,
    rs_send,
    rs_recv,
    ss_send,
    ss_recv,
    x_send,
    x_recv,
    own_sem,
    sw_mix,
    sw_exp,
    sw_small,
    mer,
    keep_exp,
    sw_send,
    sw_recv,
    sh_send,
    sh_recv,
):
    n, C, D, W, CW, rq, q = p.n, p.C, p.D, p.W, p.CW, p.rq, p.q
    SD = BF if rq % 16 == 0 else F32
    m = n // 2
    half = m // 2
    blocks = p.rows // BLOCK
    pairs = W // 128
    groups = CW // 128
    at_q, at_k, at_v, at_att, at_da = (t * pairs for t in range(5))
    at_hid, at_slope = 0, C * groups
    d = lax.axis_index("dp")
    b = lax.axis_index("branch")
    core = lax.rem(d, 2)
    chip = d // 2
    ring = jnp.where(lax.rem(chip, 2) == 0, chip // 2, m - 1 - chip // 2)
    step = 1 - 2 * core

    def around(k):
        pos = lax.rem(ring + step * k + m, m)
        return jnp.where(pos < half, 2 * pos, 2 * (m - 1 - pos) + 1)

    ahead = (2 * around(1) + core, b)
    behind = (2 * around(-1) + core, b)
    sibling = (d + step, b)
    partner = (d, 1 - b)
    ways = (ahead, behind)

    sources = [(mixing, t * D, t * rq, rq) for t in range(3)]
    sources += [(expand, t * D, (3 + t) * rq, rq) for t in range(p.FF // D)]
    sources += [(merging, 0, 7 * rq, p.rr), (shrink, 0, 8 * rq, p.hb)]
    loads = [
        pltpu.make_async_copy(
            ref.at[:, pl.ds(column, D)], dnorm.at[pl.ds(row, count)], own_sem.at[2 + t]
        )
        for t, (ref, column, row, count) in enumerate(sources)
    ]
    for load in loads:
        load.start()
    barrier = pltpu.get_barrier_semaphore()
    for other in (ahead, behind, sibling, partner):
        pl.semaphore_signal(barrier, inc=1, device_id=other, device_id_type=MESH)
    rank, origin = 2 * d + b, n * b + d
    merge_to = (lax.rem(rank, n), rank // n)
    merge_from = (origin // 2, lax.rem(origin, 2))
    moves = d != b * (n - 1)

    @pl.when(moves)
    def _():
        for other in (merge_to, merge_from):
            pl.semaphore_signal(barrier, inc=1, device_id=other, device_id_type=MESH)
        pl.semaphore_wait(barrier, 6)

    @pl.when(jnp.logical_not(moves))
    def _():
        pl.semaphore_wait(barrier, 4)


    def remote(src, dst, send, recv, to):
        return pltpu.make_async_remote_copy(
            src_ref=src, dst_ref=dst, send_sem=send, recv_sem=recv, device_id=to, device_id_type=MESH
        )

    own_rows = pl.ds(pl.multiple_of(b * p.own_rows, p.own_rows), p.own_rows)
    their_rows = pl.ds(pl.multiple_of((1 - b) * p.own_rows, p.own_rows), p.own_rows)

    def gather_ref(k):
        return wa if k == 0 else wb if k == 1 else wc.at[k - 2]

    def last_hop(way):
        return half - way

    def gather_copy(k, way, hop):
        shard = gather_ref(k).at[around((1 - hop) * (1 - 2 * way)), core]
        return remote(shard, shard, ag_send.at[k, way, hop], ag_recv.at[k, way, hop], ways[way])

    def gather_arrival(k, way, hop):
        shard = gather_ref(k).at[around(-hop * (1 - 2 * way)), core]
        return remote(shard, shard, ag_send.at[k, way, hop], ag_recv.at[k, way, hop], ways[way])

    def gather_sibling(k, whose):
        part = gather_ref(k).at[:, whose]
        return remote(part, part, as_send.at[k], as_recv.at[k], sibling)

    def gather_share(k, way, hop, arriving):
        shift = -hop * (1 - 2 * way)
        shard = gather_ref(k)
        shard = shard.at[around(-shift), 1 - core] if arriving else shard.at[around(shift), core]
        return remote(shard, shard, sh_send.at[k, way, hop], sh_recv.at[k, way, hop], sibling)

    def shares():
        hops = [(way, hop) for way in range(2) for hop in range(1, last_hop(way) + 1)]
        return [(0, 0)] + hops

    def gather_start(k):
        for way in range(2):
            gather_copy(k, way, 1).start()
        if k < 2:
            gather_share(k, 0, 0, False).start()

    def gather_event(k, hop):
        for way in range(2):
            if hop <= last_hop(way):
                gather_arrival(k, way, hop).wait_recv()
                if hop < last_hop(way):
                    gather_copy(k, way, hop + 1).start()
                if k < 2:
                    gather_share(k, way, hop, False).start()
        if hop == half and k >= 2:
            gather_sibling(k, core).start()

    def gather_ready(k):
        if k >= 2:
            gather_sibling(k, 1 - core).wait_recv()
            return
        for way, hop in shares():
            gather_share(k, way, hop, True).wait_recv()

    def gather_done(k):
        for way in range(2):
            for hop in range(1, last_hop(way) + 1):
                gather_copy(k, way, hop).wait_send()
        if k >= 2:
            gather_sibling(k, core).wait_send()
            return
        for way, hop in shares():
            gather_share(k, way, hop, False).wait_send()

    def scatter_refs(k):
        if k == 0:
            return wa, sib_a, slot_a, 6 * rq
        if k == 1:
            return wb, sib_b, slot_b, 2 * p.mr
        if k < C + 2:
            return wc.at[k - 2], sib_c.at[k - 2], slot_c.at[k - 2], p.c_rows
        return ws, sib_s, slot_s, 16

    def swap_copy(ref, src, dst, sem):
        return remote(ref.at[src], ref.at[dst], sw_send.at[sem], sw_recv.at[sem], partner)

    def exp_back(j):
        cut = pl.ds(j * rq, rq)
        return remote(
            sw_exp.at[0, cut], sw_exp.at[2, cut], sw_send.at[7 + j], sw_recv.at[7 + j], partner
        )

    def mer_back():
        return remote(mer.at[0], mer.at[1], sw_send.at[5], sw_recv.at[5], merge_from)

    def pair(upper, lower):
        return jnp.where(b == 0, upper, lower), jnp.where(b == 0, lower, upper)

    def half_lanes(t, which):
        return pl.ds(pl.multiple_of(t * D + which * W, W), W)

    def scatter_result(k, total):
        if k == 0:
            for t in range(3):
                upper = total[2 * t * rq : (2 * t + 1) * rq]
                keep, give = pair(upper, total[(2 * t + 1) * rq : (2 * t + 2) * rq])
                gmix_out[:, half_lanes(t, b)] = keep
                sw_mix[0, t * rq : (t + 1) * rq] = give.astype(SD)
            swap_copy(sw_mix, 0, 2, 4).start()
        elif k == 1:
            mer[0] = total.astype(BF)

            @pl.when(moves)
            def _():
                mer_back().start()

        elif k < C + 2:
            j = k - 2
            keep, give = pair(total[:rq], total[rq : 2 * rq])
            keep_exp[j * rq : (j + 1) * rq] = keep
            sw_exp[0, j * rq : (j + 1) * rq] = give.astype(SD)
            exp_back(j).start()
            for t in range(p.wb):
                part = total[2 * rq + t * q : 2 * rq + (t + 1) * q]
                gshr_out[j * q : (j + 1) * q, t * CW : (t + 1) * CW] = part
        else:
            sw_small[0] = total
            swap_copy(sw_small, 0, 2, 6).start()

    def scatter_sibling(k):
        whole, sib, _, rows = scatter_refs(k)
        src = whole.at[:, 1 - core, pl.ds(0, rows)]
        return remote(src, sib, ss_send.at[k], ss_recv.at[k], sibling)

    def slot_of(way, hop):
        return (hop - 1) if way == 0 else half + hop - 1

    def scatter_copy(k, way, hop):
        whole, _, slots, rows = scatter_refs(k)
        target = around((last_hop(way) + 1 - hop) * (1 - 2 * way))
        src = whole.at[target, core, pl.ds(0, rows)]
        return remote(
            src, slots.at[slot_of(way, hop)], rs_send.at[k, way, hop], rs_recv.at[k, way, hop], ways[way]
        )

    def scatter_event(k, hop):
        whole, sib, slots, rows = scatter_refs(k)
        if hop == 0:
            scatter_sibling(k).start()
            return
        if hop == 1:
            scatter_sibling(k).wait_recv()
        for way in range(2):
            if hop <= last_hop(way):
                target = around((last_hop(way) + 1 - hop) * (1 - 2 * way))
                here = whole.at[target, core, pl.ds(0, rows)]
                total = here[...].astype(F32) + sib[target].astype(F32)
                if hop > 1:
                    scatter_copy(k, way, hop - 1).wait_recv()
                    total = total + slots[slot_of(way, hop - 1)].astype(F32)
                here[...] = total.astype(BF)
                scatter_copy(k, way, hop).start()
        if hop == half + 1:
            total = whole[chip, core, pl.ds(0, rows)].astype(F32) + sib[chip].astype(F32)
            for way in range(2):
                scatter_copy(k, way, last_hop(way)).wait_recv()
                total = total + slots[slot_of(way, last_hop(way))].astype(F32)
            scatter_result(k, total)
            for way in range(2):
                for sent in range(1, last_hop(way) + 1):
                    scatter_copy(k, way, sent).wait_send()
            scatter_sibling(k).wait_send()

    piece = p.own_rows // 2

    def quarter(whose, t):
        return pl.ds(pl.multiple_of(whose * p.own_rows + t * piece, piece), piece)

    def row_copy(kind, t, receiving):
        src, dst = ((stream, x), (cotangent, g))[kind]
        sem = 2 * kind + t
        there = dst.at[quarter(1 - b if receiving else b, t)]
        return remote(src.at[pl.ds(t * piece, piece)], there, x_send.at[sem], x_recv.at[sem], partner)

    keep_x = pltpu.make_async_copy(stream, x.at[own_rows], own_sem.at[0])
    keep_g = pltpu.make_async_copy(cotangent, g.at[own_rows], own_sem.at[1])

    for t in range(3):
        loads[t].wait()
    kept_mix = []
    for t in range(3):
        v = dnorm[t * rq : (t + 1) * rq]
        keep, give = pair(v[:, :W], v[:, W:])
        kept_mix.append(keep)
        sw_mix[0, t * rq : (t + 1) * rq] = give.astype(SD)
    swap_copy(sw_mix, 0, 1, 0).start()
    sw_small[0] = small_own[...]
    swap_copy(sw_small, 0, 1, 1).start()
    row_copy(0, 0, False).start()
    for load in loads[3:]:
        load.wait()
    mer[0] = jnp.zeros((2 * p.mr, W), BF)
    own_merge = dnorm[7 * rq : 7 * rq + p.rr].astype(BF)
    for t in range(2):
        mer[0, t * p.mr : t * p.mr + p.rr] = own_merge[:, t * W : (t + 1) * W]
    mer_there = (merge_to[0] // 2, lax.rem(merge_to[0], 2))

    def mer_copy(slot):
        return remote(mer.at[0], wb.at[slot], sw_send.at[3], sw_recv.at[3], merge_to)

    @pl.when(moves)
    def _():
        mer_copy(mer_there).start()

    @pl.when(jnp.logical_not(moves))
    def _():
        wb[chip, core] = mer[0]

    swap_copy(sw_mix, 0, 1, 0).wait_recv()
    swap_copy(sw_small, 0, 1, 1).wait_recv()
    for t in range(3):
        got = sw_mix[1, t * rq : (t + 1) * rq].astype(F32)
        both_halves = jnp.concatenate(pair(kept_mix[t], got), axis=0).astype(BF)
        wa[chip, core, 2 * t * rq : 2 * (t + 1) * rq] = both_halves
    wa[chip, core, 6 * rq : 6 * rq + 16] = (sw_small[0] + sw_small[1]).astype(BF)
    gather_start(0)

    @pl.when(moves)
    def _():
        mer_copy((chip, core)).wait_recv()

    gather_start(1)
    per_lane = 128 // q

    def pieces(fetch, width):
        spot = lax.broadcasted_iota(jnp.int32, (width, 128), 1) // q
        result = None
        for e in range(per_lane):
            block, at = fetch(e)
            shift = (e * q - at) % 128
            block = pltpu.roll(block, shift, 1) if shift else block
            result = block if e == 0 else jnp.where(spot == e, block, result)
        return result

    def to_plane(block_at, width, j, plane):
        def column(o):
            def fetch(e):
                start = (2 * (o * per_lane + e) + plane) * p.hb + j * q
                return block_at(start // 128), start % 128

            return pieces(fetch, width)

        return jnp.concatenate([column(o) for o in range(groups)], axis=1)

    def from_plane(block_at, width):
        def column(c):
            def fetch(e):
                start = c * 128 + e * q
                unit_block = start // p.hb
                lane = (unit_block // 2) * q
                block = block_at(unit_block % 2, (start % p.hb) // q, lane // 128)
                return block, lane % 128

            return pieces(fetch, width)

        return [column(c) for c in range(p.FF // 128)]

    wide_blocks = D // 128

    def expand_block(c):
        at = (3 + c // wide_blocks) * rq
        lane = (c % wide_blocks) * 128
        return dnorm[at : at + rq, lane : lane + 128]

    for j in range(C):
        keep, give = pair(to_plane(expand_block, rq, j, 0), to_plane(expand_block, rq, j, 1))
        keep_exp[j * rq : (j + 1) * rq] = keep
        sw_exp[0, j * rq : (j + 1) * rq] = give.astype(SD)
    swap_copy(sw_exp, 0, 1, 2).start()

    @pl.when(b == 0)
    def _():
        row_copy(0, 1, False).start()
        row_copy(1, 0, False).start()

    @pl.when(b == 1)
    def _():
        row_copy(1, 0, False).start()
        row_copy(0, 1, False).start()

    row_copy(1, 1, False).start()
    keep_x.start()
    keep_g.start()
    for j in range(C):
        for t in range(p.wb):
            at = 8 * rq + j * q
            piece_rows = dnorm[at : at + q, t * CW : (t + 1) * CW].astype(BF)
            wc[j, chip, core, 2 * rq + t * q : 2 * rq + (t + 1) * q] = piece_rows
    def chunk_shards():
        swap_copy(sw_exp, 0, 1, 2).wait_recv()
        for j in range(C):
            got = sw_exp[1, j * rq : (j + 1) * rq].astype(F32)
            both_halves = jnp.concatenate(pair(keep_exp[j * rq : (j + 1) * rq], got), axis=0)
            wc[j, chip, core, : 2 * rq] = both_halves.astype(BF)

    out[...] = jnp.zeros((p.rows, D), F32)
    for hop in range(1, half + 1):
        gather_event(0, hop)
        gather_event(1, hop)
        if hop == half - 1:
            chunk_shards()
            gather_start(2)
    for j in range(1, C):
        gather_start(2 + j)
    swap_copy(sw_mix, 0, 1, 0).wait_send()
    swap_copy(sw_small, 0, 1, 1).wait_send()
    swap_copy(sw_exp, 0, 1, 2).wait_send()

    @pl.when(moves)
    def _():
        mer_copy(mer_there).wait_send()


    def weight(t):
        return flat2(wa[:, :, t * 2 * rq : (t + 1) * 2 * rq, :])

    def merge_weight(t):
        whole = wb[:, :, t * p.mr : (t + 1) * p.mr, :]
        if p.mr == p.rr:
            return flat2(whole)
        whole = whole.astype(F32).reshape(n, p.mr, W)[:, : p.rr]
        return whole.reshape(W, W).astype(BF)

    def wide(row):
        return jnp.concatenate([small[row : row + 1], small[row + 1 : row + 2]], axis=1)

    def unit(rows):
        v = x[rows].astype(F32)
        centred = v - jnp.mean(v, axis=1, keepdims=True)
        inverse = lax.rsqrt(jnp.mean(centred * centred, axis=1, keepdims=True) + norm_eps)
        return centred * inverse, inverse

    def rows_of(i):
        return pl.ds(pl.multiple_of(i * BLOCK, BLOCK), BLOCK)

    def project(i):
        rows = rows_of(i)
        z, _ = unit(rows)
        nb = (z * wide(0) + wide(2)).astype(BF)
        normed[rows] = nb
        cosine = tile_lanes(cos_ref[rows], pairs)
        sine = tile_lanes(sin_ref[rows], pairs)
        query = (turned(dot(nb, weight(0)), cosine, sine, False) * HEAD**-0.5).astype(BF)
        key = turned(dot(nb, weight(1)), cosine, sine, False).astype(BF)
        value = dot(nb, weight(2)).astype(BF)
        for t in range(pairs):
            cut = slice(t * 128, (t + 1) * 128)
            lanes[at_q + t, rows] = query[:, cut]
            lanes[at_k + t, rows] = key[:, cut]
            lanes[at_v + t, rows] = value[:, cut]

    def gradient(i):
        rows = rows_of(i)
        position = lax.broadcasted_iota(jnp.int32, (BLOCK, D), 0) + i * BLOCK
        gb = jnp.where(position < length[0], g[rows].astype(F32), 0.0).astype(BF)
        g[rows] = gb
        da = (dot_right(gb[:, :W], merge_weight(0)) + dot_right(gb[:, W:], merge_weight(1))).astype(BF)
        for t in range(pairs):
            lanes[at_da + t, rows] = da[:, t * 128 : (t + 1) * 128]

    def each(body, start, count):
        def run(i, carry):
            body(start + i)
            return carry

        lax.fori_loop(0, count, run, 0)

    keep_x.wait()
    keep_g.wait()
    gather_ready(0)
    small[:16] = jnp.sum(wa[:, :, 6 * rq :, :].reshape(n, 16, W).astype(F32), axis=0)
    first_bias, plane_bias, plane_grad = 2 * D // W, 32, 40

    def bias_block(c):
        row, lane = first_bias + c * 128 // W, c * 128 % W
        return jnp.broadcast_to(small[row : row + 1, lane : lane + 128], (8, 128))

    for j in range(C):
        mine, _ = pair(to_plane(bias_block, 8, j, 0), to_plane(bias_block, 8, j, 1))
        for t in range(CW // W):
            row = plane_bias + j * CW // W + t
            small[row : row + 1] = mine[:1, t * W : (t + 1) * W]
    part = blocks // 2
    each(project, b * part, part)
    gather_ready(1)
    each(gradient, b * part, part)

    @pl.when(b == 1)
    def _():
        row_copy(0, 0, True).wait_recv()
        row_copy(0, 1, True).wait_recv()
        each(project, 0, part)

    def spread(items, count, first=0):
        return [items[len(items) * t // count : len(items) * (t + 1) // count] for t in range(count)]

    events = []
    for hop in range(1, half + 1):
        events += [(2 + j, hop) for j in range(C)]
    attend_slots = spread(events[: len(events) * ATTEND_SHARE // 16], blocks * pairs)
    merge_events = events[len(events) * ATTEND_SHARE // 16 :]

    def attend(i, t):
        lane = lax.broadcasted_iota(jnp.int32, (BLOCK, 128), 1)
        rows = slice(i * BLOCK, (i + 1) * BLOCK)
        width = (i + 1) * BLOCK
        qb, dab = lanes[at_q + t, rows], lanes[at_da + t, rows]
        keys, values = lanes[at_k + t, :width], lanes[at_v + t, :width]
        zero = jnp.zeros_like(qb)
        mixed = []
        dquery = []
        dkey = jnp.zeros((width, 128), F32)
        dvalue = jnp.zeros((width, 128), F32)
        for h in range(2):
            mine = (lane < HEAD) if h == 0 else (lane >= HEAD)
            qm = jnp.where(mine, qb, zero)
            dm = jnp.where(mine, dab, zero)
            scores = dot_right(qm, keys)
            down = lax.broadcasted_iota(jnp.int32, (BLOCK, BLOCK), 0)
            over = lax.broadcasted_iota(jnp.int32, (BLOCK, BLOCK), 1)
            edge = jnp.where(down >= over, scores[:, width - BLOCK :], masked_score)
            scores = jnp.concatenate([scores[:, : width - BLOCK], edge], axis=1) if i else edge
            weights = jnp.exp(scores - jnp.max(scores, axis=1, keepdims=True))
            weights = weights * (1.0 / jnp.sum(weights, axis=1, keepdims=True))
            rounded = weights.astype(BF)
            dweights = dot_right(dm, values)
            delta = jnp.sum(weights * dweights, axis=1, keepdims=True)
            dscores = (weights * (dweights - delta)).astype(BF)
            mixed.append(dot(rounded, values))
            dquery.append(dot(dscores, keys))
            dvalue = dvalue + dot_left(rounded, dm)
            dkey = dkey + dot_left(dscores, qm)
        first = lane < HEAD
        position = lax.broadcasted_iota(jnp.int32, (BLOCK, 128), 0) + i * BLOCK
        whole = jnp.where(first, mixed[0], mixed[1])
        lanes[at_att + t, rows] = jnp.where(position < length[0], whole, 0.0).astype(BF)
        dq = jnp.where(first, dquery[0], dquery[1]) * HEAD**-0.5
        lanes[at_q + t, rows] = turned(dq, cos_ref[rows], sin_ref[rows], True).astype(BF)
        out[:width, head_lanes(t, 0)] += dkey
        out[:width, head_lanes(t, 1)] += dvalue

    def head_lanes(t, which):
        return pl.ds(pl.multiple_of(which * W + t * 128, 128), 128)

    def attention(it, carry):
        stage, t = it // pairs, lax.rem(it, pairs)
        now = lax.rem(stage + b * part, blocks)

        @pl.when((t == 0) & (b == 0) & (stage >= part))
        def _():
            for u in range(2):

                @pl.when(stage == part + u * (part // 2))
                def _(u=u):
                    row_copy(0, u, True).wait_recv()
                    row_copy(1, u, True).wait_recv()
                    each(project, part + u * (part // 2), part // 2)
                    each(gradient, part + u * (part // 2), part // 2)

        @pl.when((t == 0) & (b == 1) & (stage == part))
        def _():
            row_copy(1, 0, True).wait_recv()
            row_copy(1, 1, True).wait_recv()
            each(gradient, 0, part)

        for i in range(blocks):

            @pl.when(now == i)
            def _(i=i):
                attend(i, t)

        @pl.when(stage == blocks - 1)
        def _():
            dk = out[:, head_lanes(t, 0)]
            lanes[at_k + t] = turned(dk, cos_ref[...], sin_ref[...], True).astype(BF)
            lanes[at_v + t] = out[:, head_lanes(t, 1)].astype(BF)

        for slot, todo in enumerate(attend_slots):
            if todo:

                @pl.when(it == slot)
                def _(todo=todo):
                    for k, hop in todo:
                        gather_event(k, hop)

        return carry

    lax.fori_loop(0, blocks * pairs, attention, 0)

    def side(at, rows, count=pairs):
        return jnp.concatenate([lanes[at + t, rows] for t in range(count)], axis=1)

    def merge(i, carry):
        rows = rows_of(i)
        total = dot_right(side(at_q, rows), weight(0))
        total = total + dot_right(side(at_k, rows), weight(1))
        dnorm[rows] = total + dot_right(side(at_v, rows), weight(2))
        return carry

    lax.fori_loop(0, blocks, merge, 0)
    for k, hop in merge_events[: len(merge_events) // 2]:
        gather_event(k, hop)
    gather_done(0)
    every = slice(0, p.rows)
    chips = BLOCK // (4 * rq)

    def mix_grads(i, carry):
        left = normed[:, rows_of(i)]
        where = pl.ds(i * chips, chips)
        for t in range(3):
            res = dot_left(left, side(t * pairs, every)).astype(BF)
            wa[where, :, t * 2 * rq : (t + 1) * 2 * rq, :] = res.reshape(chips, 2, 2 * rq, W)
        return carry

    lax.fori_loop(0, D // BLOCK, mix_grads, 0)
    scatter_event(0, 0)
    for k, hop in merge_events[len(merge_events) // 2 :]:
        gather_event(k, hop)

    def attend_out(i, carry):
        rows = rows_of(i)
        ab = side(at_att, rows)
        out[rows, :W] = dot(ab, merge_weight(0))
        out[rows, W:] = dot(ab, merge_weight(1))
        return carry

    lax.fori_loop(0, blocks, attend_out, 0)
    gather_done(1)
    merged = BLOCK // (2 * p.rr)
    for i in range(W // BLOCK):
        left = side(at_att + 2 * i, every, 2)
        for t in range(2):
            res = dot_left(left, g[:, t * W : (t + 1) * W]).reshape(merged, 2, p.rr, W)
            if p.mr != p.rr:
                res = jnp.concatenate([res, jnp.zeros((merged, 2, p.mr - p.rr, W), F32)], axis=2)
            wb[i * merged : (i + 1) * merged, :, t * p.mr : (t + 1) * p.mr, :] = res.astype(BF)
    scatter_event(1, 0)

    order = [(0, j) for j in range(C)]
    for j in range(C):
        if j < C - LATE:
            order += [(1, j), (2, j)]
    order += [(1, j) for j in range(C - LATE, C)] + [(2, j) for j in range(C - LATE, C)]
    fore_at, back_at, grad_at = ({}, {}, {})
    total_slots = 0
    for kind, j in order:
        (fore_at, back_at, grad_at)[kind][j] = total_slots
        total_slots += 2 if kind == 2 else blocks
    timed = []
    pace = 4.0 / half
    for hop in range(1, half + 2):
        timed += [(AB_START + (hop - 1) * AB_STEP * pace, k, hop) for k in range(2)]
        for j in range(C):
            begin = grad_at[j] + 2 + C_START
            timed.append((begin + (hop - 1) * C_STEP * pace, 2 + j, hop))
    timed.sort()
    slots = [[e[1:] for e in timed if t <= e[0] < t + 1] for t in range(total_slots)]
    leftover = [e[1:] for e in timed if e[0] >= total_slots]

    def run_slot(slot):
        for k, hop in slots[slot]:
            scatter_event(k, hop)

    def run_when(i, start):
        for i0 in range(blocks):
            if slots[start + i0]:

                @pl.when(i == i0)
                def _(i0=i0):
                    run_slot(start + i0)

    def hidden_bias(j):
        at = plane_bias + j * CW // W
        return jnp.concatenate([small[at + t : at + t + 1] for t in range(CW // W)], axis=1)

    def shrink_weight(j, t):
        return flat2(wc[j, :, :, 2 * rq + t * q : 2 * rq + (t + 1) * q, :])

    last = (2 * D + p.FF) // W
    give_out = remote(res_out, trade.at[0], x_send.at[4], x_recv.at[4], partner)
    give_dn = remote(res_out, trade.at[1], x_send.at[5], x_recv.at[5], partner)

    def forward(j):
        gather_ready(2 + j)

        def feed(i, carry):
            rows = rows_of(i)
            pre = dot(normed[rows], flat2(wc[j, :, :, : 2 * rq, :])) + hidden_bias(j)
            hid, slope = gelu_parts(pre)
            hid, slope = hid.astype(BF), slope.astype(BF)
            for t in range(groups):
                lanes[at_hid + j * groups + t, rows] = hid[:, t * 128 : (t + 1) * 128]
                lanes[at_slope + j * groups + t, rows] = slope[:, t * 128 : (t + 1) * 128]
            for t in range(p.wb):
                out[rows, t * CW : (t + 1) * CW] += dot(hid, shrink_weight(j, t))
            run_when(i, fore_at[j])
            return carry

        lax.fori_loop(0, blocks, feed, 0)

    def backward(j):

        def back(i, carry):
            rows = rows_of(i)
            gb = g[rows]
            dhid = dot_right(gb[:, :CW], shrink_weight(j, 0))
            for t in range(1, p.wb):
                dhid = dhid + dot_right(gb[:, t * CW : (t + 1) * CW], shrink_weight(j, t))
            dp = (dhid * side(at_slope + j * groups, rows, groups).astype(F32)).astype(BF)
            for t in range(groups):
                lanes[at_slope + j * groups + t, rows] = dp[:, t * 128 : (t + 1) * 128]
            dnorm[rows] += dot_right(dp, flat2(wc[j, :, :, : 2 * rq, :]))
            run_when(i, back_at[j])
            return carry + jnp.sum(dp.astype(F32), axis=0, keepdims=True)

        bias_grad = lax.fori_loop(0, blocks, back, jnp.zeros((1, CW), F32))
        for t in range(CW // W):
            at = plane_grad + j * CW // W + t
            small[at : at + 1] = bias_grad[:, t * W : (t + 1) * W]

    def gradients(j):
        gather_done(2 + j)

        def expand_grads(i, carry):
            res = dot_left(normed[:, rows_of(i)], side(at_slope + j * groups, every, groups)).astype(BF)
            wc[j, pl.ds(i * chips, chips), :, : 2 * rq, :] = res.reshape(chips, 2, 2 * rq, CW)
            return carry

        lax.fori_loop(0, D // BLOCK, expand_grads, 0)
        run_slot(grad_at[j])
        per = BLOCK // (2 * q)

        def shrink_grads(i, carry):
            left = side(at_hid + j * groups + 2 * i, every, 2)
            for t in range(p.wb):
                res = dot_left(left, g[:, t * CW : (t + 1) * CW]).astype(BF)
                cut = slice(2 * rq + t * q, 2 * rq + (t + 1) * q)
                wc[j, pl.ds(i * per, per), :, cut, :] = res.reshape(per, 2, q, CW)
            return carry

        lax.fori_loop(0, CW // BLOCK, shrink_grads, 0)
        scatter_event(2 + j, 0)
        run_slot(grad_at[j] + 1)

    for kind, j in order:
        (forward, backward, gradients)[kind](j)
        if (kind, j) == (0, C - 1):
            res_out[...] = out[their_rows].astype(BF)
            give_out.start()
        if (kind, j) == (1, C - 1):
            give_out.wait_send()
            res_out[...] = dnorm[their_rows].astype(BF)
            give_dn.start()

    def small_gradients():
        def vector_grads(i, carry):
            rows = rows_of(i)
            z, _ = unit(rows)
            dn = dnorm[rows]
            gain = carry[0] + jnp.sum(dn * z, axis=0, keepdims=True)
            shift = carry[1] + jnp.sum(dn, axis=0, keepdims=True)
            return gain, shift, carry[2] + jnp.sum(g[rows].astype(F32), axis=0, keepdims=True)

        zero_row = jnp.zeros((1, D), F32)
        sums = lax.fori_loop(0, blocks, vector_grads, (zero_row, zero_row, zero_row))
        tail_grad = jnp.where(b == 0, sums[2], 0.0)

        def grad_block(plane, j, o):
            at = j * CW + o * 128
            row, lane = plane_grad + at // W, at % W
            v = jnp.broadcast_to(small[row : row + 1, lane : lane + 128], (8, 128))
            return jnp.where(b == plane, v, 0.0)

        for c, v in enumerate(from_plane(grad_block, 8)):
            row, lane = 16 + first_bias + c * 128 // W, c * 128 % W
            small[row : row + 1, lane : lane + 128] = v[:1]
        for at, row in ((0, sums[0]), (2, sums[1]), (last, tail_grad)):
            small[16 + at : 17 + at] = row[:, :W]
            small[17 + at : 18 + at] = row[:, W:]
        small[16 + last + 2 : 32] = jnp.zeros((14 - last, W), F32)
        ws[...] = jnp.broadcast_to(small[16:32].astype(BF)[None, None], (m, 2, 16, W))
        scatter_event(C + 2, 0)

    def finish_all():
        small_rows = p.own_rows // blocks
        give_out.wait_recv()
        give_dn.wait_recv()
        give_dn.wait_send()

        def finish_rows(i, carry):
            local = pl.ds(pl.multiple_of(i * small_rows, small_rows), small_rows)
            rows = pl.ds(pl.multiple_of(b * p.own_rows + i * small_rows, small_rows), small_rows)
            z, inverse = unit(rows)
            tail = wide(last)
            total = out[rows] + trade[0, local].astype(F32) + tail
            res_out[local] = (x[rows].astype(F32) + total).astype(BF)
            du = (dnorm[rows] + trade[1, local].astype(F32)) * wide(0)
            back = du - jnp.mean(du, axis=1, keepdims=True) - z * jnp.mean(du * z, axis=1, keepdims=True)
            sg_out[local] = g[rows].astype(F32) + inverse * back
            return carry

        lax.fori_loop(0, blocks, finish_rows, 0)

    small_hop = 0
    for k, hop in leftover:
        if k == C + 1 and hop == half + 1:
            finish_all()
        scatter_event(k, hop)
        if k == C + 1:
            if hop == 1:
                small_gradients()
            else:
                small_hop += 1
                scatter_event(C + 2, small_hop)
    scatter_event(C + 2, half + 1)

    for kind in range(2):
        for t in range(2):
            row_copy(kind, t, False).wait_send()
    swap_copy(sw_mix, 0, 2, 4).wait()
    for t in range(3):
        gmix_out[:, half_lanes(t, 1 - b)] = sw_mix[2, t * rq : (t + 1) * rq].astype(F32)

    @pl.when(moves)
    def _():
        mer_back().wait_send()
        remote(mer.at[0], mer.at[1], sw_send.at[5], sw_recv.at[5], merge_to).wait_recv()

    @pl.when(jnp.logical_not(moves))
    def _():
        mer[1] = mer[0]

    for t in range(2):
        merged_rows = mer[1, t * p.mr : (t + 1) * p.mr].astype(F32)
        gmer_out[:, t * W : (t + 1) * W] = merged_rows[: p.rr]
    for j in range(C):
        exp_back(j).wait()

    def summed_block(plane, j, o):
        rows, cols = slice(j * rq, (j + 1) * rq), slice(o * 128, (o + 1) * 128)
        return jnp.where(b == plane, keep_exp[rows, cols], sw_exp[2, rows, cols].astype(F32))

    for c, v in enumerate(from_plane(summed_block, rq)):
        gexp_out[:, c * 128 : (c + 1) * 128] = v
    swap_copy(sw_small, 0, 2, 6).wait()
    gsmall_out[...] = sw_small[0] + sw_small[2]


def core(p, stream, cotangent, lengths, mixing, merging, expand, shrink, small_own):
    n, C, D, W, CW, rq = p.n, p.C, p.D, p.W, p.CW, p.rq
    m = n // 2
    half = m // 2
    hops = 2 * half - 1
    rows = p.rows
    a_rows = 6 * rq + 16
    b_rows = 2 * p.mr
    cosine, sine = (jnp.asarray(table) for table in rope_tables(rows))
    vmem = pl.BlockSpec(memory_space=pltpu.VMEM)
    hbm = pl.BlockSpec(memory_space=pl.ANY)
    dma = pltpu.SemaphoreType.DMA
    V = pltpu.VMEM
    SD = BF if rq % 16 == 0 else F32
    scratch = [
        V((m, 2, a_rows, W), BF),
        V((m, 2, b_rows, W), BF),
        V((C, m, 2, p.c_rows, CW), BF),
        V((m, 2, 16, W), BF),
        V((rows, D), BF),
        V((rows, D), BF),
        V((rows, D), BF),
        V((max(5 * W, 2 * p.C * CW) // 128, rows, 128), BF),
        V((rows, D), F32),
        V((rows, D), F32),
        V((48, W), F32),
        V((2, p.own_rows, D), BF),
        V((m, 6 * rq, W), BF),
        V((m, b_rows, W), BF),
        V((C, m, p.c_rows, CW), BF),
        V((m, 16, W), BF),
        V((hops, 6 * rq, W), BF),
        V((hops, b_rows, W), BF),
        V((C, hops, p.c_rows, CW), BF),
        V((hops, 16, W), BF),
        dma((C + 2, 2, half + 1)),
        dma((C + 2, 2, half + 1)),
        dma((C + 2,)),
        dma((C + 2,)),
        dma((C + 3, 2, half + 1)),
        dma((C + 3, 2, half + 1)),
        dma((C + 3,)),
        dma((C + 3,)),
        dma((6,)),
        dma((6,)),
        dma((7 + p.FF // D,)),
        V((3, 3 * rq, W), SD),
        V((3, C * rq, CW), SD),
        V((3, 16, W), F32),
        V((2, b_rows, W), BF),
        V((C * rq, CW), F32),
        dma((7 + C,)),
        dma((7 + C,)),
        dma((2, 2, half + 1)),
        dma((2, 2, half + 1)),
    ]
    shapes = (
        jax.ShapeDtypeStruct((p.own_rows, D), BF),
        jax.ShapeDtypeStruct((p.own_rows, D), F32),
        jax.ShapeDtypeStruct((rq, 3 * D), F32),
        jax.ShapeDtypeStruct((p.rr, D), F32),
        jax.ShapeDtypeStruct((rq, p.FF), F32),
        jax.ShapeDtypeStruct((p.hb, D), F32),
        jax.ShapeDtypeStruct((16, W), F32),
    )
    flops = 2 * rows * D * (6 * p.FF // 2 + 9 * W + 3 * W) + 12 * rows * rows * W
    return pl.pallas_call(
        functools.partial(block_kernel, p),
        out_shape=shapes,
        in_specs=[hbm] * 6 + [vmem, pl.BlockSpec(memory_space=pltpu.SMEM), vmem, vmem],
        out_specs=tuple(vmem for _ in shapes),
        scratch_shapes=scratch,
        compiler_params=pltpu.CompilerParams(
            collective_id=0, has_side_effects=True, vmem_limit_bytes=63 * 1024 * 1024
        ),
        cost_estimate=pl.CostEstimate(flops=flops, bytes_accessed=8 << 20, transcendentals=0),
    )(stream, cotangent, mixing, merging, expand, shrink, small_own, lengths, cosine, sine)


def local(n, stream, cotangent, lengths, steps_taken, learning_rates, *params):
    masters, momenta, variances = params[:6], params[6:12], params[12:]
    p = Plan(n, stream, *masters)
    linear = lax.axis_index("dp") * 2 + lax.axis_index("branch")
    vectors, offsets = masters[4], masters[5]
    small = jnp.zeros((16 * p.W,), F32)
    for row in range(2):
        small = lax.dynamic_update_slice(small, vectors[row], (row * p.D + linear * p.vc,))
    small = lax.dynamic_update_slice(small, offsets, (2 * p.D + linear * p.ow,))
    residual, stream_grad, *grads, small = core(
        p, stream, cotangent, lengths, *masters[:4], small.reshape(16, p.W)
    )
    small = small.reshape(-1)
    rows = [
        lax.dynamic_slice(small, (row * p.D + linear * p.vc,), (p.vc,)) for row in range(2)
    ]
    grads.append(jnp.stack(rows))
    grads.append(lax.dynamic_slice(small, (2 * p.D + linear * p.ow,), (p.ow,)))
    count = steps_taken[0].astype(F32)
    outs = [residual, stream_grad]
    for k in range(6):
        decay = decay_rate if k < 4 else 0.0
        outs.extend(
            adam_update(
                masters[k], grads[k], momenta[k], variances[k], learning_rates[k], count, decay
            )
        )
    return tuple(outs)


def solution(mesh):
    rows = P(("dp", "branch"), None)
    cols = P(None, ("dp", "branch"))
    flat = P(("dp", "branch"))
    six = (rows, rows, rows, rows, cols, flat)
    return jax.shard_map(
        functools.partial(local, mesh.shape["dp"]),
        mesh=mesh,
        in_specs=(rows, rows, P("dp"), P(), P()) + six * 3,
        out_specs=(rows, rows) + sum(((s,) * 4 for s in six), ()),
        check_vma=False,
    )
```

```python
import functools

import jax
import jax.numpy as jnp
import numpy as np
from jax import lax
from jax.experimental import pallas as pl
from jax.experimental.pallas import tpu as pltpu
from jax.sharding import PartitionSpec as P

HEAD = 64
ROT = 32
beta_one = 0.9
beta_two = 0.95
adam_eps = 1e-08
decay_rate = 0.1
norm_eps = 1e-05
rope_base = 10000.0
masked_score = -1e30
BF = jnp.bfloat16
F32 = jnp.float32


def dot(left, right):
    return jnp.dot(left, right, preferred_element_type=F32)


def dot_left(left, right):
    return lax.dot_general(left, right, (((0,), (0,)), ((), ())), preferred_element_type=F32)


def dot_right(left, right):
    return lax.dot_general(left, right, (((1,), (1,)), ((), ())), preferred_element_type=F32)


def rope_tables(length):
    places = np.arange(length, dtype=np.float32)[:, None]
    column = np.arange(2 * HEAD) % HEAD
    paired = (column // 2).astype(np.float32)
    frequency = np.exp(paired * np.float32(-2.0 / ROT) * np.log(np.float32(rope_base)))
    angles = (places * frequency[None, :].astype(np.float32)).astype(np.float64)
    inside = (column < ROT)[None, :]
    signed = np.where(column % 2 == 0, -1.0, 1.0)[None, :]
    cosine = np.where(inside, np.cos(angles), 1.0).astype(np.float32)
    sine = np.where(inside, np.sin(angles) * signed, 0.0).astype(np.float32)
    return cosine, sine


def adam_update(master, gradient, momentum, variance, rate, count, decay):
    drift = beta_one * momentum + (1.0 - beta_one) * gradient
    power = beta_two * variance + (1.0 - beta_two) * gradient * gradient
    first_fix = 1.0 - jnp.power(beta_one, count)
    second_fix = 1.0 - jnp.power(beta_two, count)
    moved = drift / first_fix / (jnp.sqrt(power / second_fix) + adam_eps)
    updated = master - rate * (moved + decay * master)
    return (updated, updated.astype(BF), drift, power)


class Plan:
    def __init__(self, n, stream, mixing, merging, expand, shrink, vectors, offsets):
        self.n = n
        self.own_rows, self.D = stream.shape
        self.rows = 2 * self.own_rows
        self.W = self.D // 2
        self.FF = expand.shape[1]
        self.rq = mixing.shape[0]
        self.rr = merging.shape[0]
        self.mr = max(16, self.rr)
        self.hb = shrink.shape[0]
        self.C = 4 if self.hb >= 64 else 2
        self.q = self.hb // self.C
        self.CW = self.FF // 2 // self.C
        self.wb = self.D // self.CW
        self.vc = vectors.shape[1]
        self.ow = offsets.shape[0]
        self.o_merge = 6 * self.rq
        self.o_small = self.o_merge + 2 * self.mr
        self.g_rows = self.o_small + 16
        self.c_rows = 2 * self.rq + self.wb * self.q


MESH = pl.DeviceIdType.MESH
BLOCK = 256
ATTEND_SHARE = 14
LATE = 1
AB_START = 1.0
AB_STEP = 6.0
C_START = 0.5
C_STEP = 4.0


def turned(a, cosine, sine, back):
    lanes = a.shape[1]
    even = lax.broadcasted_iota(jnp.int32, a.shape, 1) % 2 == 0
    t = a * sine if back else a
    swapped = jnp.where(even, pltpu.roll(t, lanes - 1, 1), pltpu.roll(t, 1, 1))
    return a * cosine + (swapped if back else swapped * sine)


def tile_lanes(a, times):
    return jnp.concatenate([a] * times, axis=1) if times > 1 else a


def flat2(a):
    return a.reshape(-1, a.shape[-1])


def gelu_parts(pre):
    root = 0.7978845608028654
    square = pre * pre
    t = jnp.tanh(root * pre * (1.0 + 0.044715 * square))
    hidden = 0.5 * pre * (1.0 + t)
    slope = 0.5 * (1.0 + t) + 0.5 * pre * (1.0 - t * t) * root * (1.0 + 0.134145 * square)
    return hidden, slope


def block_kernel(
    p,
    stream,
    cotangent,
    mixing,
    merging,
    expand,
    shrink,
    small_own,
    length,
    cos_ref,
    sin_ref,
    res_out,
    sg_out,
    gmix_out,
    gmer_out,
    gexp_out,
    gshr_out,
    gsmall_out,
    wa,
    wb,
    wc,
    ws,
    x,
    g,
    normed,
    lanes,
    out,
    dnorm,
    small,
    trade,
    sib_a,
    sib_b,
    sib_c,
    sib_s,
    slot_a,
    slot_b,
    slot_c,
    slot_s,
    ag_send,
    ag_recv,
    as_send,
    as_recv,
    rs_send,
    rs_recv,
    ss_send,
    ss_recv,
    x_send,
    x_recv,
    own_sem,
    sw_mix,
    sw_exp,
    sw_small,
    mer,
    keep_exp,
    sw_send,
    sw_recv,
    sh_send,
    sh_recv,
):
    n, C, D, W, CW, rq, q = p.n, p.C, p.D, p.W, p.CW, p.rq, p.q
    SD = BF if rq % 16 == 0 else F32
    m = n // 2
    half = m // 2
    blocks = p.rows // BLOCK
    pairs = W // 128
    groups = CW // 128
    at_q, at_k, at_v, at_att, at_da = (t * pairs for t in range(5))
    at_hid, at_slope = 0, C * groups
    d = lax.axis_index("dp")
    b = lax.axis_index("branch")
    core = lax.rem(d, 2)
    chip = d // 2
    ring = jnp.where(lax.rem(chip, 2) == 0, chip // 2, m - 1 - chip // 2)
    step = 1 - 2 * core

    def around(k):
        pos = lax.rem(ring + step * k + m, m)
        return jnp.where(pos < half, 2 * pos, 2 * (m - 1 - pos) + 1)

    ahead = (2 * around(1) + core, b)
    behind = (2 * around(-1) + core, b)
    sibling = (d + step, b)
    partner = (d, 1 - b)
    ways = (ahead, behind)

    sources = [(mixing, t * D, t * rq, rq) for t in range(3)]
    sources += [(expand, t * D, (3 + t) * rq, rq) for t in range(p.FF // D)]
    sources += [(merging, 0, 7 * rq, p.rr), (shrink, 0, 8 * rq, p.hb)]
    loads = [
        pltpu.make_async_copy(
            ref.at[:, pl.ds(column, D)], dnorm.at[pl.ds(row, count)], own_sem.at[2 + t]
        )
        for t, (ref, column, row, count) in enumerate(sources)
    ]
    for load in loads:
        load.start()
    barrier = pltpu.get_barrier_semaphore()
    for other in (ahead, behind, sibling, partner):
        pl.semaphore_signal(barrier, inc=1, device_id=other, device_id_type=MESH)
    rank, origin = 2 * d + b, n * b + d
    merge_to = (lax.rem(rank, n), rank // n)
    merge_from = (origin // 2, lax.rem(origin, 2))
    moves = d != b * (n - 1)

    @pl.when(moves)
    def _():
        for other in (merge_to, merge_from):
            pl.semaphore_signal(barrier, inc=1, device_id=other, device_id_type=MESH)
        pl.semaphore_wait(barrier, 6)

    @pl.when(jnp.logical_not(moves))
    def _():
        pl.semaphore_wait(barrier, 4)


    def remote(src, dst, send, recv, to):
        return pltpu.make_async_remote_copy(
            src_ref=src, dst_ref=dst, send_sem=send, recv_sem=recv, device_id=to, device_id_type=MESH
        )

    own_rows = pl.ds(pl.multiple_of(b * p.own_rows, p.own_rows), p.own_rows)
    their_rows = pl.ds(pl.multiple_of((1 - b) * p.own_rows, p.own_rows), p.own_rows)

    def gather_ref(k):
        return wa if k == 0 else wb if k == 1 else wc.at[k - 2]

    def last_hop(way):
        return half - way

    def gather_copy(k, way, hop):
        shard = gather_ref(k).at[around((1 - hop) * (1 - 2 * way)), core]
        return remote(shard, shard, ag_send.at[k, way, hop], ag_recv.at[k, way, hop], ways[way])

    def gather_arrival(k, way, hop):
        shard = gather_ref(k).at[around(-hop * (1 - 2 * way)), core]
        return remote(shard, shard, ag_send.at[k, way, hop], ag_recv.at[k, way, hop], ways[way])

    def gather_sibling(k, whose):
        part = gather_ref(k).at[:, whose]
        return remote(part, part, as_send.at[k], as_recv.at[k], sibling)

    def gather_share(k, way, hop, arriving):
        shift = -hop * (1 - 2 * way)
        shard = gather_ref(k)
        shard = shard.at[around(-shift), 1 - core] if arriving else shard.at[around(shift), core]
        return remote(shard, shard, sh_send.at[k, way, hop], sh_recv.at[k, way, hop], sibling)

    def shares():
        hops = [(way, hop) for way in range(2) for hop in range(1, last_hop(way) + 1)]
        return [(0, 0)] + hops

    def gather_start(k):
        for way in range(2):
            gather_copy(k, way, 1).start()
        if k < 2:
            gather_share(k, 0, 0, False).start()

    def gather_event(k, hop):
        for way in range(2):
            if hop <= last_hop(way):
                gather_arrival(k, way, hop).wait_recv()
                if hop < last_hop(way):
                    gather_copy(k, way, hop + 1).start()
                if k < 2:
                    gather_share(k, way, hop, False).start()
        if hop == half and k >= 2:
            gather_sibling(k, core).start()

    def gather_ready(k):
        if k >= 2:
            gather_sibling(k, 1 - core).wait_recv()
            return
        for way, hop in shares():
            gather_share(k, way, hop, True).wait_recv()

    def gather_done(k):
        for way in range(2):
            for hop in range(1, last_hop(way) + 1):
                gather_copy(k, way, hop).wait_send()
        if k >= 2:
            gather_sibling(k, core).wait_send()
            return
        for way, hop in shares():
            gather_share(k, way, hop, False).wait_send()

    tail_group = C + 3

    def scatter_refs(k):
        if k == 0:
            return wa, sib_a, slot_a, 0, 6 * rq
        if k == 1:
            return wb, sib_b, slot_b, 0, 2 * p.mr
        if k == C + 2:
            return ws, sib_s, slot_s, 0, 16
        j = C - 1 if k == tail_group else k - 2
        first, count = (0, p.c_rows) if j < C - 1 else (0, 2 * rq)
        if k == tail_group:
            first, count = 2 * rq, p.c_rows - 2 * rq
        cut = pl.ds(first, count)
        return wc.at[j], sib_c.at[j, :, cut], slot_c.at[j, :, cut], first, count

    def swap_copy(ref, src, dst, sem):
        return remote(ref.at[src], ref.at[dst], sw_send.at[sem], sw_recv.at[sem], partner)

    def exp_back(j):
        cut = pl.ds(j * rq, rq)
        return remote(
            sw_exp.at[0, cut], sw_exp.at[2, cut], sw_send.at[7 + j], sw_recv.at[7 + j], partner
        )

    def mer_back():
        return remote(mer.at[0], mer.at[1], sw_send.at[5], sw_recv.at[5], merge_from)

    def pair(upper, lower):
        return jnp.where(b == 0, upper, lower), jnp.where(b == 0, lower, upper)

    def half_lanes(t, which):
        return pl.ds(pl.multiple_of(t * D + which * W, W), W)

    def shrink_result(j, total):
        for t in range(p.wb):
            part = total[t * q : (t + 1) * q]
            gshr_out[j * q : (j + 1) * q, t * CW : (t + 1) * CW] = part

    def scatter_result(k, total):
        if k == 0:
            for t in range(3):
                upper = total[2 * t * rq : (2 * t + 1) * rq]
                keep, give = pair(upper, total[(2 * t + 1) * rq : (2 * t + 2) * rq])
                gmix_out[:, half_lanes(t, b)] = keep
                sw_mix[0, t * rq : (t + 1) * rq] = give.astype(SD)
            swap_copy(sw_mix, 0, 2, 4).start()
        elif k == 1:
            mer[0] = total.astype(BF)

            @pl.when(moves)
            def _():
                mer_back().start()

        elif k < C + 2:
            j = k - 2
            keep, give = pair(total[:rq], total[rq : 2 * rq])
            keep_exp[j * rq : (j + 1) * rq] = keep
            sw_exp[0, j * rq : (j + 1) * rq] = give.astype(SD)
            exp_back(j).start()
            if j < C - 1:
                shrink_result(j, total[2 * rq :])
        elif k == tail_group:
            shrink_result(C - 1, total)
        else:
            sw_small[0] = total
            swap_copy(sw_small, 0, 2, 6).start()

    def scatter_sibling(k):
        whole, sib, _, first, rows = scatter_refs(k)
        src = whole.at[:, 1 - core, pl.ds(first, rows)]
        return remote(src, sib, ss_send.at[k], ss_recv.at[k], sibling)

    def slot_of(way, hop):
        return (hop - 1) if way == 0 else half + hop - 1

    def scatter_copy(k, way, hop):
        whole, _, slots, first, rows = scatter_refs(k)
        target = around((last_hop(way) + 1 - hop) * (1 - 2 * way))
        src = whole.at[target, core, pl.ds(first, rows)]
        return remote(
            src, slots.at[slot_of(way, hop)], rs_send.at[k, way, hop], rs_recv.at[k, way, hop], ways[way]
        )

    def scatter_event(k, hop):
        whole, sib, slots, first, rows = scatter_refs(k)
        if hop == 0:
            scatter_sibling(k).start()
            return
        if hop == 1:
            scatter_sibling(k).wait_recv()
        for way in range(2):
            if hop <= last_hop(way):
                target = around((last_hop(way) + 1 - hop) * (1 - 2 * way))
                here = whole.at[target, core, pl.ds(first, rows)]
                total = here[...].astype(F32) + sib[target].astype(F32)
                if hop > 1:
                    scatter_copy(k, way, hop - 1).wait_recv()
                    total = total + slots[slot_of(way, hop - 1)].astype(F32)
                here[...] = total.astype(BF)
                scatter_copy(k, way, hop).start()
        if hop == half + 1:
            total = whole[chip, core, pl.ds(first, rows)].astype(F32) + sib[chip].astype(F32)
            for way in range(2):
                scatter_copy(k, way, last_hop(way)).wait_recv()
                total = total + slots[slot_of(way, last_hop(way))].astype(F32)
            scatter_result(k, total)
            for way in range(2):
                for sent in range(1, last_hop(way) + 1):
                    scatter_copy(k, way, sent).wait_send()
            scatter_sibling(k).wait_send()

    piece = p.own_rows // 2

    def quarter(whose, t):
        return pl.ds(pl.multiple_of(whose * p.own_rows + t * piece, piece), piece)

    def row_copy(kind, t, receiving):
        src, dst = ((stream, x), (cotangent, g))[kind]
        sem = 2 * kind + t
        there = dst.at[quarter(1 - b if receiving else b, t)]
        return remote(src.at[pl.ds(t * piece, piece)], there, x_send.at[sem], x_recv.at[sem], partner)

    keep_x = pltpu.make_async_copy(stream, x.at[own_rows], own_sem.at[0])
    keep_g = pltpu.make_async_copy(cotangent, g.at[own_rows], own_sem.at[1])

    for t in range(3):
        loads[t].wait()
    kept_mix = []
    for t in range(3):
        v = dnorm[t * rq : (t + 1) * rq]
        keep, give = pair(v[:, :W], v[:, W:])
        kept_mix.append(keep)
        sw_mix[0, t * rq : (t + 1) * rq] = give.astype(SD)
    swap_copy(sw_mix, 0, 1, 0).start()
    sw_small[0] = small_own[...]
    swap_copy(sw_small, 0, 1, 1).start()
    for load in loads[3:]:
        load.wait()
    mer[0] = jnp.zeros((2 * p.mr, W), BF)
    own_merge = dnorm[7 * rq : 7 * rq + p.rr].astype(BF)
    for t in range(2):
        mer[0, t * p.mr : t * p.mr + p.rr] = own_merge[:, t * W : (t + 1) * W]
    mer_there = (merge_to[0] // 2, lax.rem(merge_to[0], 2))

    def mer_copy(slot):
        return remote(mer.at[0], wb.at[slot], sw_send.at[3], sw_recv.at[3], merge_to)

    @pl.when(moves)
    def _():
        mer_copy(mer_there).start()

    @pl.when(jnp.logical_not(moves))
    def _():
        wb[chip, core] = mer[0]

    swap_copy(sw_mix, 0, 1, 0).wait_recv()
    row_copy(0, 0, False).start()
    swap_copy(sw_small, 0, 1, 1).wait_recv()
    for t in range(3):
        got = sw_mix[1, t * rq : (t + 1) * rq].astype(F32)
        both_halves = jnp.concatenate(pair(kept_mix[t], got), axis=0).astype(BF)
        wa[chip, core, 2 * t * rq : 2 * (t + 1) * rq] = both_halves
    wa[chip, core, 6 * rq : 6 * rq + 16] = (sw_small[0] + sw_small[1]).astype(BF)
    gather_start(0)
    per_lane = 128 // q

    def pieces(fetch, width):
        spot = lax.broadcasted_iota(jnp.int32, (width, 128), 1) // q
        result = None
        for e in range(per_lane):
            block, at = fetch(e)
            shift = (e * q - at) % 128
            block = pltpu.roll(block, shift, 1) if shift else block
            result = block if e == 0 else jnp.where(spot == e, block, result)
        return result

    def to_plane(block_at, width, j, plane):
        def column(o):
            def fetch(e):
                start = (2 * (o * per_lane + e) + plane) * p.hb + j * q
                return block_at(start // 128), start % 128

            return pieces(fetch, width)

        return jnp.concatenate([column(o) for o in range(groups)], axis=1)

    def from_plane(block_at, width):
        def column(c):
            def fetch(e):
                start = c * 128 + e * q
                unit_block = start // p.hb
                lane = (unit_block // 2) * q
                block = block_at(unit_block % 2, (start % p.hb) // q, lane // 128)
                return block, lane % 128

            return pieces(fetch, width)

        return [column(c) for c in range(p.FF // 128)]

    wide_blocks = D // 128

    def expand_block(c):
        at = (3 + c // wide_blocks) * rq
        lane = (c % wide_blocks) * 128
        return dnorm[at : at + rq, lane : lane + 128]

    for j in range(C):
        keep, give = pair(to_plane(expand_block, rq, j, 0), to_plane(expand_block, rq, j, 1))
        keep_exp[j * rq : (j + 1) * rq] = keep
        sw_exp[0, j * rq : (j + 1) * rq] = give.astype(SD)
    swap_copy(sw_exp, 0, 1, 2).start()

    @pl.when(b == 0)
    def _():
        row_copy(0, 1, False).start()
        row_copy(1, 0, False).start()

    @pl.when(b == 1)
    def _():
        row_copy(1, 0, False).start()
        row_copy(0, 1, False).start()

    row_copy(1, 1, False).start()
    keep_x.start()
    keep_g.start()
    for j in range(C):
        for t in range(p.wb):
            at = 8 * rq + j * q
            piece_rows = dnorm[at : at + q, t * CW : (t + 1) * CW].astype(BF)
            wc[j, chip, core, 2 * rq + t * q : 2 * rq + (t + 1) * q] = piece_rows
    def chunk_shards():
        swap_copy(sw_exp, 0, 1, 2).wait_recv()
        for j in range(C):
            got = sw_exp[1, j * rq : (j + 1) * rq].astype(F32)
            both_halves = jnp.concatenate(pair(keep_exp[j * rq : (j + 1) * rq], got), axis=0)
            wc[j, chip, core, : 2 * rq] = both_halves.astype(BF)

    out[...] = jnp.zeros((p.rows, D), F32)
    for hop in range(1, half + 1):
        gather_event(0, hop)
        if hop == 1:

            @pl.when(moves)
            def _():
                mer_copy((chip, core)).wait_recv()

            gather_start(1)
        else:
            gather_event(1, hop - 1)
        if hop == half - 1:
            chunk_shards()
            gather_start(2)
    gather_event(1, half)
    for j in range(1, C):
        gather_start(2 + j)
    swap_copy(sw_mix, 0, 1, 0).wait_send()
    swap_copy(sw_small, 0, 1, 1).wait_send()
    swap_copy(sw_exp, 0, 1, 2).wait_send()

    @pl.when(moves)
    def _():
        mer_copy(mer_there).wait_send()


    def weight(t):
        return flat2(wa[:, :, t * 2 * rq : (t + 1) * 2 * rq, :])

    def merge_weight(t):
        whole = wb[:, :, t * p.mr : (t + 1) * p.mr, :]
        if p.mr == p.rr:
            return flat2(whole)
        whole = whole.astype(F32).reshape(n, p.mr, W)[:, : p.rr]
        return whole.reshape(W, W).astype(BF)

    def wide(row):
        return jnp.concatenate([small[row : row + 1], small[row + 1 : row + 2]], axis=1)

    def unit(rows):
        v = x[rows].astype(F32)
        centred = v - jnp.mean(v, axis=1, keepdims=True)
        inverse = lax.rsqrt(jnp.mean(centred * centred, axis=1, keepdims=True) + norm_eps)
        return centred * inverse, inverse

    def rows_of(i):
        return pl.ds(pl.multiple_of(i * BLOCK, BLOCK), BLOCK)

    def project(i):
        rows = rows_of(i)
        z, _ = unit(rows)
        nb = (z * wide(0) + wide(2)).astype(BF)
        normed[rows] = nb
        cosine = tile_lanes(cos_ref[rows], pairs)
        sine = tile_lanes(sin_ref[rows], pairs)
        query = (turned(dot(nb, weight(0)), cosine, sine, False) * HEAD**-0.5).astype(BF)
        key = turned(dot(nb, weight(1)), cosine, sine, False).astype(BF)
        value = dot(nb, weight(2)).astype(BF)
        for t in range(pairs):
            cut = slice(t * 128, (t + 1) * 128)
            lanes[at_q + t, rows] = query[:, cut]
            lanes[at_k + t, rows] = key[:, cut]
            lanes[at_v + t, rows] = value[:, cut]

    def gradient(i):
        rows = rows_of(i)
        position = lax.broadcasted_iota(jnp.int32, (BLOCK, D), 0) + i * BLOCK
        gb = jnp.where(position < length[0], g[rows].astype(F32), 0.0).astype(BF)
        g[rows] = gb
        da = (dot_right(gb[:, :W], merge_weight(0)) + dot_right(gb[:, W:], merge_weight(1))).astype(BF)
        for t in range(pairs):
            lanes[at_da + t, rows] = da[:, t * 128 : (t + 1) * 128]

    def each(body, start, count):
        def run(i, carry):
            body(start + i)
            return carry

        lax.fori_loop(0, count, run, 0)

    keep_x.wait()
    keep_g.wait()
    gather_ready(0)
    small[:16] = jnp.sum(wa[:, :, 6 * rq :, :].reshape(n, 16, W).astype(F32), axis=0)
    first_bias, plane_bias, plane_grad = 2 * D // W, 32, 40

    def bias_block(c):
        row, lane = first_bias + c * 128 // W, c * 128 % W
        return jnp.broadcast_to(small[row : row + 1, lane : lane + 128], (8, 128))

    for j in range(C):
        mine, _ = pair(to_plane(bias_block, 8, j, 0), to_plane(bias_block, 8, j, 1))
        for t in range(CW // W):
            row = plane_bias + j * CW // W + t
            small[row : row + 1] = mine[:1, t * W : (t + 1) * W]
    part = blocks // 2
    each(project, b * part, part)
    gather_ready(1)
    each(gradient, b * part, part)

    @pl.when(b == 1)
    def _():
        row_copy(0, 0, True).wait_recv()
        row_copy(0, 1, True).wait_recv()
        each(project, 0, part)

    def spread(items, count, first=0):
        return [items[len(items) * t // count : len(items) * (t + 1) // count] for t in range(count)]

    events = []
    for hop in range(1, half + 1):
        events += [(2 + j, hop) for j in range(C)]
    attend_slots = spread(events[: len(events) * ATTEND_SHARE // 16], blocks * pairs)
    merge_events = events[len(events) * ATTEND_SHARE // 16 :]

    def attend(i, t):
        lane = lax.broadcasted_iota(jnp.int32, (BLOCK, 128), 1)
        rows = slice(i * BLOCK, (i + 1) * BLOCK)
        width = (i + 1) * BLOCK
        qb, dab = lanes[at_q + t, rows], lanes[at_da + t, rows]
        keys, values = lanes[at_k + t, :width], lanes[at_v + t, :width]
        zero = jnp.zeros_like(qb)
        first = lane < HEAD
        qm = jnp.concatenate([jnp.where(first, qb, zero), jnp.where(first, zero, qb)], axis=0)
        dm = jnp.concatenate([jnp.where(first, dab, zero), jnp.where(first, zero, dab)], axis=0)
        scores = dot_right(qm, keys)
        down = lax.rem(lax.broadcasted_iota(jnp.int32, (2 * BLOCK, BLOCK), 0), BLOCK)
        over = lax.broadcasted_iota(jnp.int32, (2 * BLOCK, BLOCK), 1)
        edge = jnp.where(down >= over, scores[:, width - BLOCK :], masked_score)
        scores = jnp.concatenate([scores[:, : width - BLOCK], edge], axis=1) if i else edge
        weights = jnp.exp(scores - jnp.max(scores, axis=1, keepdims=True))
        weights = weights * (1.0 / jnp.sum(weights, axis=1, keepdims=True))
        rounded = weights.astype(BF)
        dweights = dot_right(dm, values)
        delta = jnp.sum(weights * dweights, axis=1, keepdims=True)
        dscores = (weights * (dweights - delta)).astype(BF)
        mixed = dot(rounded, values)
        dquery = dot(dscores, keys)
        dvalue = dot_left(rounded, dm)
        dkey = dot_left(dscores, qm)
        position = lax.broadcasted_iota(jnp.int32, (BLOCK, 128), 0) + i * BLOCK
        whole = jnp.where(first, mixed[:BLOCK], mixed[BLOCK:])
        lanes[at_att + t, rows] = jnp.where(position < length[0], whole, 0.0).astype(BF)
        dq = jnp.where(first, dquery[:BLOCK], dquery[BLOCK:]) * HEAD**-0.5
        lanes[at_q + t, rows] = turned(dq, cos_ref[rows], sin_ref[rows], True).astype(BF)
        out[:width, head_lanes(t, 0)] += dkey
        out[:width, head_lanes(t, 1)] += dvalue

    def head_lanes(t, which):
        return pl.ds(pl.multiple_of(which * W + t * 128, 128), 128)

    def attention(it, carry):
        stage, t = it // pairs, lax.rem(it, pairs)
        now = lax.rem(stage + b * part, blocks)

        @pl.when((t == 0) & (b == 0) & (stage >= part))
        def _():
            for u in range(2):

                @pl.when(stage == part + u * (part // 2))
                def _(u=u):
                    row_copy(0, u, True).wait_recv()
                    row_copy(1, u, True).wait_recv()
                    each(project, part + u * (part // 2), part // 2)
                    each(gradient, part + u * (part // 2), part // 2)

        @pl.when((t == 0) & (b == 1) & (stage == part))
        def _():
            row_copy(1, 0, True).wait_recv()
            row_copy(1, 1, True).wait_recv()
            each(gradient, 0, part)

        for i in range(blocks):

            @pl.when(now == i)
            def _(i=i):
                attend(i, t)

        @pl.when(stage == blocks - 1)
        def _():
            dk = out[:, head_lanes(t, 0)]
            lanes[at_k + t] = turned(dk, cos_ref[...], sin_ref[...], True).astype(BF)
            lanes[at_v + t] = out[:, head_lanes(t, 1)].astype(BF)

        for slot, todo in enumerate(attend_slots):
            if todo:

                @pl.when(it == slot)
                def _(todo=todo):
                    for k, hop in todo:
                        gather_event(k, hop)

        return carry

    lax.fori_loop(0, blocks * pairs, attention, 0)

    def side(at, rows, count=pairs):
        return jnp.concatenate([lanes[at + t, rows] for t in range(count)], axis=1)

    def merge(i, carry):
        rows = rows_of(i)
        total = dot_right(side(at_q, rows), weight(0))
        total = total + dot_right(side(at_k, rows), weight(1))
        dnorm[rows] = total + dot_right(side(at_v, rows), weight(2))
        return carry

    lax.fori_loop(0, blocks, merge, 0)
    for k, hop in merge_events[: len(merge_events) // 2]:
        gather_event(k, hop)
    gather_done(0)
    every = slice(0, p.rows)
    chips = BLOCK // (4 * rq)

    def mix_grads(i, carry):
        left = normed[:, rows_of(i)]
        where = pl.ds(i * chips, chips)
        for t in range(3):
            res = dot_left(left, side(t * pairs, every)).astype(BF)
            wa[where, :, t * 2 * rq : (t + 1) * 2 * rq, :] = res.reshape(chips, 2, 2 * rq, W)
        return carry

    lax.fori_loop(0, D // BLOCK, mix_grads, 0)
    scatter_event(0, 0)
    for k, hop in merge_events[len(merge_events) // 2 :]:
        gather_event(k, hop)

    def attend_out(i, carry):
        rows = rows_of(i)
        ab = side(at_att, rows)
        out[rows, :W] = dot(ab, merge_weight(0))
        out[rows, W:] = dot(ab, merge_weight(1))
        return carry

    lax.fori_loop(0, blocks, attend_out, 0)
    gather_done(1)
    merged = BLOCK // (2 * p.rr)
    for i in range(W // BLOCK):
        left = side(at_att + 2 * i, every, 2)
        for t in range(2):
            res = dot_left(left, g[:, t * W : (t + 1) * W]).reshape(merged, 2, p.rr, W)
            if p.mr != p.rr:
                res = jnp.concatenate([res, jnp.zeros((merged, 2, p.mr - p.rr, W), F32)], axis=2)
            wb[i * merged : (i + 1) * merged, :, t * p.mr : (t + 1) * p.mr, :] = res.astype(BF)
    scatter_event(1, 0)

    order = [(0, j) for j in range(C)]
    for j in range(C):
        if j < C - LATE:
            order += [(1, j), (2, j)]
    order += [(1, j) for j in range(C - LATE, C)] + [(2, j) for j in range(C - LATE, C)]
    fore_at, back_at, grad_at = ({}, {}, {})
    total_slots = 0
    for kind, j in order:
        (fore_at, back_at, grad_at)[kind][j] = total_slots
        total_slots += 2 if kind == 2 else blocks
    timed = []
    pace = 4.0 / half
    for hop in range(1, half + 2):
        timed += [(AB_START + (hop - 1) * AB_STEP * pace, k, hop) for k in range(2)]
        for j in range(C):
            begin = grad_at[j] + 2 + C_START
            timed.append((begin + (hop - 1) * C_STEP * pace, 2 + j, hop))
        timed.append((begin + 0.5 + (hop - 1) * C_STEP * pace, tail_group, hop))
    timed.sort()
    slots = [[e[1:] for e in timed if t <= e[0] < t + 1] for t in range(total_slots)]
    leftover = [e[1:] for e in timed if e[0] >= total_slots]

    def run_slot(slot):
        for k, hop in slots[slot]:
            scatter_event(k, hop)

    def run_when(i, start):
        for i0 in range(blocks):
            if slots[start + i0]:

                @pl.when(i == i0)
                def _(i0=i0):
                    run_slot(start + i0)

    def hidden_bias(j):
        at = plane_bias + j * CW // W
        return jnp.concatenate([small[at + t : at + t + 1] for t in range(CW // W)], axis=1)

    def shrink_weight(j, t):
        return flat2(wc[j, :, :, 2 * rq + t * q : 2 * rq + (t + 1) * q, :])

    last = (2 * D + p.FF) // W
    give_out = remote(res_out, trade.at[0], x_send.at[4], x_recv.at[4], partner)
    give_dn = remote(res_out, trade.at[1], x_send.at[5], x_recv.at[5], partner)

    def forward(j):
        gather_ready(2 + j)

        def feed(i, carry):
            rows = rows_of(i)
            pre = dot(normed[rows], flat2(wc[j, :, :, : 2 * rq, :])) + hidden_bias(j)
            hid, slope = gelu_parts(pre)
            hid, slope = hid.astype(BF), slope.astype(BF)
            for t in range(groups):
                lanes[at_hid + j * groups + t, rows] = hid[:, t * 128 : (t + 1) * 128]
                lanes[at_slope + j * groups + t, rows] = slope[:, t * 128 : (t + 1) * 128]
            for t in range(p.wb):
                out[rows, t * CW : (t + 1) * CW] += dot(hid, shrink_weight(j, t))
            run_when(i, fore_at[j])
            return carry

        lax.fori_loop(0, blocks, feed, 0)

    def backward(j):

        def back(i, carry):
            rows = rows_of(i)
            gb = g[rows]
            dhid = dot_right(gb[:, :CW], shrink_weight(j, 0))
            for t in range(1, p.wb):
                dhid = dhid + dot_right(gb[:, t * CW : (t + 1) * CW], shrink_weight(j, t))
            dp = (dhid * side(at_slope + j * groups, rows, groups).astype(F32)).astype(BF)
            for t in range(groups):
                lanes[at_slope + j * groups + t, rows] = dp[:, t * 128 : (t + 1) * 128]
            dnorm[rows] += dot_right(dp, flat2(wc[j, :, :, : 2 * rq, :]))
            run_when(i, back_at[j])
            return carry + jnp.sum(dp.astype(F32), axis=0, keepdims=True)

        bias_grad = lax.fori_loop(0, blocks, back, jnp.zeros((1, CW), F32))
        for t in range(CW // W):
            at = plane_grad + j * CW // W + t
            small[at : at + 1] = bias_grad[:, t * W : (t + 1) * W]

    def gradients(j):
        gather_done(2 + j)

        def expand_grads(i, carry):
            res = dot_left(normed[:, rows_of(i)], side(at_slope + j * groups, every, groups)).astype(BF)
            wc[j, pl.ds(i * chips, chips), :, : 2 * rq, :] = res.reshape(chips, 2, 2 * rq, CW)
            return carry

        lax.fori_loop(0, D // BLOCK, expand_grads, 0)
        if j == C - 1:
            scatter_event(2 + j, 0)
        run_slot(grad_at[j])
        per = BLOCK // (2 * q)

        def shrink_grads(i, carry):
            left = side(at_hid + j * groups + 2 * i, every, 2)
            for t in range(p.wb):
                res = dot_left(left, g[:, t * CW : (t + 1) * CW]).astype(BF)
                cut = slice(2 * rq + t * q, 2 * rq + (t + 1) * q)
                wc[j, pl.ds(i * per, per), :, cut, :] = res.reshape(per, 2, q, CW)
            return carry

        lax.fori_loop(0, CW // BLOCK, shrink_grads, 0)
        scatter_event(2 + j if j < C - 1 else tail_group, 0)
        run_slot(grad_at[j] + 1)

    for kind, j in order:
        (forward, backward, gradients)[kind](j)
        if (kind, j) == (0, C - 1):
            res_out[...] = out[their_rows].astype(BF)
            give_out.start()
        if (kind, j) == (1, C - 1):
            give_out.wait_send()
            res_out[...] = dnorm[their_rows].astype(BF)
            give_dn.start()

    def small_gradients():
        def vector_grads(i, carry):
            rows = rows_of(i)
            z, _ = unit(rows)
            dn = dnorm[rows]
            gain = carry[0] + jnp.sum(dn * z, axis=0, keepdims=True)
            shift = carry[1] + jnp.sum(dn, axis=0, keepdims=True)
            return gain, shift, carry[2] + jnp.sum(g[rows].astype(F32), axis=0, keepdims=True)

        zero_row = jnp.zeros((1, D), F32)
        sums = lax.fori_loop(0, blocks, vector_grads, (zero_row, zero_row, zero_row))
        tail_grad = jnp.where(b == 0, sums[2], 0.0)

        def grad_block(plane, j, o):
            at = j * CW + o * 128
            row, lane = plane_grad + at // W, at % W
            v = jnp.broadcast_to(small[row : row + 1, lane : lane + 128], (8, 128))
            return jnp.where(b == plane, v, 0.0)

        for c, v in enumerate(from_plane(grad_block, 8)):
            row, lane = 16 + first_bias + c * 128 // W, c * 128 % W
            small[row : row + 1, lane : lane + 128] = v[:1]
        for at, row in ((0, sums[0]), (2, sums[1]), (last, tail_grad)):
            small[16 + at : 17 + at] = row[:, :W]
            small[17 + at : 18 + at] = row[:, W:]
        small[16 + last + 2 : 32] = jnp.zeros((14 - last, W), F32)
        ws[...] = jnp.broadcast_to(small[16:32].astype(BF)[None, None], (m, 2, 16, W))
        scatter_event(C + 2, 0)

    def finish_all():
        small_rows = p.own_rows // blocks
        give_out.wait_recv()
        give_dn.wait_recv()
        give_dn.wait_send()

        def finish_rows(i, carry):
            local = pl.ds(pl.multiple_of(i * small_rows, small_rows), small_rows)
            rows = pl.ds(pl.multiple_of(b * p.own_rows + i * small_rows, small_rows), small_rows)
            z, inverse = unit(rows)
            tail = wide(last)
            total = out[rows] + trade[0, local].astype(F32) + tail
            res_out[local] = (x[rows].astype(F32) + total).astype(BF)
            du = (dnorm[rows] + trade[1, local].astype(F32)) * wide(0)
            back = du - jnp.mean(du, axis=1, keepdims=True) - z * jnp.mean(du * z, axis=1, keepdims=True)
            sg_out[local] = g[rows].astype(F32) + inverse * back
            return carry

        lax.fori_loop(0, blocks, finish_rows, 0)

    small_hop = 0
    for k, hop in leftover:
        if k == C + 1 and hop == half + 1:
            finish_all()
        scatter_event(k, hop)
        if k == tail_group:
            if hop == 1:
                small_gradients()
            else:
                small_hop += 1
                scatter_event(C + 2, small_hop)
    scatter_event(C + 2, half + 1)

    for kind in range(2):
        for t in range(2):
            row_copy(kind, t, False).wait_send()
    swap_copy(sw_mix, 0, 2, 4).wait()
    for t in range(3):
        gmix_out[:, half_lanes(t, 1 - b)] = sw_mix[2, t * rq : (t + 1) * rq].astype(F32)

    @pl.when(moves)
    def _():
        mer_back().wait_send()
        remote(mer.at[0], mer.at[1], sw_send.at[5], sw_recv.at[5], merge_to).wait_recv()

    @pl.when(jnp.logical_not(moves))
    def _():
        mer[1] = mer[0]

    for t in range(2):
        merged_rows = mer[1, t * p.mr : (t + 1) * p.mr].astype(F32)
        gmer_out[:, t * W : (t + 1) * W] = merged_rows[: p.rr]
    for j in range(C):
        exp_back(j).wait()

    def summed_block(plane, j, o):
        rows, cols = slice(j * rq, (j + 1) * rq), slice(o * 128, (o + 1) * 128)
        return jnp.where(b == plane, keep_exp[rows, cols], sw_exp[2, rows, cols].astype(F32))

    for c, v in enumerate(from_plane(summed_block, rq)):
        gexp_out[:, c * 128 : (c + 1) * 128] = v
    swap_copy(sw_small, 0, 2, 6).wait()
    gsmall_out[...] = sw_small[0] + sw_small[2]


def core(p, stream, cotangent, lengths, mixing, merging, expand, shrink, small_own):
    n, C, D, W, CW, rq = p.n, p.C, p.D, p.W, p.CW, p.rq
    m = n // 2
    half = m // 2
    hops = 2 * half - 1
    rows = p.rows
    a_rows = 6 * rq + 16
    b_rows = 2 * p.mr
    cosine, sine = (jnp.asarray(table) for table in rope_tables(rows))
    vmem = pl.BlockSpec(memory_space=pltpu.VMEM)
    hbm = pl.BlockSpec(memory_space=pl.ANY)
    dma = pltpu.SemaphoreType.DMA
    V = pltpu.VMEM
    SD = BF if rq % 16 == 0 else F32
    scratch = [
        V((m, 2, a_rows, W), BF),
        V((m, 2, b_rows, W), BF),
        V((C, m, 2, p.c_rows, CW), BF),
        V((m, 2, 16, W), BF),
        V((rows, D), BF),
        V((rows, D), BF),
        V((rows, D), BF),
        V((max(5 * W, 2 * p.C * CW) // 128, rows, 128), BF),
        V((rows, D), F32),
        V((rows, D), F32),
        V((48, W), F32),
        V((2, p.own_rows, D), BF),
        V((m, 6 * rq, W), BF),
        V((m, b_rows, W), BF),
        V((C, m, p.c_rows, CW), BF),
        V((m, 16, W), BF),
        V((hops, 6 * rq, W), BF),
        V((hops, b_rows, W), BF),
        V((C, hops, p.c_rows, CW), BF),
        V((hops, 16, W), BF),
        dma((C + 2, 2, half + 1)),
        dma((C + 2, 2, half + 1)),
        dma((C + 2,)),
        dma((C + 2,)),
        dma((C + 4, 2, half + 1)),
        dma((C + 4, 2, half + 1)),
        dma((C + 4,)),
        dma((C + 4,)),
        dma((6,)),
        dma((6,)),
        dma((7 + p.FF // D,)),
        V((3, 3 * rq, W), SD),
        V((3, C * rq, CW), SD),
        V((3, 16, W), F32),
        V((2, b_rows, W), BF),
        V((C * rq, CW), F32),
        dma((7 + C,)),
        dma((7 + C,)),
        dma((2, 2, half + 1)),
        dma((2, 2, half + 1)),
    ]
    shapes = (
        jax.ShapeDtypeStruct((p.own_rows, D), BF),
        jax.ShapeDtypeStruct((p.own_rows, D), F32),
        jax.ShapeDtypeStruct((rq, 3 * D), F32),
        jax.ShapeDtypeStruct((p.rr, D), F32),
        jax.ShapeDtypeStruct((rq, p.FF), F32),
        jax.ShapeDtypeStruct((p.hb, D), F32),
        jax.ShapeDtypeStruct((16, W), F32),
    )
    flops = 2 * rows * D * (6 * p.FF // 2 + 9 * W + 3 * W) + 12 * rows * rows * W
    return pl.pallas_call(
        functools.partial(block_kernel, p),
        out_shape=shapes,
        in_specs=[hbm] * 6 + [vmem, pl.BlockSpec(memory_space=pltpu.SMEM), vmem, vmem],
        out_specs=tuple(vmem for _ in shapes),
        scratch_shapes=scratch,
        compiler_params=pltpu.CompilerParams(
            collective_id=0, has_side_effects=True, vmem_limit_bytes=63 * 1024 * 1024
        ),
        cost_estimate=pl.CostEstimate(flops=flops, bytes_accessed=8 << 20, transcendentals=0),
    )(stream, cotangent, mixing, merging, expand, shrink, small_own, lengths, cosine, sine)


def local(n, stream, cotangent, lengths, steps_taken, learning_rates, *params):
    masters, momenta, variances = params[:6], params[6:12], params[12:]
    p = Plan(n, stream, *masters)
    linear = lax.axis_index("dp") * 2 + lax.axis_index("branch")
    vectors, offsets = masters[4], masters[5]
    small = jnp.zeros((16 * p.W,), F32)
    for row in range(2):
        small = lax.dynamic_update_slice(small, vectors[row], (row * p.D + linear * p.vc,))
    small = lax.dynamic_update_slice(small, offsets, (2 * p.D + linear * p.ow,))
    residual, stream_grad, *grads, small = core(
        p, stream, cotangent, lengths, *masters[:4], small.reshape(16, p.W)
    )
    small = small.reshape(-1)
    rows = [
        lax.dynamic_slice(small, (row * p.D + linear * p.vc,), (p.vc,)) for row in range(2)
    ]
    grads.append(jnp.stack(rows))
    grads.append(lax.dynamic_slice(small, (2 * p.D + linear * p.ow,), (p.ow,)))
    count = steps_taken[0].astype(F32)
    outs = [residual, stream_grad]
    for k in range(6):
        decay = decay_rate if k < 4 else 0.0
        outs.extend(
            adam_update(
                masters[k], grads[k], momenta[k], variances[k], learning_rates[k], count, decay
            )
        )
    return tuple(outs)


def solution(mesh):
    rows = P(("dp", "branch"), None)
    cols = P(None, ("dp", "branch"))
    flat = P(("dp", "branch"))
    six = (rows, rows, rows, rows, cols, flat)
    return jax.shard_map(
        functools.partial(local, mesh.shape["dp"]),
        mesh=mesh,
        in_specs=(rows, rows, P("dp"), P(), P()) + six * 3,
        out_specs=(rows, rows) + sum(((s,) * 4 for s in six), ()),
        check_vma=False,
    )
```

```python
import functools

import jax
import jax.numpy as jnp
import numpy as np
from jax import lax
from jax.experimental import pallas as pl
from jax.experimental.pallas import tpu as pltpu
from jax.sharding import PartitionSpec as P

HEAD = 64
ROT = 32
beta_one = 0.9
beta_two = 0.95
adam_eps = 1e-08
decay_rate = 0.1
norm_eps = 1e-05
rope_base = 10000.0
masked_score = -1e30
BF = jnp.bfloat16
F32 = jnp.float32


def dot(left, right):
    return jnp.dot(left, right, preferred_element_type=F32)


def dot_left(left, right):
    return lax.dot_general(left, right, (((0,), (0,)), ((), ())), preferred_element_type=F32)


def dot_right(left, right):
    return lax.dot_general(left, right, (((1,), (1,)), ((), ())), preferred_element_type=F32)


def rope_tables(length):
    places = np.arange(length, dtype=np.float32)[:, None]
    column = np.arange(2 * HEAD) % HEAD
    paired = (column // 2).astype(np.float32)
    frequency = np.exp(paired * np.float32(-2.0 / ROT) * np.log(np.float32(rope_base)))
    angles = (places * frequency[None, :].astype(np.float32)).astype(np.float64)
    inside = (column < ROT)[None, :]
    signed = np.where(column % 2 == 0, -1.0, 1.0)[None, :]
    cosine = np.where(inside, np.cos(angles), 1.0).astype(np.float32)
    sine = np.where(inside, np.sin(angles) * signed, 0.0).astype(np.float32)
    return cosine, sine


def adam_update(master, gradient, momentum, variance, rate, count, decay):
    drift = beta_one * momentum + (1.0 - beta_one) * gradient
    power = beta_two * variance + (1.0 - beta_two) * gradient * gradient
    first_fix = 1.0 - jnp.power(beta_one, count)
    second_fix = 1.0 - jnp.power(beta_two, count)
    moved = drift / first_fix / (jnp.sqrt(power / second_fix) + adam_eps)
    updated = master - rate * (moved + decay * master)
    return (updated, updated.astype(BF), drift, power)


class Plan:
    def __init__(self, n, stream, mixing, merging, expand, shrink, vectors, offsets):
        self.n = n
        self.own_rows, self.D = stream.shape
        self.rows = 2 * self.own_rows
        self.W = self.D // 2
        self.FF = expand.shape[1]
        self.rq = mixing.shape[0]
        self.rr = merging.shape[0]
        self.mr = max(16, self.rr)
        self.hb = shrink.shape[0]
        self.C = 4 if self.hb >= 64 else 2
        self.q = self.hb // self.C
        self.CW = self.FF // 2 // self.C
        self.wb = self.D // self.CW
        self.vc = vectors.shape[1]
        self.ow = offsets.shape[0]
        self.o_merge = 6 * self.rq
        self.o_small = self.o_merge + 2 * self.mr
        self.g_rows = self.o_small + 16
        self.c_rows = 2 * self.rq + self.wb * self.q


MESH = pl.DeviceIdType.MESH
BLOCK = 256
ATTEND_SHARE = 14
LATE = 1
AB_START = 1.0
AB_STEP = 3.5
C_START = 0.5
C_STEP = 2.5


def turned(a, cosine, sine, back):
    lanes = a.shape[1]
    even = lax.broadcasted_iota(jnp.int32, a.shape, 1) % 2 == 0
    t = a * sine if back else a
    swapped = jnp.where(even, pltpu.roll(t, lanes - 1, 1), pltpu.roll(t, 1, 1))
    return a * cosine + (swapped if back else swapped * sine)


def tile_lanes(a, times):
    return jnp.concatenate([a] * times, axis=1) if times > 1 else a


def flat2(a):
    return a.reshape(-1, a.shape[-1])


def gelu_parts(pre):
    root = 0.7978845608028654
    square = pre * pre
    t = jnp.tanh(root * pre * (1.0 + 0.044715 * square))
    hidden = 0.5 * pre * (1.0 + t)
    slope = 0.5 * (1.0 + t) + 0.5 * pre * (1.0 - t * t) * root * (1.0 + 0.134145 * square)
    return hidden, slope


def block_kernel(
    p,
    stream,
    cotangent,
    mixing,
    merging,
    expand,
    shrink,
    small_own,
    length,
    cos_ref,
    sin_ref,
    res_out,
    sg_out,
    gmix_out,
    gmer_out,
    gexp_out,
    gshr_out,
    gsmall_out,
    wa,
    wb,
    wc,
    ws,
    x,
    g,
    normed,
    lanes,
    out,
    dnorm,
    small,
    trade,
    sib_a,
    sib_b,
    sib_c,
    sib_s,
    slot_a,
    slot_b,
    slot_c,
    slot_s,
    ag_send,
    ag_recv,
    as_send,
    as_recv,
    rs_send,
    rs_recv,
    ss_send,
    ss_recv,
    x_send,
    x_recv,
    own_sem,
    sw_mix,
    sw_exp,
    sw_small,
    mer,
    keep_exp,
    sw_send,
    sw_recv,
    sh_send,
    sh_recv,
):
    n, C, D, W, CW, rq, q = p.n, p.C, p.D, p.W, p.CW, p.rq, p.q
    SD = BF if rq % 16 == 0 else F32
    m = n // 2
    half = m // 2
    blocks = p.rows // BLOCK
    pairs = W // 128
    groups = CW // 128
    at_q, at_k, at_v, at_att, at_da = (t * pairs for t in range(5))
    at_hid, at_slope = 0, C * groups
    d = lax.axis_index("dp")
    b = lax.axis_index("branch")
    core = lax.rem(d, 2)
    chip = d // 2
    ring = jnp.where(lax.rem(chip, 2) == 0, chip // 2, m - 1 - chip // 2)
    step = 1 - 2 * core

    def around(k):
        pos = lax.rem(ring + step * k + m, m)
        return jnp.where(pos < half, 2 * pos, 2 * (m - 1 - pos) + 1)

    ahead = (2 * around(1) + core, b)
    behind = (2 * around(-1) + core, b)
    sibling = (d + step, b)
    partner = (d, 1 - b)
    ways = (ahead, behind)

    sources = [(mixing, t * D, t * rq, rq) for t in range(3)]
    sources += [(expand, t * D, (3 + t) * rq, rq) for t in range(p.FF // D)]
    sources += [(merging, 0, 7 * rq, p.rr), (shrink, 0, 8 * rq, p.hb)]
    loads = [
        pltpu.make_async_copy(
            ref.at[:, pl.ds(column, D)], dnorm.at[pl.ds(row, count)], own_sem.at[2 + t]
        )
        for t, (ref, column, row, count) in enumerate(sources)
    ]
    for load in loads:
        load.start()
    barrier = pltpu.get_barrier_semaphore()
    for other in (ahead, behind, sibling, partner):
        pl.semaphore_signal(barrier, inc=1, device_id=other, device_id_type=MESH)
    rank, origin = 2 * d + b, n * b + d
    merge_to = (lax.rem(rank, n), rank // n)
    merge_from = (origin // 2, lax.rem(origin, 2))
    moves = d != b * (n - 1)

    @pl.when(moves)
    def _():
        for other in (merge_to, merge_from):
            pl.semaphore_signal(barrier, inc=1, device_id=other, device_id_type=MESH)
        pl.semaphore_wait(barrier, 6)

    @pl.when(jnp.logical_not(moves))
    def _():
        pl.semaphore_wait(barrier, 4)


    def remote(src, dst, send, recv, to):
        return pltpu.make_async_remote_copy(
            src_ref=src, dst_ref=dst, send_sem=send, recv_sem=recv, device_id=to, device_id_type=MESH
        )

    own_rows = pl.ds(pl.multiple_of(b * p.own_rows, p.own_rows), p.own_rows)
    their_rows = pl.ds(pl.multiple_of((1 - b) * p.own_rows, p.own_rows), p.own_rows)

    def gather_ref(k):
        return wa if k == 0 else wb if k == 1 else wc.at[k - 2]

    def last_hop(way):
        return half - way

    def gather_copy(k, way, hop):
        shard = gather_ref(k).at[around((1 - hop) * (1 - 2 * way)), core]
        return remote(shard, shard, ag_send.at[k, way, hop], ag_recv.at[k, way, hop], ways[way])

    def gather_arrival(k, way, hop):
        shard = gather_ref(k).at[around(-hop * (1 - 2 * way)), core]
        return remote(shard, shard, ag_send.at[k, way, hop], ag_recv.at[k, way, hop], ways[way])

    def gather_sibling(k, whose):
        part = gather_ref(k).at[:, whose]
        return remote(part, part, as_send.at[k], as_recv.at[k], sibling)

    def gather_share(k, way, hop, arriving):
        shift = -hop * (1 - 2 * way)
        shard = gather_ref(k)
        shard = shard.at[around(-shift), 1 - core] if arriving else shard.at[around(shift), core]
        return remote(shard, shard, sh_send.at[k, way, hop], sh_recv.at[k, way, hop], sibling)

    def shares():
        hops = [(way, hop) for way in range(2) for hop in range(1, last_hop(way) + 1)]
        return [(0, 0)] + hops

    def gather_start(k):
        for way in range(2):
            gather_copy(k, way, 1).start()
        if k < 2:
            gather_share(k, 0, 0, False).start()

    def gather_event(k, hop):
        for way in range(2):
            if hop <= last_hop(way):
                gather_arrival(k, way, hop).wait_recv()
                if hop < last_hop(way):
                    gather_copy(k, way, hop + 1).start()
                if k < 2:
                    gather_share(k, way, hop, False).start()
        if hop == half and k >= 2:
            gather_sibling(k, core).start()

    def gather_ready(k):
        if k >= 2:
            gather_sibling(k, 1 - core).wait_recv()
            return
        for way, hop in shares():
            gather_share(k, way, hop, True).wait_recv()

    def gather_done(k):
        for way in range(2):
            for hop in range(1, last_hop(way) + 1):
                gather_copy(k, way, hop).wait_send()
        if k >= 2:
            gather_sibling(k, core).wait_send()
            return
        for way, hop in shares():
            gather_share(k, way, hop, False).wait_send()

    tail_group = C + 3

    def scatter_refs(k):
        if k == 0:
            return wa, sib_a, slot_a, 0, 6 * rq
        if k == 1:
            return wb, sib_b, slot_b, 0, 2 * p.mr
        if k == C + 2:
            return ws, sib_s, slot_s, 0, 16
        j = C - 1 if k == tail_group else k - 2
        first, count = (0, p.c_rows) if j < C - 1 else (0, 2 * rq)
        if k == tail_group:
            first, count = 2 * rq, p.c_rows - 2 * rq
        cut = pl.ds(first, count)
        return wc.at[j], sib_c.at[j, :, cut], slot_c.at[j, :, cut], first, count

    def swap_copy(ref, src, dst, sem):
        return remote(ref.at[src], ref.at[dst], sw_send.at[sem], sw_recv.at[sem], partner)

    def exp_back(j):
        cut = pl.ds(j * rq, rq)
        return remote(
            sw_exp.at[0, cut], sw_exp.at[2, cut], sw_send.at[7 + j], sw_recv.at[7 + j], partner
        )

    def mer_back():
        return remote(mer.at[0], mer.at[1], sw_send.at[5], sw_recv.at[5], merge_from)

    def pair(upper, lower):
        return jnp.where(b == 0, upper, lower), jnp.where(b == 0, lower, upper)

    def half_lanes(t, which):
        return pl.ds(pl.multiple_of(t * D + which * W, W), W)

    def shrink_result(j, total):
        for t in range(p.wb):
            part = total[t * q : (t + 1) * q]
            gshr_out[j * q : (j + 1) * q, t * CW : (t + 1) * CW] = part

    def scatter_result(k, total):
        if k == 0:
            for t in range(3):
                upper = total[2 * t * rq : (2 * t + 1) * rq]
                keep, give = pair(upper, total[(2 * t + 1) * rq : (2 * t + 2) * rq])
                gmix_out[:, half_lanes(t, b)] = keep
                sw_mix[0, t * rq : (t + 1) * rq] = give.astype(SD)
            swap_copy(sw_mix, 0, 2, 4).start()
        elif k == 1:
            mer[0] = total.astype(BF)

            @pl.when(moves)
            def _():
                mer_back().start()

        elif k < C + 2:
            j = k - 2
            keep, give = pair(total[:rq], total[rq : 2 * rq])
            keep_exp[j * rq : (j + 1) * rq] = keep
            sw_exp[0, j * rq : (j + 1) * rq] = give.astype(SD)
            exp_back(j).start()
            if j < C - 1:
                shrink_result(j, total[2 * rq :])
        elif k == tail_group:
            shrink_result(C - 1, total)
        else:
            sw_small[0] = total
            swap_copy(sw_small, 0, 2, 6).start()

    def scatter_sibling(k):
        whole, sib, _, first, rows = scatter_refs(k)
        src = whole.at[:, 1 - core, pl.ds(first, rows)]
        return remote(src, sib, ss_send.at[k], ss_recv.at[k], sibling)

    def slot_of(way, hop):
        return (hop - 1) if way == 0 else half + hop - 1

    def scatter_copy(k, way, hop):
        whole, _, slots, first, rows = scatter_refs(k)
        target = around((last_hop(way) + 1 - hop) * (1 - 2 * way))
        src = whole.at[target, core, pl.ds(first, rows)]
        return remote(
            src, slots.at[slot_of(way, hop)], rs_send.at[k, way, hop], rs_recv.at[k, way, hop], ways[way]
        )

    def scatter_event(k, hop):
        whole, sib, slots, first, rows = scatter_refs(k)
        if hop == 0:
            scatter_sibling(k).start()
            return
        if hop == 1:
            scatter_sibling(k).wait_recv()
        for way in range(2):
            if hop <= last_hop(way):
                target = around((last_hop(way) + 1 - hop) * (1 - 2 * way))
                here = whole.at[target, core, pl.ds(first, rows)]
                total = here[...].astype(F32) + sib[target].astype(F32)
                if hop > 1:
                    scatter_copy(k, way, hop - 1).wait_recv()
                    total = total + slots[slot_of(way, hop - 1)].astype(F32)
                here[...] = total.astype(BF)
                scatter_copy(k, way, hop).start()
        if hop == half + 1:
            total = whole[chip, core, pl.ds(first, rows)].astype(F32) + sib[chip].astype(F32)
            for way in range(2):
                scatter_copy(k, way, last_hop(way)).wait_recv()
                total = total + slots[slot_of(way, last_hop(way))].astype(F32)
            scatter_result(k, total)
            for way in range(2):
                for sent in range(1, last_hop(way) + 1):
                    scatter_copy(k, way, sent).wait_send()
            scatter_sibling(k).wait_send()

    piece = p.own_rows // 2

    def quarter(whose, t):
        return pl.ds(pl.multiple_of(whose * p.own_rows + t * piece, piece), piece)

    def row_copy(kind, t, receiving):
        src, dst = ((stream, x), (cotangent, g))[kind]
        sem = 2 * kind + t
        there = dst.at[quarter(1 - b if receiving else b, t)]
        return remote(src.at[pl.ds(t * piece, piece)], there, x_send.at[sem], x_recv.at[sem], partner)

    keep_x = pltpu.make_async_copy(stream, x.at[own_rows], own_sem.at[0])
    keep_g = pltpu.make_async_copy(cotangent, g.at[own_rows], own_sem.at[1])

    for t in range(3):
        loads[t].wait()
    kept_mix = []
    for t in range(3):
        v = dnorm[t * rq : (t + 1) * rq]
        keep, give = pair(v[:, :W], v[:, W:])
        kept_mix.append(keep)
        sw_mix[0, t * rq : (t + 1) * rq] = give.astype(SD)
    swap_copy(sw_mix, 0, 1, 0).start()
    sw_small[0] = small_own[...]
    swap_copy(sw_small, 0, 1, 1).start()
    for load in loads[3:]:
        load.wait()
    mer[0] = jnp.zeros((2 * p.mr, W), BF)
    own_merge = dnorm[7 * rq : 7 * rq + p.rr].astype(BF)
    for t in range(2):
        mer[0, t * p.mr : t * p.mr + p.rr] = own_merge[:, t * W : (t + 1) * W]
    mer_there = (merge_to[0] // 2, lax.rem(merge_to[0], 2))

    def mer_copy(slot):
        return remote(mer.at[0], wb.at[slot], sw_send.at[3], sw_recv.at[3], merge_to)

    @pl.when(moves)
    def _():
        mer_copy(mer_there).start()

    @pl.when(jnp.logical_not(moves))
    def _():
        wb[chip, core] = mer[0]

    swap_copy(sw_mix, 0, 1, 0).wait_recv()
    row_copy(0, 0, False).start()
    swap_copy(sw_small, 0, 1, 1).wait_recv()
    for t in range(3):
        got = sw_mix[1, t * rq : (t + 1) * rq].astype(F32)
        both_halves = jnp.concatenate(pair(kept_mix[t], got), axis=0).astype(BF)
        wa[chip, core, 2 * t * rq : 2 * (t + 1) * rq] = both_halves
    wa[chip, core, 6 * rq : 6 * rq + 16] = (sw_small[0] + sw_small[1]).astype(BF)
    gather_start(0)
    per_lane = 128 // q

    def pieces(fetch, width):
        spot = lax.broadcasted_iota(jnp.int32, (width, 128), 1) // q
        result = None
        for e in range(per_lane):
            block, at = fetch(e)
            shift = (e * q - at) % 128
            block = pltpu.roll(block, shift, 1) if shift else block
            result = block if e == 0 else jnp.where(spot == e, block, result)
        return result

    def to_plane(block_at, width, j, plane):
        def column(o):
            def fetch(e):
                start = (2 * (o * per_lane + e) + plane) * p.hb + j * q
                return block_at(start // 128), start % 128

            return pieces(fetch, width)

        return jnp.concatenate([column(o) for o in range(groups)], axis=1)

    def from_plane(block_at, width):
        def column(c):
            def fetch(e):
                start = c * 128 + e * q
                unit_block = start // p.hb
                lane = (unit_block // 2) * q
                block = block_at(unit_block % 2, (start % p.hb) // q, lane // 128)
                return block, lane % 128

            return pieces(fetch, width)

        return [column(c) for c in range(p.FF // 128)]

    wide_blocks = D // 128

    def expand_block(c):
        at = (3 + c // wide_blocks) * rq
        lane = (c % wide_blocks) * 128
        return dnorm[at : at + rq, lane : lane + 128]

    for j in range(C):
        keep, give = pair(to_plane(expand_block, rq, j, 0), to_plane(expand_block, rq, j, 1))
        keep_exp[j * rq : (j + 1) * rq] = keep
        sw_exp[0, j * rq : (j + 1) * rq] = give.astype(SD)
    swap_copy(sw_exp, 0, 1, 2).start()

    @pl.when(b == 0)
    def _():
        row_copy(0, 1, False).start()
        row_copy(1, 0, False).start()

    @pl.when(b == 1)
    def _():
        row_copy(1, 0, False).start()
        row_copy(0, 1, False).start()

    row_copy(1, 1, False).start()
    keep_x.start()
    keep_g.start()
    for j in range(C):
        for t in range(p.wb):
            at = 8 * rq + j * q
            piece_rows = dnorm[at : at + q, t * CW : (t + 1) * CW].astype(BF)
            wc[j, chip, core, 2 * rq + t * q : 2 * rq + (t + 1) * q] = piece_rows
    def chunk_shards():
        swap_copy(sw_exp, 0, 1, 2).wait_recv()
        for j in range(C):
            got = sw_exp[1, j * rq : (j + 1) * rq].astype(F32)
            both_halves = jnp.concatenate(pair(keep_exp[j * rq : (j + 1) * rq], got), axis=0)
            wc[j, chip, core, : 2 * rq] = both_halves.astype(BF)

    out[...] = jnp.zeros((p.rows, D), F32)
    for hop in range(1, half + 1):
        gather_event(0, hop)
        if hop == 1:

            @pl.when(moves)
            def _():
                mer_copy((chip, core)).wait_recv()

            gather_start(1)
        else:
            gather_event(1, hop - 1)
        if hop == half - 1:
            chunk_shards()
            gather_start(2)
    gather_event(1, half)
    for j in range(1, C):
        gather_start(2 + j)
    swap_copy(sw_mix, 0, 1, 0).wait_send()
    swap_copy(sw_small, 0, 1, 1).wait_send()
    swap_copy(sw_exp, 0, 1, 2).wait_send()

    @pl.when(moves)
    def _():
        mer_copy(mer_there).wait_send()


    def weight(t):
        return flat2(wa[:, :, t * 2 * rq : (t + 1) * 2 * rq, :])

    def merge_weight(t):
        whole = wb[:, :, t * p.mr : (t + 1) * p.mr, :]
        if p.mr == p.rr:
            return flat2(whole)
        whole = whole.astype(F32).reshape(n, p.mr, W)[:, : p.rr]
        return whole.reshape(W, W).astype(BF)

    def wide(row):
        return jnp.concatenate([small[row : row + 1], small[row + 1 : row + 2]], axis=1)

    def unit(rows):
        v = x[rows].astype(F32)
        centred = v - jnp.mean(v, axis=1, keepdims=True)
        inverse = lax.rsqrt(jnp.mean(centred * centred, axis=1, keepdims=True) + norm_eps)
        return centred * inverse, inverse

    def rows_of(i):
        return pl.ds(pl.multiple_of(i * BLOCK, BLOCK), BLOCK)

    def project(i):
        rows = rows_of(i)
        z, _ = unit(rows)
        nb = (z * wide(0) + wide(2)).astype(BF)
        normed[rows] = nb
        cosine = tile_lanes(cos_ref[rows], pairs)
        sine = tile_lanes(sin_ref[rows], pairs)
        query = (turned(dot(nb, weight(0)), cosine, sine, False) * HEAD**-0.5).astype(BF)
        key = turned(dot(nb, weight(1)), cosine, sine, False).astype(BF)
        value = dot(nb, weight(2)).astype(BF)
        for t in range(pairs):
            cut = slice(t * 128, (t + 1) * 128)
            lanes[at_q + t, rows] = query[:, cut]
            lanes[at_k + t, rows] = key[:, cut]
            lanes[at_v + t, rows] = value[:, cut]

    def gradient(i):
        rows = rows_of(i)
        position = lax.broadcasted_iota(jnp.int32, (BLOCK, D), 0) + i * BLOCK
        gb = jnp.where(position < length[0], g[rows].astype(F32), 0.0).astype(BF)
        g[rows] = gb
        da = (dot_right(gb[:, :W], merge_weight(0)) + dot_right(gb[:, W:], merge_weight(1))).astype(BF)
        for t in range(pairs):
            lanes[at_da + t, rows] = da[:, t * 128 : (t + 1) * 128]

    def each(body, start, count):
        def run(i, carry):
            body(start + i)
            return carry

        lax.fori_loop(0, count, run, 0)

    keep_x.wait()
    keep_g.wait()
    gather_ready(0)
    small[:16] = jnp.sum(wa[:, :, 6 * rq :, :].reshape(n, 16, W).astype(F32), axis=0)
    first_bias, plane_bias, plane_grad = 2 * D // W, 32, 40

    def bias_block(c):
        row, lane = first_bias + c * 128 // W, c * 128 % W
        return jnp.broadcast_to(small[row : row + 1, lane : lane + 128], (8, 128))

    for j in range(C):
        mine, _ = pair(to_plane(bias_block, 8, j, 0), to_plane(bias_block, 8, j, 1))
        for t in range(CW // W):
            row = plane_bias + j * CW // W + t
            small[row : row + 1] = mine[:1, t * W : (t + 1) * W]
    part = blocks // 2
    each(project, b * part, part)
    gather_ready(1)
    each(gradient, b * part, part)

    @pl.when(b == 1)
    def _():
        row_copy(0, 0, True).wait_recv()
        row_copy(0, 1, True).wait_recv()
        each(project, 0, part)

    def spread(items, count, first=0):
        return [items[len(items) * t // count : len(items) * (t + 1) // count] for t in range(count)]

    events = []
    for hop in range(1, half + 1):
        events += [(2 + j, hop) for j in range(C)]
    attend_slots = spread(events[: len(events) * ATTEND_SHARE // 16], blocks * pairs)
    merge_events = events[len(events) * ATTEND_SHARE // 16 :]

    def attend(i, t):
        lane = lax.broadcasted_iota(jnp.int32, (BLOCK, 128), 1)
        rows = slice(i * BLOCK, (i + 1) * BLOCK)
        width = (i + 1) * BLOCK
        qb, dab = lanes[at_q + t, rows], lanes[at_da + t, rows]
        keys, values = lanes[at_k + t, :width], lanes[at_v + t, :width]
        zero = jnp.zeros_like(qb)
        first = lane < HEAD
        qm = jnp.concatenate([jnp.where(first, qb, zero), jnp.where(first, zero, qb)], axis=0)
        dm = jnp.concatenate([jnp.where(first, dab, zero), jnp.where(first, zero, dab)], axis=0)
        scores = dot_right(qm, keys)
        down = lax.rem(lax.broadcasted_iota(jnp.int32, (2 * BLOCK, BLOCK), 0), BLOCK)
        over = lax.broadcasted_iota(jnp.int32, (2 * BLOCK, BLOCK), 1)
        edge = jnp.where(down >= over, scores[:, width - BLOCK :], masked_score)
        scores = jnp.concatenate([scores[:, : width - BLOCK], edge], axis=1) if i else edge
        weights = jnp.exp(scores - jnp.max(scores, axis=1, keepdims=True))
        weights = weights * (1.0 / jnp.sum(weights, axis=1, keepdims=True))
        rounded = weights.astype(BF)
        dweights = dot_right(dm, values)
        delta = jnp.sum(weights * dweights, axis=1, keepdims=True)
        dscores = (weights * (dweights - delta)).astype(BF)
        mixed = dot(rounded, values)
        dquery = dot(dscores, keys)
        dvalue = dot_left(rounded, dm)
        dkey = dot_left(dscores, qm)
        position = lax.broadcasted_iota(jnp.int32, (BLOCK, 128), 0) + i * BLOCK
        whole = jnp.where(first, mixed[:BLOCK], mixed[BLOCK:])
        lanes[at_att + t, rows] = jnp.where(position < length[0], whole, 0.0).astype(BF)
        dq = jnp.where(first, dquery[:BLOCK], dquery[BLOCK:]) * HEAD**-0.5
        lanes[at_q + t, rows] = turned(dq, cos_ref[rows], sin_ref[rows], True).astype(BF)
        out[:width, head_lanes(t, 0)] += dkey
        out[:width, head_lanes(t, 1)] += dvalue

    def head_lanes(t, which):
        return pl.ds(pl.multiple_of(which * W + t * 128, 128), 128)

    def attention(it, carry):
        stage, t = it // pairs, lax.rem(it, pairs)
        now = lax.rem(stage + b * part, blocks)

        @pl.when((t == 0) & (b == 0) & (stage >= part))
        def _():
            for u in range(2):

                @pl.when(stage == part + u * (part // 2))
                def _(u=u):
                    row_copy(0, u, True).wait_recv()
                    row_copy(1, u, True).wait_recv()
                    each(project, part + u * (part // 2), part // 2)
                    each(gradient, part + u * (part // 2), part // 2)

        @pl.when((t == 0) & (b == 1) & (stage == part))
        def _():
            row_copy(1, 0, True).wait_recv()
            row_copy(1, 1, True).wait_recv()
            each(gradient, 0, part)

        for i in range(blocks):

            @pl.when(now == i)
            def _(i=i):
                attend(i, t)

        @pl.when(stage == blocks - 1)
        def _():
            dk = out[:, head_lanes(t, 0)]
            lanes[at_k + t] = turned(dk, cos_ref[...], sin_ref[...], True).astype(BF)
            lanes[at_v + t] = out[:, head_lanes(t, 1)].astype(BF)

        for slot, todo in enumerate(attend_slots):
            if todo:

                @pl.when(it == slot)
                def _(todo=todo):
                    for k, hop in todo:
                        gather_event(k, hop)

        return carry

    lax.fori_loop(0, blocks * pairs, attention, 0)

    def side(at, rows, count=pairs):
        return jnp.concatenate([lanes[at + t, rows] for t in range(count)], axis=1)

    def merge(i, carry):
        rows = rows_of(i)
        total = dot_right(side(at_q, rows), weight(0))
        total = total + dot_right(side(at_k, rows), weight(1))
        dnorm[rows] = total + dot_right(side(at_v, rows), weight(2))
        return carry

    lax.fori_loop(0, blocks, merge, 0)
    for k, hop in merge_events[: len(merge_events) // 2]:
        gather_event(k, hop)
    gather_done(0)
    every = slice(0, p.rows)
    chips = BLOCK // (4 * rq)

    def mix_grads(i, carry):
        left = normed[:, rows_of(i)]
        where = pl.ds(i * chips, chips)
        for t in range(3):
            res = dot_left(left, side(t * pairs, every)).astype(BF)
            wa[where, :, t * 2 * rq : (t + 1) * 2 * rq, :] = res.reshape(chips, 2, 2 * rq, W)
        return carry

    lax.fori_loop(0, D // BLOCK, mix_grads, 0)
    scatter_event(0, 0)
    for k, hop in merge_events[len(merge_events) // 2 :]:
        gather_event(k, hop)

    def attend_out(i, carry):
        rows = rows_of(i)
        ab = side(at_att, rows)
        out[rows, :W] = dot(ab, merge_weight(0))
        out[rows, W:] = dot(ab, merge_weight(1))
        return carry

    lax.fori_loop(0, blocks, attend_out, 0)
    gather_done(1)
    merged = BLOCK // (2 * p.rr)
    for i in range(W // BLOCK):
        left = side(at_att + 2 * i, every, 2)
        for t in range(2):
            res = dot_left(left, g[:, t * W : (t + 1) * W]).reshape(merged, 2, p.rr, W)
            if p.mr != p.rr:
                res = jnp.concatenate([res, jnp.zeros((merged, 2, p.mr - p.rr, W), F32)], axis=2)
            wb[i * merged : (i + 1) * merged, :, t * p.mr : (t + 1) * p.mr, :] = res.astype(BF)
    scatter_event(1, 0)

    order = [(0, j) for j in range(C)]
    for j in range(C):
        if j < C - LATE:
            order += [(1, j), (2, j)]
    order += [(1, j) for j in range(C - LATE, C)] + [(2, j) for j in range(C - LATE, C)]
    fore_at, back_at, grad_at = ({}, {}, {})
    total_slots = 0
    for kind, j in order:
        (fore_at, back_at, grad_at)[kind][j] = total_slots
        total_slots += 2 if kind == 2 else blocks // 2
    timed = []
    pace = 4.0 / half
    for hop in range(1, half + 2):
        timed += [(AB_START + (hop - 1) * AB_STEP * pace, k, hop) for k in range(2)]
        for j in range(C):
            begin = grad_at[j] + 2 + C_START
            timed.append((begin + (hop - 1) * C_STEP * pace, 2 + j, hop))
        timed.append((begin + 0.5 + (hop - 1) * C_STEP * pace, tail_group, hop))
    timed.sort()
    slots = [[e[1:] for e in timed if t <= e[0] < t + 1] for t in range(total_slots)]
    leftover = [e[1:] for e in timed if e[0] >= total_slots]

    def run_slot(slot):
        for k, hop in slots[slot]:
            scatter_event(k, hop)

    def run_when(i, start, count):
        for i0 in range(count):
            if slots[start + i0]:

                @pl.when(i == i0)
                def _(i0=i0):
                    run_slot(start + i0)

    def hidden_bias(j):
        at = plane_bias + j * CW // W
        return jnp.concatenate([small[at + t : at + t + 1] for t in range(CW // W)], axis=1)

    def shrink_weight(j, t):
        return flat2(wc[j, :, :, 2 * rq + t * q : 2 * rq + (t + 1) * q, :])

    last = (2 * D + p.FF) // W
    give_out = remote(res_out, trade.at[0], x_send.at[4], x_recv.at[4], partner)
    give_dn = remote(res_out, trade.at[1], x_send.at[5], x_recv.at[5], partner)

    def forward(j):
        gather_ready(2 + j)

        def feed(i, carry):
            rows = pl.ds(pl.multiple_of(i * 2 * BLOCK, 2 * BLOCK), 2 * BLOCK)
            pre = dot(normed[rows], flat2(wc[j, :, :, : 2 * rq, :])) + hidden_bias(j)
            hid, slope = gelu_parts(pre)
            hid, slope = hid.astype(BF), slope.astype(BF)
            for t in range(groups):
                lanes[at_hid + j * groups + t, rows] = hid[:, t * 128 : (t + 1) * 128]
                lanes[at_slope + j * groups + t, rows] = slope[:, t * 128 : (t + 1) * 128]
            for t in range(p.wb):
                out[rows, t * CW : (t + 1) * CW] += dot(hid, shrink_weight(j, t))
            run_when(i, fore_at[j], blocks // 2)
            return carry

        lax.fori_loop(0, blocks // 2, feed, 0)

    def backward(j):

        def back(i, carry):
            rows = pl.ds(pl.multiple_of(i * 2 * BLOCK, 2 * BLOCK), 2 * BLOCK)
            gb = g[rows]
            dhid = dot_right(gb[:, :CW], shrink_weight(j, 0))
            for t in range(1, p.wb):
                dhid = dhid + dot_right(gb[:, t * CW : (t + 1) * CW], shrink_weight(j, t))
            dp = (dhid * side(at_slope + j * groups, rows, groups).astype(F32)).astype(BF)
            for t in range(groups):
                lanes[at_slope + j * groups + t, rows] = dp[:, t * 128 : (t + 1) * 128]
            dnorm[rows] += dot_right(dp, flat2(wc[j, :, :, : 2 * rq, :]))
            run_when(i, back_at[j], blocks // 2)
            return carry + jnp.sum(dp.astype(F32), axis=0, keepdims=True)

        bias_grad = lax.fori_loop(0, blocks // 2, back, jnp.zeros((1, CW), F32))
        for t in range(CW // W):
            at = plane_grad + j * CW // W + t
            small[at : at + 1] = bias_grad[:, t * W : (t + 1) * W]

    def gradients(j):
        gather_done(2 + j)

        def expand_grads(i, carry):
            res = dot_left(normed[:, rows_of(i)], side(at_slope + j * groups, every, groups)).astype(BF)
            wc[j, pl.ds(i * chips, chips), :, : 2 * rq, :] = res.reshape(chips, 2, 2 * rq, CW)
            return carry

        lax.fori_loop(0, D // BLOCK, expand_grads, 0)
        if j == C - 1:
            scatter_event(2 + j, 0)
        run_slot(grad_at[j])
        per = BLOCK // (2 * q)

        def shrink_grads(i, carry):
            left = side(at_hid + j * groups + 2 * i, every, 2)
            for t in range(p.wb):
                res = dot_left(left, g[:, t * CW : (t + 1) * CW]).astype(BF)
                cut = slice(2 * rq + t * q, 2 * rq + (t + 1) * q)
                wc[j, pl.ds(i * per, per), :, cut, :] = res.reshape(per, 2, q, CW)
            return carry

        lax.fori_loop(0, CW // BLOCK, shrink_grads, 0)
        scatter_event(2 + j if j < C - 1 else tail_group, 0)
        run_slot(grad_at[j] + 1)

    for kind, j in order:
        (forward, backward, gradients)[kind](j)
        if (kind, j) == (0, C - 1):
            res_out[...] = out[their_rows].astype(BF)
            give_out.start()
        if (kind, j) == (1, C - 1):
            give_out.wait_send()
            res_out[...] = dnorm[their_rows].astype(BF)
            give_dn.start()

    def small_gradients():
        def vector_grads(i, carry):
            rows = rows_of(i)
            z, _ = unit(rows)
            dn = dnorm[rows]
            gain = carry[0] + jnp.sum(dn * z, axis=0, keepdims=True)
            shift = carry[1] + jnp.sum(dn, axis=0, keepdims=True)
            return gain, shift, carry[2] + jnp.sum(g[rows].astype(F32), axis=0, keepdims=True)

        zero_row = jnp.zeros((1, D), F32)
        sums = lax.fori_loop(0, blocks, vector_grads, (zero_row, zero_row, zero_row))
        tail_grad = jnp.where(b == 0, sums[2], 0.0)

        def grad_block(plane, j, o):
            at = j * CW + o * 128
            row, lane = plane_grad + at // W, at % W
            v = jnp.broadcast_to(small[row : row + 1, lane : lane + 128], (8, 128))
            return jnp.where(b == plane, v, 0.0)

        for c, v in enumerate(from_plane(grad_block, 8)):
            row, lane = 16 + first_bias + c * 128 // W, c * 128 % W
            small[row : row + 1, lane : lane + 128] = v[:1]
        for at, row in ((0, sums[0]), (2, sums[1]), (last, tail_grad)):
            small[16 + at : 17 + at] = row[:, :W]
            small[17 + at : 18 + at] = row[:, W:]
        small[16 + last + 2 : 32] = jnp.zeros((14 - last, W), F32)
        ws[...] = jnp.broadcast_to(small[16:32].astype(BF)[None, None], (m, 2, 16, W))
        scatter_event(C + 2, 0)

    def finish_all():
        small_rows = p.own_rows // blocks
        give_out.wait_recv()
        give_dn.wait_recv()
        give_dn.wait_send()

        def finish_rows(i, carry):
            local = pl.ds(pl.multiple_of(i * small_rows, small_rows), small_rows)
            rows = pl.ds(pl.multiple_of(b * p.own_rows + i * small_rows, small_rows), small_rows)
            z, inverse = unit(rows)
            tail = wide(last)
            total = out[rows] + trade[0, local].astype(F32) + tail
            res_out[local] = (x[rows].astype(F32) + total).astype(BF)
            du = (dnorm[rows] + trade[1, local].astype(F32)) * wide(0)
            back = du - jnp.mean(du, axis=1, keepdims=True) - z * jnp.mean(du * z, axis=1, keepdims=True)
            sg_out[local] = g[rows].astype(F32) + inverse * back
            return carry

        lax.fori_loop(0, blocks, finish_rows, 0)

    small_hop = 0
    for k, hop in leftover:
        if k == C + 1 and hop == half + 1:
            finish_all()
        scatter_event(k, hop)
        if k == tail_group:
            if hop == 1:
                small_gradients()
            else:
                small_hop += 1
                scatter_event(C + 2, small_hop)
    scatter_event(C + 2, half + 1)

    for kind in range(2):
        for t in range(2):
            row_copy(kind, t, False).wait_send()
    swap_copy(sw_mix, 0, 2, 4).wait()
    for t in range(3):
        gmix_out[:, half_lanes(t, 1 - b)] = sw_mix[2, t * rq : (t + 1) * rq].astype(F32)

    @pl.when(moves)
    def _():
        mer_back().wait_send()
        remote(mer.at[0], mer.at[1], sw_send.at[5], sw_recv.at[5], merge_to).wait_recv()

    @pl.when(jnp.logical_not(moves))
    def _():
        mer[1] = mer[0]

    for t in range(2):
        merged_rows = mer[1, t * p.mr : (t + 1) * p.mr].astype(F32)
        gmer_out[:, t * W : (t + 1) * W] = merged_rows[: p.rr]
    for j in range(C):
        exp_back(j).wait()

    def summed_block(plane, j, o):
        rows, cols = slice(j * rq, (j + 1) * rq), slice(o * 128, (o + 1) * 128)
        return jnp.where(b == plane, keep_exp[rows, cols], sw_exp[2, rows, cols].astype(F32))

    for c, v in enumerate(from_plane(summed_block, rq)):
        gexp_out[:, c * 128 : (c + 1) * 128] = v
    swap_copy(sw_small, 0, 2, 6).wait()
    gsmall_out[...] = sw_small[0] + sw_small[2]


def core(p, stream, cotangent, lengths, mixing, merging, expand, shrink, small_own):
    n, C, D, W, CW, rq = p.n, p.C, p.D, p.W, p.CW, p.rq
    m = n // 2
    half = m // 2
    hops = 2 * half - 1
    rows = p.rows
    a_rows = 6 * rq + 16
    b_rows = 2 * p.mr
    cosine, sine = (jnp.asarray(table) for table in rope_tables(rows))
    vmem = pl.BlockSpec(memory_space=pltpu.VMEM)
    hbm = pl.BlockSpec(memory_space=pl.ANY)
    dma = pltpu.SemaphoreType.DMA
    V = pltpu.VMEM
    SD = BF if rq % 16 == 0 else F32
    scratch = [
        V((m, 2, a_rows, W), BF),
        V((m, 2, b_rows, W), BF),
        V((C, m, 2, p.c_rows, CW), BF),
        V((m, 2, 16, W), BF),
        V((rows, D), BF),
        V((rows, D), BF),
        V((rows, D), BF),
        V((max(5 * W, 2 * p.C * CW) // 128, rows, 128), BF),
        V((rows, D), F32),
        V((rows, D), F32),
        V((48, W), F32),
        V((2, p.own_rows, D), BF),
        V((m, 6 * rq, W), BF),
        V((m, b_rows, W), BF),
        V((C, m, p.c_rows, CW), BF),
        V((m, 16, W), BF),
        V((hops, 6 * rq, W), BF),
        V((hops, b_rows, W), BF),
        V((C, hops, p.c_rows, CW), BF),
        V((hops, 16, W), BF),
        dma((C + 2, 2, half + 1)),
        dma((C + 2, 2, half + 1)),
        dma((C + 2,)),
        dma((C + 2,)),
        dma((C + 4, 2, half + 1)),
        dma((C + 4, 2, half + 1)),
        dma((C + 4,)),
        dma((C + 4,)),
        dma((6,)),
        dma((6,)),
        dma((7 + p.FF // D,)),
        V((3, 3 * rq, W), SD),
        V((3, C * rq, CW), SD),
        V((3, 16, W), F32),
        V((2, b_rows, W), BF),
        V((C * rq, CW), F32),
        dma((7 + C,)),
        dma((7 + C,)),
        dma((2, 2, half + 1)),
        dma((2, 2, half + 1)),
    ]
    shapes = (
        jax.ShapeDtypeStruct((p.own_rows, D), BF),
        jax.ShapeDtypeStruct((p.own_rows, D), F32),
        jax.ShapeDtypeStruct((rq, 3 * D), F32),
        jax.ShapeDtypeStruct((p.rr, D), F32),
        jax.ShapeDtypeStruct((rq, p.FF), F32),
        jax.ShapeDtypeStruct((p.hb, D), F32),
        jax.ShapeDtypeStruct((16, W), F32),
    )
    flops = 2 * rows * D * (6 * p.FF // 2 + 9 * W + 3 * W) + 12 * rows * rows * W
    return pl.pallas_call(
        functools.partial(block_kernel, p),
        out_shape=shapes,
        in_specs=[hbm] * 6 + [vmem, pl.BlockSpec(memory_space=pltpu.SMEM), vmem, vmem],
        out_specs=tuple(vmem for _ in shapes),
        scratch_shapes=scratch,
        compiler_params=pltpu.CompilerParams(
            collective_id=0, has_side_effects=True, vmem_limit_bytes=63 * 1024 * 1024
        ),
        cost_estimate=pl.CostEstimate(flops=flops, bytes_accessed=8 << 20, transcendentals=0),
    )(stream, cotangent, mixing, merging, expand, shrink, small_own, lengths, cosine, sine)


def local(n, stream, cotangent, lengths, steps_taken, learning_rates, *params):
    masters, momenta, variances = params[:6], params[6:12], params[12:]
    p = Plan(n, stream, *masters)
    linear = lax.axis_index("dp") * 2 + lax.axis_index("branch")
    vectors, offsets = masters[4], masters[5]
    small = jnp.zeros((16 * p.W,), F32)
    for row in range(2):
        small = lax.dynamic_update_slice(small, vectors[row], (row * p.D + linear * p.vc,))
    small = lax.dynamic_update_slice(small, offsets, (2 * p.D + linear * p.ow,))
    residual, stream_grad, *grads, small = core(
        p, stream, cotangent, lengths, *masters[:4], small.reshape(16, p.W)
    )
    small = small.reshape(-1)
    rows = [
        lax.dynamic_slice(small, (row * p.D + linear * p.vc,), (p.vc,)) for row in range(2)
    ]
    grads.append(jnp.stack(rows))
    grads.append(lax.dynamic_slice(small, (2 * p.D + linear * p.ow,), (p.ow,)))
    count = steps_taken[0].astype(F32)
    outs = [residual, stream_grad]
    for k in range(6):
        decay = decay_rate if k < 4 else 0.0
        outs.extend(
            adam_update(
                masters[k], grads[k], momenta[k], variances[k], learning_rates[k], count, decay
            )
        )
    return tuple(outs)


def solution(mesh):
    rows = P(("dp", "branch"), None)
    cols = P(None, ("dp", "branch"))
    flat = P(("dp", "branch"))
    six = (rows, rows, rows, rows, cols, flat)
    return jax.shard_map(
        functools.partial(local, mesh.shape["dp"]),
        mesh=mesh,
        in_specs=(rows, rows, P("dp"), P(), P()) + six * 3,
        out_specs=(rows, rows) + sum(((s,) * 4 for s in six), ()),
        check_vma=False,
    )
```
